32 devices in a mesh: dp: 16 (over z, y, x), tensor: 2 (over core).
Axes of the slice: x: 2, y: 2, z: 4, core: 2. Of those that a mesh axis runs over, the one named last changes fastest.
Arguments:
- inputs: bfloat16 [16416, 1024], P('dp'), may hold values from -6 to 6
- skips: bfloat16 [2, 16416, 1024], P(None, 'dp'), may hold values from -6 to 6
- cotangent: bfloat16 [16416, 1024], P('dp'), may hold values from -6 to 6
- skip_weight: bfloat16 [2, 2, 1024, 1024], P(None, 'tensor'), may hold values from -0.125 to 0.125
- skip_bias: bfloat16 [2, 1024], replicated, may hold values from -3 to 3
- attn_norm_gain: bfloat16 [2, 1024], replicated, may hold values from 0.5 to 1.5
- attn_norm_bias: bfloat16 [2, 1024], replicated, may hold values from -1 to 1
- qkv_weight: bfloat16 [2, 1024, 3, 1024], P(None, None, None, 'tensor'), may hold values from -0.1875 to 0.1875
- proj_weight: bfloat16 [2, 1024, 1024], P(None, None, 'tensor'), may hold values from -6 to 6
- proj_bias: bfloat16 [2, 1024], replicated, may hold values from -3 to 3
- ffn_norm_gain: bfloat16 [2, 1024], replicated, may hold values from 0.5 to 1.5
- ffn_norm_bias: bfloat16 [2, 1024], replicated, may hold values from -1 to 1
- up_weight: bfloat16 [2, 1024, 4096], P(None, None, 'tensor'), may hold values from -0.1875 to 0.1875
- up_bias: bfloat16 [2, 4096], P(None, 'tensor'), may hold values from -3 to 3
- down_weight: bfloat16 [2, 1024, 4096], P(None, None, 'tensor'), may hold values from -0.125 to 0.125
- down_bias: bfloat16 [2, 1024], replicated, may hold values from -3 to 3
Outputs:
- output: bfloat16 [16416, 1024], P('dp')
- input_grad: bfloat16 [16416, 1024], P('dp')
- skip_grad: bfloat16 [2, 16416, 1024], P(None, 'dp')
- skip_weight_grad: float32 [2, 2, 1024, 1024], P(None, 'tensor', 'dp')
- skip_bias_grad: float32 [2, 1024], P(None, 'dp')
- attn_norm_gain_grad: float32 [2, 1024], P(None, 'dp')
- attn_norm_bias_grad: float32 [2, 1024], P(None, 'dp')
- qkv_weight_grad: float32 [2, 1024, 3, 1024], P(None, 'dp', None, 'tensor')
- proj_weight_grad: float32 [2, 1024, 1024], P(None, 'dp', 'tensor')
- proj_bias_grad: float32 [2, 1024], P(None, 'dp')
- ffn_norm_gain_grad: float32 [2, 1024], P(None, 'dp')
- ffn_norm_bias_grad: float32 [2, 1024], P(None, 'dp')
- up_weight_grad: float32 [2, 1024, 4096], P(None, 'dp', 'tensor')
- up_bias_grad: float32 [2, 4096], P(None, ('tensor', 'dp'))
- down_weight_grad: float32 [2, 1024, 4096], P(None, 'dp', 'tensor')
- down_bias_grad: float32 [2, 1024], P(None, 'dp')
The draws below stay inside these ranges and needn't reach their ends.
All inputs are finite; a program needn't handle non-finite values.
Results may differ from the reference program's by a relative error of at most 0.02.
Values may be sent and summed in bfloat16 or wider, within the bound.
No kernel may reach another device: no remote copies, remote signals or barrier semaphores. Data moves between devices by JAX's collectives and lax.ppermute only.
A program may use at most 512 MiB of HBM per device.

```python
import jax
import jax.numpy as jnp
from jax import lax

D = 1024
HEADS = 16
HD = 64
FF = 4096
LAYERS = 2
SEQ = 1026
SEQS = 16
TOKENS = 16416
N_TENSOR = 2


def raised(entries, stream_key, source, target, blocks, factor):
    def block_of(position):
        return (jnp.arange(entries.shape[position]) // (entries.shape[position] // blocks)).reshape((-1,) + (1,) * (entries.ndim - 1 - position))

    near = jax.random.permutation(stream_key, blocks)[block_of(target)]
    far = (block_of(target) + blocks // 2) % blocks
    return jnp.where((block_of(source) == near) | (block_of(source) == far), factor * entries, entries)


def block_scale(key, extent, cuts, smallest, largest):
    level, own = 1.0, jax.random.fold_in(key, 6)
    for position, blocks in cuts:
        steps = jnp.exp(jax.random.uniform(jax.random.fold_in(own, position), (blocks,), jnp.float32, smallest / len(cuts), largest / len(cuts)))
        level = level * jnp.repeat(steps, extent[position] // blocks).reshape([-1 if axis == position else 1 for axis in range(len(extent))])
    return level


def normal_values(own_key, extent, width, bound, cuts=(), kind=jnp.bfloat16):
    gain = block_scale(own_key, extent, cuts, -0.22, 0.18) if cuts else 1.0
    drawn = jax.random.normal(own_key, extent, jnp.float32) * width * gain
    return jnp.minimum(jnp.maximum(drawn, -bound), bound).astype(kind)


def gaussian_with(own_key, extent, deviation, reach, pieces, heavy, held_as=jnp.bfloat16):
    array = deviation * jax.random.normal(own_key, extent, jnp.float32)
    if pieces:
        array = array * block_scale(own_key, extent, pieces, -0.22, 0.18)
    return jnp.clip(raised(array, jax.random.fold_in(own_key, 3), *heavy), -reach, reach).astype(held_as)


def setup_inputs(seed: int = 0) -> dict:
    arg_keys = jax.random.split(jax.random.key(seed), 17)
    inputs = normal_values(arg_keys[0], (TOKENS, D), 1.0, 6.0, ((0, 16),))
    skips = normal_values(arg_keys[1], (LAYERS, TOKENS, D), 1.0, 6.0, ((1, 16),))
    cotangent = gaussian_with(arg_keys[2], (TOKENS, D), 1.0, 6.0, ((0, 16),), (0, 1, 16, 2.0))
    skip_weight = normal_values(arg_keys[3], (LAYERS, 2, D, D), (2 * D) ** -0.5, 0.125, ((1, 2),))
    skip_bias = normal_values(arg_keys[4], (LAYERS, D), 0.5, 3.0)
    attn_norm_gain = jnp.clip(1.0 + 0.1 * jax.random.normal(arg_keys[5], (LAYERS, D), jnp.float32), 0.5, 1.5).astype(jnp.bfloat16)
    attn_norm_bias = normal_values(arg_keys[6], (LAYERS, D), 0.2, 1.0)
    qkv_weight = normal_values(arg_keys[7], (LAYERS, D, 3, HEADS * HD), D ** -0.5, 0.1875, ((3, 2),))
    proj_weight = normal_values(arg_keys[8], (LAYERS, D, HEADS * HD), (1 + HD * HD // (4 * SEQ)) ** -0.5, 6.0, ((2, 2),))
    proj_bias = normal_values(arg_keys[9], (LAYERS, D), 0.5, 3.0)
    ffn_norm_gain = jnp.clip(1.0 + 0.1 * jax.random.normal(arg_keys[10], (LAYERS, D), jnp.float32), 0.5, 1.5).astype(jnp.bfloat16)
    ffn_norm_bias = normal_values(arg_keys[11], (LAYERS, D), 0.2, 1.0)
    up_weight = normal_values(arg_keys[12], (LAYERS, D, FF), D ** -0.5, 0.1875, ((2, 2),))
    up_bias = normal_values(arg_keys[13], (LAYERS, FF), 0.5, 3.0, ((1, 2),))
    down_weight = normal_values(arg_keys[14], (LAYERS, D, FF), (FF // 2) ** -0.5, 0.125, ((2, 2),))
    down_bias = normal_values(arg_keys[15], (LAYERS, D), 0.5, 3.0)
    return {"inputs": inputs, "skips": skips, "cotangent": cotangent, "skip_weight": skip_weight, "skip_bias": skip_bias, "attn_norm_gain": attn_norm_gain, "attn_norm_bias": attn_norm_bias, "qkv_weight": qkv_weight, "proj_weight": proj_weight, "proj_bias": proj_bias, "ffn_norm_gain": ffn_norm_gain, "ffn_norm_bias": ffn_norm_bias, "up_weight": up_weight, "up_bias": up_bias, "down_weight": down_weight, "down_bias": down_bias}


@jax.custom_vjp
def low(v):
    return lax.optimization_barrier(v.astype(jnp.bfloat16)).astype(jnp.float32)

@jax.custom_vjp
def low_back(v):
    return v

def low_keep(v):
    return (low(v), None)

def low_pass(kept, grad):
    return (grad,)

def back_keep(v):
    return (v, None)

def back_low(kept, grad):
    return (low(grad),)
low.defvjp(low_keep, low_pass)
low_back.defvjp(back_keep, back_low)
highest = lax.Precision.HIGHEST
epsilon = 1e-05

def block_count(length):
    total = max(1, length // 512)
    while length % total:
        total = total - 1
    return total

def layer_norm(values_in, gain_row, shift_row):
    average = lax.optimization_barrier(jnp.mean(values_in, axis=-1, keepdims=True))
    centred = values_in - average
    variance = lax.optimization_barrier(jnp.mean(centred * centred, axis=-1, keepdims=True))
    return centred * lax.rsqrt(variance + epsilon) * gain_row + shift_row

def attend(queries, key_rows, value_rows):
    blocks = block_count(SEQ)
    scale = HD ** (-0.5)

    def one_block(query_block):
        scores = low_back(jnp.einsum('qhd,khd->hqk', query_block, key_rows, precision=highest) * scale)
        softened = jax.nn.softmax(scores, axis=-1)
        return jnp.einsum('hqk,khd->qhd', low(softened), value_rows, precision=highest)
    split = queries.reshape(blocks, SEQ // blocks, HEADS, HD)
    return lax.map(jax.checkpoint(one_block), split).reshape(SEQ, HEADS, HD)

def layer(residual, skip_rows, params):
    skip_matrix, skip_offset, gain_one, shift_one, qkv_matrix, proj_matrix, proj_offset, gain_two, shift_two, up_matrix, up_offset, down_matrix, down_offset = params
    joined = low(jnp.stack([residual, skip_rows]))
    halves = jnp.einsum('tsd,tde->tse', joined, skip_matrix, precision=highest)
    hidden = low_back(lax.optimization_barrier(jnp.sum(halves, axis=0))) + skip_offset
    normed_one = low(layer_norm(hidden, gain_one, shift_one))
    projected = jnp.dot(normed_one, qkv_matrix.reshape(D, 3 * HEADS * HD), precision=highest)
    projected = low(low_back(projected)).reshape(SEQ, 3, HEADS, HD)
    attended = attend(projected[:, 0], projected[:, 1], projected[:, 2])
    attended = low(low_back(attended.reshape(SEQ, HEADS * HD)))
    head_group = HEADS * HD // N_TENSOR
    mixed = jnp.einsum('sgc,dgc->gsd', attended.reshape(SEQ, N_TENSOR, head_group), proj_matrix.reshape(D, N_TENSOR, head_group), precision=highest)
    middle = hidden + low_back(lax.optimization_barrier(jnp.sum(mixed, axis=0))) + proj_offset
    normed_two = low(layer_norm(middle, gain_two, shift_two))
    up_proj = low_back(jnp.dot(normed_two, up_matrix, precision=highest)) + up_offset
    activation = low(jax.nn.gelu(up_proj, approximate=False))
    unit_group = FF // N_TENSOR
    ffn_out = jnp.einsum('sgf,dgf->gsd', activation.reshape(SEQ, N_TENSOR, unit_group), down_matrix.reshape(D, N_TENSOR, unit_group), precision=highest)
    return middle + low_back(lax.optimization_barrier(jnp.sum(ffn_out, axis=0))) + down_offset

def sequence(weights, seq_input, seq_skips):
    residual = seq_input
    for layer_index in range(LAYERS):
        residual = layer(residual, seq_skips[layer_index], tuple((item[layer_index] for item in weights)))
    return residual

def reference(inputs, skips, cotangent, skip_weight, skip_bias, attn_norm_gain, attn_norm_bias, qkv_weight, proj_weight, proj_bias, ffn_norm_gain, ffn_norm_bias, up_weight, up_bias, down_weight, down_bias):
    weights = tuple((item.astype(jnp.float32) for item in (skip_weight, skip_bias, attn_norm_gain, attn_norm_bias, qkv_weight, proj_weight, proj_bias, ffn_norm_gain, ffn_norm_bias, up_weight, up_bias, down_weight, down_bias)))
    seq_inputs = inputs.astype(jnp.float32).reshape(SEQS, SEQ, D)
    seq_skips = skips.astype(jnp.float32).reshape(LAYERS, SEQS, SEQ, D).transpose(1, 0, 2, 3)

    def forward(weight_set, input_set, skip_set):

        def single(pair):
            return sequence(weight_set, pair[0], pair[1])
        return lax.map(jax.checkpoint(single), (input_set, skip_set))
    result, pullback = jax.vjp(forward, weights, seq_inputs, seq_skips)
    weight_grads, input_grads, skip_grads = pullback(cotangent.astype(jnp.float32).reshape(SEQS, SEQ, D))
    output = result.reshape(TOKENS, D).astype(jnp.bfloat16)
    input_grad = input_grads.reshape(TOKENS, D).astype(jnp.bfloat16)
    skip_grad = skip_grads.transpose(1, 0, 2, 3).reshape(LAYERS, TOKENS, D).astype(jnp.bfloat16)
    return (output, input_grad, skip_grad, weight_grads[0], weight_grads[1], weight_grads[2], weight_grads[3], weight_grads[4], weight_grads[5], weight_grads[6], weight_grads[7], weight_grads[8], weight_grads[9], weight_grads[10], weight_grads[11], weight_grads[12])
```

```python
import functools
import jax
import jax.numpy as jnp
from jax import lax
from jax.experimental import pallas as pl
from jax.experimental.pallas import tpu as pltpu
from jax.sharding import PartitionSpec as P

F32 = jnp.float32
BF16 = jnp.bfloat16
HD = 64
MAIN = 512
PAD = 528
GROUP = 256
HEADS_IN_GROUP = GROUP // HD
VMEM_LIMIT = 60 * 1024 * 1024


def _dot(a, b, dims):
    return lax.dot_general(a, b, (dims, ((), ())), preferred_element_type=F32)


def _extra_rows(mine_ref, other_ref):
    row = lax.broadcasted_iota(jnp.int32, (16, GROUP), 0)
    lane = lax.broadcasted_iota(jnp.int32, (16, GROUP), 1)
    mine = jnp.broadcast_to(mine_ref[MAIN : MAIN + 16, :][0:1].astype(F32), (16, GROUP))
    other = jnp.broadcast_to(other_ref[MAIN : MAIN + 16, :][0:1].astype(F32), (16, GROUP))
    value = jnp.where(row % 2 == 0, mine, other)
    return jnp.where(row // 2 == lane // HD, value, 0.0).astype(BF16)


def _attn_fwd_kernel(q_ref, km_ref, vm_ref, ko_ref, vo_ref, o_ref, e_ref, ex_ref, il_ref, k_s, v_s):
    k_s[:MAIN] = km_ref[:MAIN]
    k_s[MAIN:] = ko_ref[:MAIN]
    v_s[:MAIN] = vm_ref[:MAIN]
    v_s[MAIN:] = vo_ref[:MAIN]
    lane = lax.broadcasted_iota(jnp.int32, (PAD, GROUP), 1) // HD
    slot = lax.broadcasted_iota(jnp.int32, (PAD, 16), 1) // 2
    q = q_ref[...] * jnp.asarray(HD**-0.5, BF16)
    kx = _extra_rows(km_ref, ko_ref)
    vx = _extra_rows(vm_ref, vo_ref)
    sx = _dot(q, kx, ((1,), (1,)))
    out = jnp.zeros((PAD, GROUP), F32)
    ex_all = jnp.zeros((PAD, 16), F32)
    il_all = jnp.zeros((PAD, 16), F32)
    for h in range(HEADS_IN_GROUP):
        qh = jnp.where(lane == h, q, jnp.zeros_like(q))
        s = _dot(qh, k_s[...], ((1,), (1,)))
        sxh = jnp.where(slot == h, sx, -jnp.inf)
        top = jnp.maximum(jnp.max(s, axis=1, keepdims=True), jnp.max(sxh, axis=1, keepdims=True))
        e = jnp.exp(s - top)
        exh = jnp.exp(sxh - top)
        total = jnp.sum(e, axis=1, keepdims=True) + jnp.sum(exh, axis=1, keepdims=True)
        inverse = 1.0 / total
        low = e.astype(BF16)
        e_ref[h] = low
        out = out + jnp.where(lane == h, _dot(low, v_s[...], ((1,), (0,))) * inverse, 0.0)
        ex_all = ex_all + exh
        il_all = il_all + jnp.where(slot == h, inverse, 0.0)
    out = out + _dot((ex_all * il_all).astype(BF16), vx, ((1,), (0,)))
    o_ref[...] = out.astype(BF16)
    ex_ref[0] = ex_all
    il_ref[0] = il_all


def attn_forward(q, kv, kv_other):
    width = q.shape[1]
    groups = width // GROUP

    def near(offset):
        return pl.BlockSpec((PAD, GROUP), lambda g: (0, g + offset))

    def far(offset):
        return pl.BlockSpec((PAD, GROUP), lambda g: (0, (g + groups // 2) % groups + offset))

    heads = width // HD
    elements = heads * PAD * (2 * MAIN)
    return pl.pallas_call(
        _attn_fwd_kernel,
        grid=(groups,),
        in_specs=[near(0), near(0), near(groups), far(0), far(groups)],
        out_specs=[
            near(0),
            pl.BlockSpec((HEADS_IN_GROUP, PAD, 2 * MAIN), lambda g: (g, 0, 0)),
            pl.BlockSpec((1, PAD, 16), lambda g: (g, 0, 0)),
            pl.BlockSpec((1, PAD, 16), lambda g: (g, 0, 0)),
        ],
        out_shape=[
            jax.ShapeDtypeStruct((PAD, width), BF16),
            jax.ShapeDtypeStruct((heads, PAD, 2 * MAIN), BF16),
            jax.ShapeDtypeStruct((groups, PAD, 16), F32),
            jax.ShapeDtypeStruct((groups, PAD, 16), F32),
        ],
        scratch_shapes=[pltpu.VMEM((2 * MAIN, GROUP), BF16), pltpu.VMEM((2 * MAIN, GROUP), BF16)],
        compiler_params=pltpu.CompilerParams(vmem_limit_bytes=VMEM_LIMIT),
        cost_estimate=pl.CostEstimate(
            flops=4 * elements * GROUP, bytes_accessed=3 * elements, transcendentals=elements
        ),
        name="attn_forward",
    )(q, kv, kv, kv_other, kv_other)


def _attn_bwd_kernel(
    q_ref, km_ref, vm_ref, ko_ref, vo_ref, do_ref, o_ref, e_ref, ex_ref, il_ref,
    dq_ref, dkm_ref, dko_ref, dvm_ref, dvo_ref, k_s, v_s, dk_s, dv_s,
):
    k_s[:MAIN] = km_ref[:MAIN]
    k_s[MAIN:] = ko_ref[:MAIN]
    v_s[:MAIN] = vm_ref[:MAIN]
    v_s[MAIN:] = vo_ref[:MAIN]
    scale = HD**-0.5
    lane = lax.broadcasted_iota(jnp.int32, (PAD, GROUP), 1) // HD
    slot = lax.broadcasted_iota(jnp.int32, (PAD, 16), 1) // 2
    q = q_ref[...] * jnp.asarray(scale, BF16)
    kx = _extra_rows(km_ref, ko_ref)
    vx = _extra_rows(vm_ref, vo_ref)
    il = il_ref[0]
    do = do_ref[...].astype(F32)
    product = do * o_ref[...].astype(F32)
    spread = jnp.zeros((PAD, GROUP), F32)
    inner = jnp.zeros((PAD, 16), F32)
    inners = []
    for h in range(HEADS_IN_GROUP):
        inverse = il[:, 2 * h : 2 * h + 1]
        spread = jnp.where(lane == h, inverse, spread)
        one = jnp.sum(jnp.where(lane == h, product, 0.0), axis=1, keepdims=True) * inverse
        inners.append(one)
        inner = jnp.where(slot == h, one, inner)
    dos = (do * spread).astype(BF16)
    dos_t = dos.T
    q_t = q.T
    dq = jnp.zeros((PAD, GROUP), F32)
    for h in range(HEADS_IN_GROUP):
        rows = slice(h * HD, (h + 1) * HD)
        dosh = jnp.where(lane == h, dos, jnp.zeros_like(dos))
        e = e_ref[h]
        dp = _dot(dosh, v_s[...], ((1,), (1,)))
        ds = (e.astype(F32) * (dp - inners[h])).astype(BF16)
        dq = dq + jnp.where(lane == h, _dot(ds, k_s[...], ((1,), (0,))), 0.0)
        dk_s[rows, :] = (
            _dot(q_t[rows, :MAIN], ds[:MAIN], ((1,), (0,)))
            + q_t[rows, MAIN : MAIN + 1].astype(F32) * ds[MAIN : MAIN + 16].astype(F32)[0:1]
        )
        dv_s[rows, :] = (
            _dot(dos_t[rows, :MAIN], e[:MAIN], ((1,), (0,)))
            + dos_t[rows, MAIN : MAIN + 1].astype(F32) * e[MAIN : MAIN + 16].astype(F32)[0:1]
        )
    ex = ex_ref[0]
    dsx = (ex * (_dot(dos, vx, ((1,), (1,))) - inner)).astype(BF16)
    dq = dq + _dot(dsx, kx, ((1,), (0,)))
    dq_ref[...] = (dq * scale).astype(BF16)
    dkx = _dot(dsx, q, ((0,), (0,)))
    dvx = _dot(ex.astype(BF16), dos, ((0,), (0,)))
    row = lax.broadcasted_iota(jnp.int32, (16, GROUP), 0)
    own = row // 2 == lax.broadcasted_iota(jnp.int32, (16, GROUP), 1) // HD
    for half, (dk_ref, dv_ref) in enumerate(((dkm_ref, dvm_ref), (dko_ref, dvo_ref))):
        keep = jnp.logical_and(own, row % 2 == half)
        for ref, grad_s, tail in ((dk_ref, dk_s, dkx), (dv_ref, dv_s, dvx)):
            ref[:MAIN] = grad_s[:, half * MAIN : (half + 1) * MAIN].T.astype(BF16)
            last = jnp.sum(jnp.where(keep, tail, 0.0), axis=0, keepdims=True)
            ref[MAIN:] = jnp.where(row == 0, jnp.broadcast_to(last, (16, GROUP)), 0.0).astype(BF16)


def attn_backward(q, kv, kv_other, dout, out, e, ex, il):
    width = q.shape[1]
    groups = width // GROUP

    def near(offset):
        return pl.BlockSpec((PAD, GROUP), lambda g: (0, g + offset))

    def far(offset):
        return pl.BlockSpec((PAD, GROUP), lambda g: (0, (g + groups // 2) % groups + offset))

    small = pl.BlockSpec((1, PAD, 16), lambda g: (g, 0, 0))
    heads = width // HD
    elements = heads * PAD * (2 * MAIN)
    block = jax.ShapeDtypeStruct((PAD, width), BF16)
    far_out = pl.BlockSpec((PAD, GROUP), lambda g: (0, (g + groups // 2) % groups))
    return pl.pallas_call(
        _attn_bwd_kernel,
        grid=(groups,),
        in_specs=[
            near(0), near(0), near(groups), far(0), far(groups), near(0), near(0),
            pl.BlockSpec((HEADS_IN_GROUP, PAD, 2 * MAIN), lambda g: (g, 0, 0)), small, small,
        ],
        out_specs=[near(0), near(0), far_out, near(0), far_out],
        out_shape=[block] * 5,
        scratch_shapes=[
            pltpu.VMEM((2 * MAIN, GROUP), BF16),
            pltpu.VMEM((2 * MAIN, GROUP), BF16),
            pltpu.VMEM((GROUP, 2 * MAIN), F32),
            pltpu.VMEM((GROUP, 2 * MAIN), F32),
        ],
        compiler_params=pltpu.CompilerParams(vmem_limit_bytes=VMEM_LIMIT),
        cost_estimate=pl.CostEstimate(
            flops=8 * elements * GROUP, bytes_accessed=3 * elements, transcendentals=0
        ),
        name="attn_backward",
    )(q, kv, kv, kv_other, kv_other, dout, out, e, ex, il)


def _grad_kernel(has_received, pieces, coords_ref, x_ref, dy_ref, *refs):
    if has_received:
        received_ref, send_ref, keep_ref, xt_s, column_s = refs
    else:
        all_ref, xt_s, column_s = refs
    rows = xt_s.shape[0] // pieces
    span = max(rows, 128)

    @pl.when(pl.program_id(0) == 0)
    def _():
        for start in range(0, xt_s.shape[0], span):
            turned = x_ref[:MAIN, start : start + span].T
            last = x_ref[MAIN:, start : start + span].T.astype(F32)[:, 0:1]
            for part in range(span // rows):
                piece = start // rows + part
                first = jnp.bitwise_xor((piece >> coords_ref[2]) & 1, coords_ref[0])
                second = jnp.bitwise_xor((piece >> coords_ref[3]) & 1, coords_ref[1])
                place = first * (pieces // 2) + second * (pieces // 4) + (piece >> 2)
                at = pl.ds(pl.multiple_of(place * rows, rows), rows)
                xt_s[at, :] = turned[part * rows : (part + 1) * rows]
                column_s[at, :] = jnp.broadcast_to(
                    last[part * rows : (part + 1) * rows], (rows, 128)
                )

    width = dy_ref.shape[1]
    half = xt_s.shape[0] // 2
    last_row = dy_ref[MAIN:, :].astype(F32)[0:1]
    for part in range(2):
        at = slice(part * half, (part + 1) * half)
        total = _dot(xt_s[at, :], dy_ref[:MAIN, :], ((1,), (0,)))
        column = jnp.concatenate([column_s[at, :]] * (width // 128), axis=1)
        total = total + column * last_row
        if has_received:
            total = total + received_ref[at, :].astype(F32)
            (keep_ref if part == 0 else send_ref)[...] = total.astype(BF16)
        else:
            all_ref[at, :] = total.astype(BF16)


def weight_grad(coords, pieces, x, dy, offset, width, received=None):
    features = x.shape[1]
    tile = 512
    start = offset // tile
    in_specs = [
        pl.BlockSpec((PAD, features), lambda j, c: (0, 0)),
        pl.BlockSpec((PAD, tile), lambda j, c: (0, start + j)),
    ]
    whole = pl.BlockSpec((features, tile), lambda j, c: (0, j))
    half = pl.BlockSpec((features // 2, tile), lambda j, c: (0, j))
    operands = [x, dy]
    if received is None:
        out_specs = [whole]
        out_shape = [jax.ShapeDtypeStruct((features, width), BF16)]
    else:
        in_specs.append(whole)
        operands.append(received)
        out_specs = [half, half]
        out_shape = [jax.ShapeDtypeStruct((features // 2, width), BF16)] * 2
    result = pl.pallas_call(
        functools.partial(_grad_kernel, received is not None, pieces),
        grid_spec=pltpu.PrefetchScalarGridSpec(
            num_scalar_prefetch=1,
            grid=(width // tile,),
            in_specs=in_specs,
            out_specs=out_specs,
            scratch_shapes=[
                pltpu.VMEM((features, MAIN), BF16),
                pltpu.VMEM((features, 128), F32),
            ],
        ),
        out_shape=out_shape,
        compiler_params=pltpu.CompilerParams(vmem_limit_bytes=VMEM_LIMIT),
        cost_estimate=pl.CostEstimate(
            flops=2 * PAD * features * width,
            bytes_accessed=2 * features * width * (1 if received is None else 2),
            transcendentals=0,
        ),
        name="weight_grad",
    )(coords, *operands)
    return result[0] if received is None else result


epsilon = 1e-05


def swap_cores(value):
    return lax.ppermute(value, "tensor", [(0, 1), (1, 0)])


def swap_bit(value, bit, size):
    return lax.ppermute(value, "dp", [(i, i ^ (1 << bit)) for i in range(size)])


def add_low(a, b):
    return (a.astype(F32) + b.astype(F32)).astype(BF16)


class Reducer:
    def __init__(self, size):
        self.size = size
        self.bits = size.bit_length() - 1
        assert size == 1 << self.bits and self.bits >= 2
        self.index = lax.axis_index("dp")

    def bit(self, which):
        return (self.index >> which) & 1

    def order(self, flip):
        return (1, 0) if flip else (0, 1)

    def coords(self, flip):
        first, second = self.order(flip)
        values = [self.bit(first), self.bit(second), first, second]
        return jnp.stack([jnp.asarray(v, jnp.int32) for v in values])

    def arrange(self, value, flip):
        first, second = self.order(flip)
        rows = value.shape[0] // self.size
        view = value.reshape(self.size // 4, 2, 2, rows, value.shape[1])
        if not flip:
            view = view.transpose(2, 1, 0, 3, 4)
        else:
            view = view.transpose(1, 2, 0, 3, 4)
        view = jnp.where(self.bit(first) == 1, view[::-1], view)
        view = jnp.where(self.bit(second) == 1, view[:, ::-1], view)
        return view.reshape(value.shape)

    def finish(self, keep, send, flip):
        first, second = self.order(flip)
        got = swap_bit(send, first, self.size)
        half = keep.shape[0] // 2
        send = add_low(keep[half:], got[half:])
        keep = add_low(keep[:half], got[:half])
        got = swap_bit(send, second, self.size)
        total = add_low(keep, got)
        width = total.shape[1]
        rows = total.shape[0] // (self.size // 4)
        blocks = self.size // 4
        for which in range(2, self.bits):
            view = total.reshape(blocks // 2, 2, rows, width)
            mine = self.bit(which)
            keep = lax.dynamic_index_in_dim(view, mine, 1, keepdims=False)
            send = lax.dynamic_index_in_dim(view, 1 - mine, 1, keepdims=False)
            got = swap_bit(send, which, self.size)
            if which == self.bits - 1:
                total = keep.astype(F32) + got.astype(F32)
            else:
                total = add_low(keep, got)
            blocks = blocks // 2
        return total.reshape(rows, width)


def localize(value, core):
    main = lax.dynamic_slice_in_dim(value, core * MAIN, MAIN, 0)
    extra = lax.dynamic_slice_in_dim(value, 2 * MAIN + core, 1, 0)
    blank = jnp.zeros((PAD - MAIN - 1, value.shape[1]), value.dtype)
    return jnp.concatenate([main, extra, blank], axis=0)


def globalize(mine, core):
    theirs = swap_cores(mine)
    low = jnp.where(core == 0, mine, theirs)
    high = jnp.where(core == 0, theirs, mine)
    return jnp.concatenate(
        [low[:MAIN], high[:MAIN], low[MAIN : MAIN + 1], high[MAIN : MAIN + 1]], axis=0
    )


def layer_norm(values_in, gain_row, shift_row):
    average = jnp.mean(values_in, axis=-1, keepdims=True)
    centred = values_in - average
    variance = jnp.mean(centred * centred, axis=-1, keepdims=True)
    return centred * lax.rsqrt(variance + epsilon) * gain_row + shift_row


def norm_backward(values_in, gain_row, grad):
    average = jnp.mean(values_in, axis=-1, keepdims=True)
    centred = values_in - average
    variance = jnp.mean(centred * centred, axis=-1, keepdims=True)
    inverse = lax.rsqrt(variance + epsilon)
    normed = centred * inverse
    scaled = grad * gain_row
    back = (
        scaled
        - jnp.mean(scaled, axis=-1, keepdims=True)
        - normed * jnp.mean(scaled * normed, axis=-1, keepdims=True)
    ) * inverse
    return back, jnp.sum(grad * normed, axis=0), jnp.sum(grad, axis=0)


def matmul(a, b):
    return _dot(a, b, ((1,), (0,)))


def matmul_t(a, b):
    return _dot(a, b, ((1,), (1,)))


def gelu_parts(up):
    cumulative = 0.5 * lax.erfc(-up * (0.5**0.5))
    density = jnp.exp(-0.5 * up * up) * 0.3989422804014327
    return up * cumulative, cumulative + up * density


def both(own, axis):
    return jnp.concatenate([own, swap_cores(own)], axis=axis)


def layer_forward(residual, skip_rows, params, core):
    (
        skip_own, skip_peer, skip_offset, gain_one, shift_one, qkv_matrix, proj_matrix, proj_offset,
        gain_two, shift_two, up_matrix, up_offset, down_matrix, down_offset,
    ) = params
    first = residual.astype(BF16)
    x_own = jnp.where(core == 0, first, skip_rows)
    x_peer = jnp.where(core == 0, skip_rows, first)
    hidden = matmul(x_own, skip_own) + matmul(x_peer, skip_peer) + skip_offset
    normed_one = layer_norm(hidden, gain_one, shift_one).astype(BF16)
    width = qkv_matrix.shape[1] // 3
    kv = matmul(normed_one, qkv_matrix[:, width:]).astype(BF16)
    kv_other = swap_cores(kv)
    q = matmul(normed_one, qkv_matrix[:, :width]).astype(BF16)
    attended, e, ex, il = attn_forward(q, kv, kv_other)
    middle = hidden + matmul_t(attended, proj_matrix) + proj_offset
    normed_two = layer_norm(middle, gain_two, shift_two).astype(BF16)
    up = matmul(normed_two, up_matrix) + up_offset
    activation, slope = gelu_parts(up)
    activation = activation.astype(BF16)
    slope = slope.astype(BF16)
    result = middle + matmul_t(activation, down_matrix) + down_offset
    kept = (x_own, x_peer, hidden, normed_one, q, kv, kv_other, attended, e, ex, il, middle, normed_two,
            activation, slope)
    return result, kept


def layer_backward(gradient, kept, params, core, reducer):
    (
        skip_own, skip_peer, skip_offset, gain_one, shift_one, qkv_matrix, proj_matrix, proj_offset,
        gain_two, shift_two, up_matrix, up_offset, down_matrix, down_offset,
    ) = params
    (x_own, x_peer, hidden, normed_one, q, kv, kv_other, attended, e, ex, il, middle, normed_two,
     activation, slope) = kept
    size = reducer.size

    def reduced(pairs, flip):
        coords = reducer.coords(flip)
        keeps, sends = [], []
        for x, x_other, dy, own_at, peer_at, width in pairs:
            theirs = weight_grad(coords, size, x_other, dy, peer_at, width)
            got = swap_cores(theirs)
            send, keep = weight_grad(coords, size, x, dy, own_at, width, got)
            keeps.append(keep)
            sends.append(send)
        return reducer.finish(jnp.concatenate(keeps, axis=1), jnp.concatenate(sends, axis=1), flip)

    model = gradient.shape[1]
    half_units = activation.shape[1] // 2
    grad_low = gradient.astype(BF16)
    down_offset_grad = jnp.sum(gradient, axis=0)
    down_grad = reduced([(grad_low, grad_low, activation, 0, half_units, half_units)], False)
    act_grad = matmul(grad_low, down_matrix)
    up_grad = act_grad * slope.astype(F32)
    up_offset_grad = jnp.sum(up_grad, axis=0)
    up_low = up_grad.astype(BF16)
    up_matrix_grad = reduced([(normed_two, normed_two, up_low, 0, half_units, half_units)], True)
    normed_two_grad = matmul_t(up_low, up_matrix)
    middle_part, gain_two_grad, shift_two_grad = norm_backward(middle, gain_two, normed_two_grad)
    middle_grad = gradient + middle_part
    proj_offset_grad = jnp.sum(middle_grad, axis=0)
    middle_low = middle_grad.astype(BF16)
    attended_grad = matmul(middle_low, proj_matrix).astype(BF16)
    half_heads = model // 2
    proj_grad = reduced([(middle_low, middle_low, attended, 0, half_heads, half_heads)], False)
    dq, dk_mine, dk_other, dv_mine, dv_other = attn_backward(
        q, kv, kv_other, attended_grad, attended, e, ex, il
    )
    dk_got = swap_cores(dk_other)
    dv_got = swap_cores(dv_other)
    dk = add_low(dk_mine, dk_got)
    dv = add_low(dv_mine, dv_got)
    dqkv = jnp.concatenate([dq, dk, dv], axis=1)
    normed_one_grad = matmul_t(dqkv, qkv_matrix)
    qkv_grad = reduced(
        [
            (normed_one, normed_one, dqkv, part * model, part * model + half_heads, half_heads)
            for part in range(3)
        ],
        True,
    )
    hidden_part, gain_one_grad, shift_one_grad = norm_backward(hidden, gain_one, normed_one_grad)
    hidden_grad = middle_grad + hidden_part
    skip_offset_grad = jnp.sum(hidden_grad, axis=0)
    hidden_low = hidden_grad.astype(BF16)
    skip_grad = reduced([(x_own, x_peer, hidden_low, 0, 0, model)], False)
    back_own = matmul_t(hidden_low, skip_own)
    back_peer = matmul_t(hidden_low, skip_peer)
    residual_part = jnp.where(core == 0, back_own, back_peer)
    skip_part = jnp.where(core == 0, back_peer, back_own).astype(BF16)
    weights = (skip_grad, qkv_grad, proj_grad, up_matrix_grad, down_grad)
    shared = jnp.stack(
        [skip_offset_grad, gain_one_grad, shift_one_grad, proj_offset_grad, gain_two_grad,
         shift_two_grad, down_offset_grad]
    )
    return residual_part, skip_part, weights, shared, up_offset_grad


def sum_vectors(shared, up_offsets, reducer):
    layers, count, width = shared.shape
    half = up_offsets.shape[1] // 2
    shared = shared.reshape(layers * count, width)

    def columns(value):
        parts = value.reshape(layers, reducer.size, half // width, width // reducer.size)
        return parts.transpose(0, 2, 1, 3).reshape(-1, width)

    mine = jnp.concatenate([shared, columns(up_offsets[:, :half])], axis=0).T
    theirs = jnp.concatenate([shared, columns(up_offsets[:, half:])], axis=0).T
    total = add_low(mine, swap_cores(theirs.astype(BF16)))
    total = reducer.arrange(total, False)
    middle = total.shape[0] // 2
    result = reducer.finish(total[:middle], total[middle:], False).T
    vectors = result[: layers * count].reshape(layers, count, -1)
    return vectors, result[layers * count :].reshape(layers, -1)


def body(
    inputs, skips, cotangent, skip_weight, skip_bias, attn_norm_gain, attn_norm_bias, qkv_weight,
    proj_weight, proj_bias, ffn_norm_gain, ffn_norm_bias, up_weight, up_bias, down_weight, down_bias,
):
    core = lax.axis_index("tensor")
    reducer = Reducer(lax.axis_size("dp"))
    layer_total, model = skip_bias.shape
    skip_own = skip_weight[:, 0]
    skip_peer = swap_cores(skip_own)
    qkv_full = jnp.stack([qkv_weight, swap_cores(qkv_weight)], axis=3)
    qkv_full = qkv_full.reshape(layer_total, model, -1)
    proj_full = both(proj_weight, 2)
    up_full = both(up_weight, 2)
    down_full = both(down_weight, 2)
    units = up_weight.shape[2]
    up_own = up_bias
    up_bias_full = jnp.concatenate([up_own, swap_cores(up_own)], axis=1)
    rows = tuple(
        item.astype(F32)
        for item in (skip_bias, attn_norm_gain, attn_norm_bias, proj_bias, ffn_norm_gain,
                     ffn_norm_bias, up_bias_full, down_bias)
    )
    every = (
        skip_own, skip_peer, rows[0], rows[1], rows[2], qkv_full, proj_full, rows[3], rows[4], rows[5],
        up_full, rows[6], down_full, rows[7],
    )
    residual = localize(inputs, core).astype(F32)
    saved = []
    for layer_index in range(layer_total):
        params = tuple(item[layer_index] for item in every)
        skip_rows = localize(skips[layer_index], core)
        residual, kept = layer_forward(residual, skip_rows, params, core)
        saved.append(kept)
    output = globalize(residual.astype(BF16), core)
    gradient = localize(cotangent, core).astype(F32)
    skip_grads, collected, shared, offsets = [], [], [], []
    for layer_index in reversed(range(layer_total)):
        params = tuple(item[layer_index] for item in every)
        gradient, skip_part, weights, vector, offset = layer_backward(
            gradient, saved[layer_index], params, core, reducer
        )
        skip_grads.insert(0, globalize(skip_part, core))
        collected.insert(0, weights)
        shared.insert(0, vector)
        offsets.insert(0, offset)
    vectors, up_bias_grad = sum_vectors(jnp.stack(shared), jnp.stack(offsets), reducer)
    skip_w, qkv_w, proj_w, up_w, down_w = (
        jnp.stack([entry[member] for entry in collected]) for member in range(5)
    )
    return (
        output, globalize(gradient.astype(BF16), core), jnp.stack(skip_grads), skip_w[:, None],
        vectors[:, 0], vectors[:, 1], vectors[:, 2],
        qkv_w.reshape(layer_total, -1, 3, qkv_weight.shape[3]), proj_w, vectors[:, 3], vectors[:, 4],
        vectors[:, 5], up_w, up_bias_grad, down_w, vectors[:, 6],
    )


def solution(mesh):
    return jax.shard_map(
        body,
        mesh=mesh,
        in_specs=(
            P("dp", None), P(None, "dp", None), P("dp", None), P(None, "tensor", None, None), P(), P(),
            P(), P(None, None, None, "tensor"), P(None, None, "tensor"), P(), P(), P(),
            P(None, None, "tensor"), P(None, "tensor"), P(None, None, "tensor"), P(),
        ),
        out_specs=(
            P("dp", None), P("dp", None), P(None, "dp", None), P(None, "tensor", "dp", None),
            P(None, "dp"), P(None, "dp"), P(None, "dp"), P(None, "dp", None, "tensor"),
            P(None, "dp", "tensor"), P(None, "dp"), P(None, "dp"), P(None, "dp"),
            P(None, "dp", "tensor"), P(None, ("tensor", "dp")), P(None, "dp", "tensor"), P(None, "dp"),
        ),
        check_vma=False,
    )
```

```python
import functools
import jax
import jax.numpy as jnp
from jax import lax
from jax.experimental import pallas as pl
from jax.experimental.pallas import tpu as pltpu
from jax.sharding import PartitionSpec as P

F32 = jnp.float32
BF16 = jnp.bfloat16
HD = 64
MAIN = 512
PAD = 528
GROUP = 256
HEADS_IN_GROUP = GROUP // HD
VMEM_LIMIT = 60 * 1024 * 1024
LIGHT = pl.CostEstimate(flops=1, bytes_accessed=1, transcendentals=0)


def _dot(a, b, dims):
    return lax.dot_general(a, b, (dims, ((), ())), preferred_element_type=F32)


def _extra_rows(mine_ref, other_ref):
    row = lax.broadcasted_iota(jnp.int32, (16, GROUP), 0)
    lane = lax.broadcasted_iota(jnp.int32, (16, GROUP), 1)
    mine = jnp.broadcast_to(mine_ref[MAIN : MAIN + 16, :][0:1].astype(F32), (16, GROUP))
    other = jnp.broadcast_to(other_ref[MAIN : MAIN + 16, :][0:1].astype(F32), (16, GROUP))
    value = jnp.where(row % 2 == 0, mine, other)
    return jnp.where(row // 2 == lane // HD, value, 0.0).astype(BF16)


def _attn_fwd_kernel(q_ref, km_ref, vm_ref, ko_ref, vo_ref, o_ref, of_ref, e_ref, ex_ref, il_ref, k_s, v_s):
    k_s[:MAIN] = km_ref[:MAIN]
    k_s[MAIN:] = ko_ref[:MAIN]
    v_s[:MAIN] = vm_ref[:MAIN]
    v_s[MAIN:] = vo_ref[:MAIN]
    lane = lax.broadcasted_iota(jnp.int32, (PAD, GROUP), 1) // HD
    slot = lax.broadcasted_iota(jnp.int32, (PAD, 16), 1) // 2
    q = q_ref[...] * jnp.asarray(HD**-0.5, BF16)
    kx = _extra_rows(km_ref, ko_ref)
    vx = _extra_rows(vm_ref, vo_ref)
    sx = _dot(q, kx, ((1,), (1,)))
    out = jnp.zeros((PAD, GROUP), F32)
    ex_all = jnp.zeros((PAD, 16), F32)
    il_all = jnp.zeros((PAD, 16), F32)
    for h in range(HEADS_IN_GROUP):
        qh = jnp.where(lane == h, q, jnp.zeros_like(q))
        s = _dot(qh, k_s[...], ((1,), (1,)))
        sxh = jnp.where(slot == h, sx, -jnp.inf)
        top = jnp.maximum(jnp.max(s, axis=1, keepdims=True), jnp.max(sxh, axis=1, keepdims=True))
        e = jnp.exp(s - top)
        exh = jnp.exp(sxh - top)
        total = jnp.sum(e, axis=1, keepdims=True) + jnp.sum(exh, axis=1, keepdims=True)
        inverse = 1.0 / total
        low = e.astype(BF16)
        e_ref[h] = low
        out = out + jnp.where(lane == h, _dot(low, v_s[...], ((1,), (0,))) * inverse, 0.0)
        ex_all = ex_all + exh
        il_all = il_all + jnp.where(slot == h, inverse, 0.0)
    out = out + _dot((ex_all * il_all).astype(BF16), vx, ((1,), (0,)))
    o_ref[...] = out.astype(BF16)
    of_ref[...] = out
    ex_ref[0] = ex_all
    il_ref[0] = il_all


def attn_forward(q, kv, kv_other):
    width = q.shape[1]
    groups = width // GROUP

    def near(offset):
        return pl.BlockSpec((PAD, GROUP), lambda g: (0, g + offset))

    def far(offset):
        return pl.BlockSpec((PAD, GROUP), lambda g: (0, (g + groups // 2) % groups + offset))

    heads = width // HD
    return pl.pallas_call(
        _attn_fwd_kernel,
        grid=(groups,),
        in_specs=[near(0), near(0), near(groups), far(0), far(groups)],
        out_specs=[
            near(0),
            near(0),
            pl.BlockSpec((HEADS_IN_GROUP, PAD, 2 * MAIN), lambda g: (g, 0, 0)),
            pl.BlockSpec((1, PAD, 16), lambda g: (g, 0, 0)),
            pl.BlockSpec((1, PAD, 16), lambda g: (g, 0, 0)),
        ],
        out_shape=[
            jax.ShapeDtypeStruct((PAD, width), BF16),
            jax.ShapeDtypeStruct((PAD, width), F32),
            jax.ShapeDtypeStruct((heads, PAD, 2 * MAIN), BF16),
            jax.ShapeDtypeStruct((groups, PAD, 16), F32),
            jax.ShapeDtypeStruct((groups, PAD, 16), F32),
        ],
        scratch_shapes=[pltpu.VMEM((2 * MAIN, GROUP), BF16), pltpu.VMEM((2 * MAIN, GROUP), BF16)],
        compiler_params=pltpu.CompilerParams(vmem_limit_bytes=VMEM_LIMIT),
        cost_estimate=LIGHT,
        name="attn_forward",
    )(q, kv, kv, kv_other, kv_other)


def _attn_bwd_kernel(
    q_ref, km_ref, vm_ref, ko_ref, vo_ref, do_ref, o_ref, e_ref, ex_ref, il_ref,
    dq_ref, dkm_ref, dko_ref, dvm_ref, dvo_ref, k_s, v_s, dk_s, dv_s,
):
    k_s[:MAIN] = km_ref[:MAIN]
    k_s[MAIN:] = ko_ref[:MAIN]
    v_s[:MAIN] = vm_ref[:MAIN]
    v_s[MAIN:] = vo_ref[:MAIN]
    scale = HD**-0.5
    lane = lax.broadcasted_iota(jnp.int32, (PAD, GROUP), 1) // HD
    slot = lax.broadcasted_iota(jnp.int32, (PAD, 16), 1) // 2
    q = q_ref[...] * jnp.asarray(scale, BF16)
    kx = _extra_rows(km_ref, ko_ref)
    vx = _extra_rows(vm_ref, vo_ref)
    il = il_ref[0]
    do = do_ref[...].astype(F32)
    spread = jnp.zeros((PAD, GROUP), F32)
    for h in range(HEADS_IN_GROUP):
        spread = jnp.where(lane == h, il[:, 2 * h : 2 * h + 1], spread)
    dos = (do * spread).astype(BF16)
    product = dos.astype(F32) * o_ref[...]
    inner = jnp.zeros((PAD, 16), F32)
    inners = []
    for h in range(HEADS_IN_GROUP):
        one = jnp.sum(jnp.where(lane == h, product, 0.0), axis=1, keepdims=True)
        inners.append(one)
        inner = jnp.where(slot == h, one, inner)
    dos_t = dos.T
    q_t = q.T
    dq = jnp.zeros((PAD, GROUP), F32)
    for h in range(HEADS_IN_GROUP):
        rows = slice(h * HD, (h + 1) * HD)
        dosh = jnp.where(lane == h, dos, jnp.zeros_like(dos))
        e = e_ref[h]
        dp = _dot(dosh, v_s[...], ((1,), (1,)))
        ds = (e.astype(F32) * (dp - inners[h])).astype(BF16)
        dq = dq + jnp.where(lane == h, _dot(ds, k_s[...], ((1,), (0,))), 0.0)
        dk_s[rows, :] = (
            _dot(q_t[rows, :MAIN], ds[:MAIN], ((1,), (0,)))
            + q_t[rows, MAIN : MAIN + 1].astype(F32) * ds[MAIN : MAIN + 16].astype(F32)[0:1]
        )
        dv_s[rows, :] = (
            _dot(dos_t[rows, :MAIN], e[:MAIN], ((1,), (0,)))
            + dos_t[rows, MAIN : MAIN + 1].astype(F32) * e[MAIN : MAIN + 16].astype(F32)[0:1]
        )
    ex = ex_ref[0]
    dsx = (ex * (_dot(dos, vx, ((1,), (1,))) - inner)).astype(BF16)
    dq = dq + _dot(dsx, kx, ((1,), (0,)))
    dq_ref[...] = (dq * scale).astype(BF16)
    dkx = _dot(dsx, q, ((0,), (0,)))
    dvx = _dot(ex.astype(BF16), dos, ((0,), (0,)))
    row = lax.broadcasted_iota(jnp.int32, (16, GROUP), 0)
    own = row // 2 == lax.broadcasted_iota(jnp.int32, (16, GROUP), 1) // HD
    for half, (dk_ref, dv_ref) in enumerate(((dkm_ref, dvm_ref), (dko_ref, dvo_ref))):
        keep = jnp.logical_and(own, row % 2 == half)
        for ref, grad_s, tail in ((dk_ref, dk_s, dkx), (dv_ref, dv_s, dvx)):
            ref[:MAIN] = grad_s[:, half * MAIN : (half + 1) * MAIN].T.astype(BF16)
            last = jnp.sum(jnp.where(keep, tail, 0.0), axis=0, keepdims=True)
            ref[MAIN:] = jnp.where(row == 0, jnp.broadcast_to(last, (16, GROUP)), 0.0).astype(BF16)


def attn_backward(q, kv, kv_other, dout, out, e, ex, il):
    width = q.shape[1]
    groups = width // GROUP

    def near(offset):
        return pl.BlockSpec((PAD, GROUP), lambda g: (0, g + offset))

    def far(offset):
        return pl.BlockSpec((PAD, GROUP), lambda g: (0, (g + groups // 2) % groups + offset))

    small = pl.BlockSpec((1, PAD, 16), lambda g: (g, 0, 0))
    heads = width // HD
    block = jax.ShapeDtypeStruct((PAD, width), BF16)
    far_out = pl.BlockSpec((PAD, GROUP), lambda g: (0, (g + groups // 2) % groups))
    return pl.pallas_call(
        _attn_bwd_kernel,
        grid=(groups,),
        in_specs=[
            near(0), near(0), near(groups), far(0), far(groups), near(0), near(0),
            pl.BlockSpec((HEADS_IN_GROUP, PAD, 2 * MAIN), lambda g: (g, 0, 0)), small, small,
        ],
        out_specs=[near(0), near(0), far_out, near(0), far_out],
        out_shape=[block] * 5,
        scratch_shapes=[
            pltpu.VMEM((2 * MAIN, GROUP), BF16),
            pltpu.VMEM((2 * MAIN, GROUP), BF16),
            pltpu.VMEM((GROUP, 2 * MAIN), F32),
            pltpu.VMEM((GROUP, 2 * MAIN), F32),
        ],
        compiler_params=pltpu.CompilerParams(vmem_limit_bytes=VMEM_LIMIT),
        cost_estimate=LIGHT,
        name="attn_backward",
    )(q, kv, kv, kv_other, kv_other, dout, out, e, ex, il)


EPSILON = 1e-05
TILE = 512


def _row(ref, layer):
    return ref[layer : layer + 1, :].astype(F32)


def _fill_turned(coords_ref, order, pieces, x_ref, xt_s, column_s, theirs=False):
    features = xt_s.shape[0]
    rows = features // pieces
    span = max(rows, 128)
    me = coords_ref[0]
    for start in range(0, features, span):
        turned = x_ref[:MAIN, start : start + span].T
        last = x_ref[MAIN:, start : start + span].T.astype(F32)[:, 0:1]
        for part in range(span // rows):
            relative = jnp.bitwise_xor(me, start // rows + part)
            place = jnp.int32(0)
            for bit in order:
                shift = jnp.bitwise_xor(coords_ref[1], bit ^ int(theirs)) if bit < 2 else bit
                place = place * 2 + (jnp.right_shift(relative, shift) & 1)
            at = pl.ds(pl.multiple_of(place * rows, rows), rows)
            xt_s[at, :] = turned[part * rows : (part + 1) * rows]
            column_s[at, :] = jnp.broadcast_to(last[part * rows : (part + 1) * rows], (rows, 128))


def _outer(xt_s, column_s, dy, out_ref):
    width = dy.shape[1]
    last_row = dy[MAIN:].astype(F32)[0:1]
    step = xt_s.shape[0] // 2
    for start in range(0, xt_s.shape[0], step):
        at = slice(start, start + step)
        column = jnp.concatenate([column_s[at, :]] * (width // 128), axis=1)
        total = _dot(xt_s[at, :], dy[:MAIN], ((1,), (0,))) + column * last_row
        out_ref[at, :] = total.astype(BF16)


def _moments(values):
    average = jnp.mean(values, axis=-1, keepdims=True)
    centred = values - average
    inverse = lax.rsqrt(jnp.mean(centred * centred, axis=-1, keepdims=True) + EPSILON)
    return centred * inverse, inverse


def _norm_back(normed, inverse, gain, grad):
    scaled = grad * gain
    first = jnp.mean(scaled, axis=-1, keepdims=True)
    second = jnp.mean(scaled * normed, axis=-1, keepdims=True)
    return (scaled - first - normed * second) * inverse


def _gelu_parts(up):
    square = up * up
    bell = jnp.exp(-0.5 * square)
    size = jnp.abs(up)
    t = 1.0 / (1.0 + (0.375 * 0.5**0.5) * size)
    terms = (
        0.21133947372436523, 0.21568892896175385, 0.16666550934314728, 0.2830598056316376,
        -0.1295955926179886, 0.3879369795322418, -0.1350957304239273,
    )
    value = jnp.full_like(t, 0.5 * terms[-1])
    for term in terms[-2::-1]:
        value = value * t + 0.5 * term
    tail = value * t * bell
    cumulative = jnp.where(up < 0.0, tail, 1.0 - tail)
    return up * cumulative, cumulative + up * (bell * 0.3989422804014327)


def _entry_kernel(
    layer, xa_ref, xb_ref, wa_ref, wb_ref, bias_ref, gain_ref, shift_ref, qa_ref, qb_ref,
    hidden_ref, normed_ref, q_ref, kv_ref, normed_s,
):
    step = pl.program_id(0)

    @pl.when(step == 0)
    def _():
        hidden = (
            _dot(xa_ref[...], wa_ref[...], ((1,), (0,)))
            + _dot(xb_ref[...], wb_ref[...], ((1,), (0,)))
            + _row(bias_ref, layer)
        )
        hidden_ref[...] = hidden
        normed, _unused = _moments(hidden)
        low = (normed * _row(gain_ref, layer) + _row(shift_ref, layer)).astype(BF16)
        normed_s[...] = low
        normed_ref[...] = low

    @pl.when(jnp.logical_and(step >= 1, step <= 2))
    def _():
        half = qa_ref.shape[1]
        kv_ref[:, :half] = _dot(normed_s[...], qa_ref[...], ((1,), (0,))).astype(BF16)
        kv_ref[:, half:] = _dot(normed_s[...], qb_ref[...], ((1,), (0,))).astype(BF16)

    @pl.when(step == 3)
    def _():
        half = qa_ref.shape[1]
        q_ref[:, :half] = _dot(normed_s[...], qa_ref[...], ((1,), (0,))).astype(BF16)
        q_ref[:, half:] = _dot(normed_s[...], qb_ref[...], ((1,), (0,))).astype(BF16)


def entry_forward(layer, xa, xb, wa, wb, bias, gain, shift, qa, qb):
    model = xa.shape[1]
    half = qa.shape[3]

    def part(step):
        return jnp.where(step == 3, 0, jnp.maximum(step, 1))

    rows = pl.BlockSpec((PAD, model), lambda j: (0, 0))
    square = pl.BlockSpec((None, None, model, model), lambda j: (layer, 0, 0, 0))
    single = pl.BlockSpec((None, None, model, model), lambda j: (0, 0, 0, 0))
    vector = pl.BlockSpec(bias.shape, lambda j: (0, 0))
    third = pl.BlockSpec((None, None, model, half), lambda j: (layer, part(j), 0, 0))
    single_third = pl.BlockSpec((None, None, model, half), lambda j: (0, part(j), 0, 0))
    return pl.pallas_call(
        functools.partial(_entry_kernel, layer),
        grid=(4,),
        in_specs=[rows, rows, square, single, vector, vector, vector, third, single_third],
        out_specs=[
            rows,
            rows,
            rows,
            pl.BlockSpec((PAD, 2 * half), lambda j: (0, jnp.clip(j - 1, 0, 1))),
        ],
        out_shape=[
            jax.ShapeDtypeStruct((PAD, model), F32),
            jax.ShapeDtypeStruct((PAD, model), BF16),
            jax.ShapeDtypeStruct((PAD, 2 * half), BF16),
            jax.ShapeDtypeStruct((PAD, 4 * half), BF16),
        ],
        scratch_shapes=[pltpu.VMEM((PAD, model), BF16)],
        compiler_params=pltpu.CompilerParams(vmem_limit_bytes=VMEM_LIMIT),
        cost_estimate=LIGHT,
        name="entry_forward",
    )(xa, xb, wa, wb, bias, gain, shift, qa, qb)


class _Refs:
    def __init__(self):
        self.names, self.values = [], []

    def add(self, name, *value):
        self.names.append(name)
        self.values.append(value[0] if len(value) == 1 else value)


def _mlp_kernel(names, plan, coords_ref, *refs):
    layer, first, last, forward, backward, sets, pieces, order = plan
    ref = dict(zip(names, refs, strict=True))
    step = pl.program_id(0)
    steps_per_set = pl.num_programs(0) // len(sets)

    @pl.when(step == 0)
    def _():
        if first and forward:
            half = ref["proj_own"].shape[1]
            middle = (
                ref["hidden"][...]
                + _dot(ref["attended"][:, :half], ref["proj_own"][...], ((1,), (1,)))
                + _dot(ref["attended"][:, half:], ref["proj_peer"][...], ((1,), (1,)))
                + _row(ref["proj_bias"], layer)
            )
            ref["middle_out"][...] = middle
            normed, _unused = _moments(middle)
            low = (normed * _row(ref["gain"], layer) + _row(ref["shift"], layer)).astype(BF16)
            ref["normed_out"][...] = low
            ref["normed_s"][...] = low
            ref["acc_s"][...] = middle + _row(ref["down_bias"], layer)
        else:
            ref["normed_s"][...] = ref["normed"][...]
            if forward:
                ref["acc_s"][...] = ref["acc"][...]
        if backward:
            assert len(sets) == 1
            ref["grad_s"][...] = ref["grad"][...].astype(BF16)
            if first:
                ref["dn_s"][...] = jnp.zeros_like(ref["dn_s"])
            else:
                ref["dn_s"][...] = ref["dn"][...]
            _fill_turned(coords_ref, order, pieces, ref["grad_s"], ref["grad_t"], ref["grad_c"], sets[0] == "peer")
            _fill_turned(coords_ref, order, pieces, ref["normed_s"], ref["normed_t"], ref["normed_c"], sets[0] == "peer")

    for number, name in enumerate(sets):

        def tile(name=name):
            up_w = ref["up_" + name]
            down_w = ref["down_" + name]
            if forward:
                up = _dot(ref["normed_s"][...], up_w[...], ((1,), (0,))) + _row(ref["up_bias_" + name], layer)
                active, slope = _gelu_parts(up)
                active = active.astype(BF16)
                ref["acc_s"][...] += _dot(active, down_w[...], ((1,), (1,)))
                if not backward:
                    ref["active_" + name][...] = active
                    ref["slope_" + name][...] = slope.astype(BF16)
            else:
                active = ref["active_" + name][...]
                slope = ref["slope_" + name][...].astype(F32)
            if backward:
                du = _dot(ref["grad_s"][...], down_w[...], ((1,), (0,))) * slope
                ref["up_bias_grad_" + name][...] = jnp.sum(du, axis=0, keepdims=True)
                du = du.astype(BF16)
                ref["dn_s"][...] += _dot(du, up_w[...], ((1,), (1,)))
                _outer(ref["grad_t"], ref["grad_c"], active, ref["grads_own"].at[0] if name == "own" else ref["down_grad"])
                _outer(ref["normed_t"], ref["normed_c"], du, ref["grads_own"].at[1] if name == "own" else ref["up_grad"])

        if len(sets) == 1:
            tile()
        else:
            pl.when(step // steps_per_set == number)(tile)

    @pl.when(step == pl.num_programs(0) - 1)
    def _():
        if not last:
            if forward:
                ref["acc_out"][...] = ref["acc_s"][...]
            if backward:
                ref["dn_out"][...] = ref["dn_s"][...]
            return
        if forward:
            ref["result"][...] = ref["acc_s"][...].astype(BF16)
        if backward:
            gradient = ref["grad"][...].astype(F32)
            dn = ref["dn_s"][...]
            normed, inverse = _moments(ref["middle"][...])
            sums = ref["sums"]
            sums[0:1, :] = jnp.sum(gradient, axis=0, keepdims=True)
            sums[1:2, :] = jnp.sum(dn * normed, axis=0, keepdims=True)
            sums[2:3, :] = jnp.sum(dn, axis=0, keepdims=True)
            dmid = gradient + _norm_back(normed, inverse, _row(ref["gain"], layer), dn)
            sums[3:4, :] = jnp.sum(dmid, axis=0, keepdims=True)
            sums[4:8, :] = jnp.zeros_like(sums[4:8, :])
            ref["dmid"][...] = dmid
            low = dmid.astype(BF16)
            half = ref["proj_own"].shape[1]
            for at, name in ((0, "own"), (half, "peer")):
                ref["dattn"][:, at : at + half] = _dot(low, ref["proj_" + name][...], ((1,), (0,))).astype(BF16)


def mlp(layer, first, last, forward, backward, sets, pieces, order, values):
    _unused, model, units = values["up_" + sets[0]].shape
    steps = units // TILE
    plan = (layer, first, last, forward, backward, sets, pieces, order)
    names, in_specs, operands = [], [], []
    rows = pl.BlockSpec((PAD, model), lambda j, c: (0, 0))
    vector = pl.BlockSpec(values["gain"].shape, lambda j, c: (0, 0))

    def take(name, spec):
        names.append(name)
        in_specs.append(spec)
        operands.append(values[name])

    def moving(number, shape):
        def index(j, c):
            tile = (0, jnp.clip(j - number * steps, 0, steps - 1))
            return tile if len(shape) == 2 else (layer, *tile)

        return pl.BlockSpec(shape, index)

    half = values["proj_own"].shape[2]
    whole_proj = pl.BlockSpec((None, model, half), lambda j, c: (layer, 0, 0))

    if first and forward:
        for name, spec in (("hidden", rows), ("attended", rows), ("proj_own", whole_proj), ("proj_peer", whole_proj),
                           ("proj_bias", vector), ("gain", vector), ("shift", vector), ("down_bias", vector)):
            take(name, spec)
    else:
        take("normed", rows)
        if forward:
            take("acc", rows)
    if backward:
        take("grad", rows)
        if not first:
            take("dn", rows)
        if last:
            take("middle", rows)
            for name, spec in (("proj_own", whole_proj), ("proj_peer", whole_proj), ("gain", vector)):
                if name not in names:
                    take(name, spec)
    for number, name in enumerate(sets):
        take("up_" + name, moving(number, (None, model, TILE)))
        take("down_" + name, moving(number, (None, model, TILE)))
        if forward:
            take("up_bias_" + name, moving(number, (2, TILE)))
        else:
            take("active_" + name, moving(number, (PAD, TILE)))
            take("slope_" + name, moving(number, (PAD, TILE)))
    out_names, out_specs, out_shape = [], [], []

    def give(name, spec, shape, kind):
        out_names.append(name)
        out_specs.append(spec)
        out_shape.append(jax.ShapeDtypeStruct(shape, kind))

    full = (PAD, model)
    if first and forward:
        give("middle_out", rows, full, F32)
        give("normed_out", rows, full, BF16)
    if not last:
        if forward:
            give("acc_out", rows, full, F32)
        if backward:
            give("dn_out", rows, full, F32)
    else:
        if forward:
            give("result", rows, full, BF16)
        if backward:
            give("sums", pl.BlockSpec((8, model), lambda j, c: (0, 0)), (8, model), F32)
            give("dmid", rows, full, F32)
            give("dattn", rows, full, BF16)
    for number, name in enumerate(sets):
        if forward and not backward:
            for kind in ("active_", "slope_"):
                give(kind + name, moving(number, (PAD, TILE)), (PAD, units), BF16)
        if backward:
            stacked = pl.BlockSpec(
                (2, model, TILE),
                lambda j, c, number=number: (0, 0, jnp.clip(j - number * steps, 0, steps - 1)),
            )
            if name == "own":
                give("grads_own", stacked, (2, model, units), BF16)
            else:
                for kind in ("down_grad", "up_grad"):
                    give(kind, moving(number, (model, TILE)), (model, units), BF16)
            give("up_bias_grad_" + name, moving(number, (1, TILE)), (1, units), F32)
    scratch_names = ["normed_s"]
    scratch = [pltpu.VMEM(full, BF16)]
    if forward:
        scratch_names.append("acc_s")
        scratch.append(pltpu.VMEM(full, F32))
    if backward:
        for name, shape, kind in (("grad_s", full, BF16), ("dn_s", full, F32), ("grad_t", (model, MAIN), BF16),
                                  ("grad_c", (model, 128), F32), ("normed_t", (model, MAIN), BF16),
                                  ("normed_c", (model, 128), F32)):
            scratch_names.append(name)
            scratch.append(pltpu.VMEM(shape, kind))
    results = pl.pallas_call(
        functools.partial(_mlp_kernel, tuple(names + out_names + scratch_names), plan),
        grid_spec=pltpu.PrefetchScalarGridSpec(
            num_scalar_prefetch=1,
            grid=(steps * len(sets),),
            in_specs=in_specs,
            out_specs=out_specs,
            scratch_shapes=scratch,
        ),
        out_shape=out_shape,
        compiler_params=pltpu.CompilerParams(vmem_limit_bytes=VMEM_LIMIT),
        cost_estimate=LIGHT,
        name="mlp_" + ("f" if forward else "") + ("b" if backward else "") + "_" + "_".join(sets),
    )(values["coords"], *operands)
    return dict(zip(out_names, results, strict=True))


def _entry_back_kernel(
    layer, pieces, order, coords_ref, dq_ref, dk_ref, dk_got_ref, dv_ref, dv_got_ref, dmid_ref, hidden_ref,
    normed_ref, xa_ref, xb_ref, attended_ref, gain_ref, qa_ref, qb_ref, wa_ref, wb_ref,
    own_ref, peer_ref, peer_rest_ref, back_ref, skip_back_ref, sums_ref,
    da_s, low_s, xt_s, column_s, yt_s, column_y,
):
    step = pl.program_id(0)
    half = qa_ref.shape[1]

    def turn(x_ref, to_s, to_c, theirs):
        _fill_turned(coords_ref, order, pieces, x_ref, to_s, to_c, theirs)

    @pl.when(step == 0)
    def _():
        da_s[...] = jnp.zeros_like(da_s)
        turn(normed_ref, xt_s, column_s, False)
        turn(normed_ref, yt_s, column_y, True)

    def columns(refs):
        def run():
            total = refs[0][...]
            if len(refs) == 2:
                total = (total.astype(F32) + refs[1][...].astype(F32)).astype(BF16)
            own, peer = total[:, :half], total[:, half:]
            da_s[...] += _dot(own, qa_ref[...], ((1,), (1,))) + _dot(peer, qb_ref[...], ((1,), (1,)))
            _outer(xt_s, column_s, own, own_ref)
            _outer(yt_s, column_y, peer, peer_ref)

        return run

    pl.when(step == 0)(columns((dq_ref,)))
    pl.when(step == 1)(columns((dk_ref, dk_got_ref)))
    pl.when(step == 2)(columns((dv_ref, dv_got_ref)))

    @pl.when(step == 3)
    def _():
        da = da_s[...]
        normed, inverse = _moments(hidden_ref[...])
        sums_ref[0:1, :] = jnp.sum(da * normed, axis=0, keepdims=True)
        sums_ref[1:2, :] = jnp.sum(da, axis=0, keepdims=True)
        dhid = dmid_ref[...] + _norm_back(normed, inverse, _row(gain_ref, layer), da)
        sums_ref[2:3, :] = jnp.sum(dhid, axis=0, keepdims=True)
        sums_ref[3:8, :] = jnp.zeros_like(sums_ref[3:8, :])
        low_s[...] = dhid.astype(BF16)
        turn(xa_ref, xt_s, column_s, False)
        turn(xb_ref, yt_s, column_y, True)

    for number in range(2):

        @pl.when(step == 3 + number)
        def _(number=number):
            dy = low_s[:, number * half : (number + 1) * half]
            _outer(xt_s, column_s, dy, own_ref)
            _outer(yt_s, column_y, dy, peer_rest_ref)

    @pl.when(step == 4)
    def _():
        first = coords_ref[1] == 0
        one = _dot(low_s[...], wa_ref[...], ((1,), (1,)))
        two = _dot(low_s[...], wb_ref[...], ((1,), (1,)))
        back_ref[...] = jnp.where(first, one, two)
        skip_back_ref[...] = jnp.where(first, two, one).astype(BF16)

    @pl.when(step == 5)
    def _():
        low_s[...] = dmid_ref[...].astype(BF16)
        turn(low_s, xt_s, column_s, False)
        turn(low_s, yt_s, column_y, True)
        _outer(xt_s, column_s, attended_ref[:, :half], own_ref)
        _outer(yt_s, column_y, attended_ref[:, half:], peer_rest_ref)


def entry_backward(layer, pieces, order, coords, dq, dk, dk_got, dv, dv_got, dmid, hidden, normed, xa, xb, attended, gain, qa, qb, wa, wb):
    model = xa.shape[1]
    half = qa.shape[3]
    rows = pl.BlockSpec((PAD, model), lambda j, c: (0, 0))
    linear = pl.BlockSpec((None, None, model, model), lambda j, c: (layer, 0, 0, 0))
    single = pl.BlockSpec((None, None, model, model), lambda j, c: (0, 0, 0, 0))
    single_third = pl.BlockSpec((None, None, model, half), lambda j, c: (0, jnp.minimum(j, 2), 0, 0))
    vector = pl.BlockSpec(gain.shape, lambda j, c: (0, 0))
    third = pl.BlockSpec((None, None, model, half), lambda j, c: (layer, jnp.minimum(j, 2), 0, 0))
    grads = pl.BlockSpec((model, half), lambda j, c: (0, j))
    early = pl.BlockSpec((model, half), lambda j, c: (0, jnp.minimum(j, 2)))
    late = pl.BlockSpec((model, half), lambda j, c: (0, jnp.maximum(j, 3) - 3))
    weight = jax.ShapeDtypeStruct((model, 6 * half), BF16)
    part = jax.ShapeDtypeStruct((model, 3 * half), BF16)
    return pl.pallas_call(
        functools.partial(_entry_back_kernel, layer, pieces, order),
        grid_spec=pltpu.PrefetchScalarGridSpec(
            num_scalar_prefetch=1,
            grid=(6,),
            in_specs=[rows] * 11 + [vector, third, single_third, linear, single],
            out_specs=[grads, early, late, rows, rows, pl.BlockSpec((8, model), lambda j, c: (0, 0))],
            scratch_shapes=[
                pltpu.VMEM((PAD, model), F32),
                pltpu.VMEM((PAD, model), BF16),
                pltpu.VMEM((model, MAIN), BF16),
                pltpu.VMEM((model, 128), F32),
                pltpu.VMEM((model, MAIN), BF16),
                pltpu.VMEM((model, 128), F32),
            ],
        ),
        out_shape=[
            weight,
            part,
            part,
            jax.ShapeDtypeStruct((PAD, model), F32),
            jax.ShapeDtypeStruct((PAD, model), BF16),
            jax.ShapeDtypeStruct((8, model), F32),
        ],
        compiler_params=pltpu.CompilerParams(vmem_limit_bytes=VMEM_LIMIT),
        cost_estimate=LIGHT,
        name="entry_backward",
    )(coords, dq, dk, dk_got, dv, dv_got, dmid, hidden, normed, xa, xb, attended, gain, qa, qb, wa, wb)


def _gather_kernel(count, core_ref, *refs):
    first = core_ref[0] == 0
    out_ref = refs[-1]
    for layer in range(count):
        mine, theirs = refs[2 * layer][...], refs[2 * layer + 1][...]
        low = jnp.where(first, mine, theirs)
        high = jnp.where(first, theirs, mine)
        for start, part in ((0, low[:MAIN]), (MAIN, high[:MAIN]), (2 * MAIN, low[MAIN : MAIN + 1]), (2 * MAIN + 1, high[MAIN : MAIN + 1])):
            at = slice(start, start + part.shape[0])
            if count == 1:
                out_ref[at, :] = part
            else:
                out_ref[at, layer, :] = part


def gather_rows(core, *pairs):
    width = pairs[0][0].shape[1]
    count = len(pairs)
    shape = (2 * MAIN + 2, width) if count == 1 else (2 * MAIN + 2, count, width)
    flat = [value for pair in pairs for value in pair]
    return pl.pallas_call(
        functools.partial(_gather_kernel, count),
        in_specs=[pl.BlockSpec(memory_space=pltpu.SMEM)] + [pl.BlockSpec(memory_space=pltpu.VMEM)] * len(flat),
        out_specs=pl.BlockSpec(memory_space=pltpu.VMEM),
        out_shape=jax.ShapeDtypeStruct(shape, BF16),
        compiler_params=pltpu.CompilerParams(vmem_limit_bytes=VMEM_LIMIT),
        cost_estimate=LIGHT,
        name="gather_rows",
    )(jnp.reshape(core, (1,)).astype(jnp.int32), *flat)


def swap_cores(value):
    return lax.ppermute(value, "tensor", [(0, 1), (1, 0)])


def swap_bit(value, bit, size, crossed):
    cores = 2
    pairs = []
    for index in range(size):
        for core in range(cores):
            other = index ^ (1 << ((bit ^ core) if crossed and bit < 2 else bit))
            pairs.append((index * cores + core, other * cores + core))
    return lax.ppermute(value, ("dp", "tensor"), pairs)


def after(value, *others):
    return lax.optimization_barrier((value, others))[0]


def total(parts):
    result = parts[0].astype(F32)
    for part in parts[1:]:
        result = result + part.astype(F32)
    return result


class Reduction:
    def __init__(self, parts, order, size, axis=0, crossed=True):
        self.parts = [(part if isinstance(part, tuple) else (part,), 0) for part in parts]
        self.length, self.order, self.size = parts[0].shape[axis], list(order), size
        self.axis, self.crossed = axis, crossed

    def span(self, start, stop):
        values = []
        for arrays, at in self.parts:
            if len(arrays) == 1:
                values.append(lax.slice_in_dim(arrays[0], at + start, at + stop, axis=self.axis))
            elif self.axis == 1:
                values.append(jnp.stack([array[at + start : at + stop] for array in arrays]))
            else:
                values.append(jnp.concatenate([array[at + start : at + stop] for array in arrays], axis=1))
        return total(values)

    def send(self, gate):
        bit = self.order.pop(0)
        half = self.length // 2
        held = lax.optimization_barrier(([arrays for arrays, _ in self.parts], gate))[0]
        self.parts = [(arrays, at) for arrays, (_, at) in zip(held, self.parts)]
        payload = self.span(half, self.length).astype(held[0][0].dtype)
        self.parts.append(((swap_bit(payload, bit, self.size, self.crossed),), 0))
        self.length = half
        return payload

    def result(self):
        return self.span(0, self.length)


def arrange(value, order, size):
    bits = size.bit_length() - 1
    index = lax.axis_index("dp")
    view = value.reshape((2,) * bits + value.shape[1:])
    for bit in range(bits):
        axis = bits - 1 - bit
        view = jnp.where((index >> bit) & 1 == 1, jnp.flip(view, axis), view)
    axes = [bits - 1 - bit for bit in order] + list(range(bits, view.ndim))
    return view.transpose(axes).reshape(value.shape)


def localize(value, core):
    main = lax.dynamic_slice_in_dim(value, core * MAIN, MAIN, 0)
    extra = lax.dynamic_slice_in_dim(value, 2 * MAIN + core, 1, 0)
    blank = jnp.zeros((PAD - MAIN - 1,) + value.shape[1:], value.dtype)
    return jnp.concatenate([main, extra, blank], axis=0)


def globalize(core, *mine):
    return gather_rows(core, *((value, swap_cores(value)) for value in mine))


def sum_vectors(shared, up_own, up_peer, size):
    count, model = shared.shape
    layers, units = up_own.shape
    order = tuple(range(size.bit_length() - 1))

    def blocks(offsets):
        first = shared.reshape(count, size, model // size).transpose(1, 0, 2)
        second = offsets.reshape(layers, size, units // model, model // size)
        second = second.transpose(1, 0, 2, 3).reshape(size, -1, model // size)
        return arrange(jnp.concatenate([first, second], axis=1), order, size)

    return Reduction([blocks(up_own), swap_cores(blocks(up_peer))], order, size, crossed=False)


def body(
    inputs, skips, cotangent, skip_weight, skip_bias, attn_norm_gain, attn_norm_bias, qkv_weight,
    proj_weight, proj_bias, ffn_norm_gain, ffn_norm_bias, up_weight, up_bias, down_weight, down_bias,
):
    core = lax.axis_index("tensor")
    size = lax.axis_size("dp")
    bits = size.bit_length() - 1
    assert size == 1 << bits and bits >= 2
    order = tuple(range(bits))
    layers, model = skip_bias.shape
    assert layers == 2
    coords = jnp.stack([lax.axis_index("dp"), core]).astype(jnp.int32)

    qkv_turned = qkv_weight.transpose(0, 2, 1, 3)
    skip_own = [skip_weight[layer : layer + 1] for layer in range(layers)]
    qkv_own = [qkv_turned[layer : layer + 1] for layer in range(layers)]
    skip_peer = [swap_cores(skip_own[0]), None]
    qkv_peer = [swap_cores(qkv_own[0]), None]
    up_bias_peer = swap_cores(up_bias)
    weights = {
        "coords": coords, "proj_own": proj_weight, "up_own": up_weight, "down_own": down_weight,
        "up_bias_own": up_bias, "up_bias_peer": up_bias_peer, "proj_bias": proj_bias,
        "down_bias": down_bias, "gain": ffn_norm_gain, "shift": ffn_norm_bias,
    }
    skip_parts = localize(skips.transpose(1, 0, 2), core)

    def enter(layer, residual):
        skip_rows = skip_parts[:, layer]
        xa = jnp.where(core == 0, residual, skip_rows)
        xb = jnp.where(core == 0, skip_rows, residual)
        hidden, normed, q, kv = entry_forward(
            layer, xa, xb, skip_weight, skip_peer[layer], skip_bias, attn_norm_gain, attn_norm_bias,
            qkv_turned, qkv_peer[layer],
        )
        kv_other = swap_cores(kv)
        attended, exact, e, ex, il = attn_forward(q, kv, kv_other)
        return dict(xa=xa, xb=xb, hidden=hidden, normed=normed, q=q, kv=kv, kv_other=kv_other,
                    attended=attended, exact=exact, e=e, ex=ex, il=il)

    items = {}

    def add(layer, name, own, peer, axis):
        theirs = tuple(swap_cores(value) for value in peer)
        items[name, layer] = Reduction([own, theirs], order, size, axis)

    def sends(gate, *keys):
        made = []
        for key in keys:
            if items[key].order:
                made.append(items[key].send(gate))
        return after(gate, *made)

    def back(layer, kept, mid, dattn, *keys):
        dq, dk, dk_other, dv, dv_other = attn_backward(
            kept["q"], kept["kv"], kept["kv_other"], dattn, kept["exact"], kept["e"], kept["ex"], kept["il"]
        )
        dk_got, dv_got = swap_cores(dk_other), swap_cores(dv_other)
        dq = sends(dq, *keys)
        own, peer, peer_rest, gradient, skip_grad, sums = entry_backward(
            layer, size, order, coords, dq, dk, dk_got, dv, dv_got, mid["dmid"], kept["hidden"], kept["normed"],
            kept["xa"], kept["xb"], kept["attended"], attn_norm_gain, qkv_turned, qkv_peer[layer],
            skip_weight, skip_peer[layer],
        )
        add(layer, "attn", own, (peer, peer_rest), 0)
        return gradient, skip_grad, sums

    kept = [None] * layers
    kept[0] = enter(0, localize(inputs, core))
    weights["up_peer"] = swap_cores(after(up_weight, skip_peer[0], qkv_peer[0]))
    late = after((proj_weight, down_weight, skip_own[1], qkv_own[1]), kept[0]["kv_other"])
    weights["proj_peer"], weights["down_peer"], skip_peer[1], qkv_peer[1] = (swap_cores(item) for item in late)
    mid0 = mlp(0, True, True, True, False, ("peer", "own"), size, order, {**weights, **kept[0]})
    kept[1] = enter(1, mid0["result"])
    values = {**weights, **kept[1], "grad": localize(cotangent, core)}
    one = mlp(1, True, False, True, True, ("peer",), size, order, values)
    values.update(normed=one["normed_out"], middle=one["middle_out"], acc=one["acc_out"], dn=one["dn_out"])
    two = mlp(1, False, True, True, True, ("own",), size, order, values)
    add(1, "mlp", two["grads_own"], (one["down_grad"], one["up_grad"]), 1)
    output = globalize(core, two["result"])
    dattn = sends(two["dattn"], ("mlp", 1))
    gradient, skip_grad1, sums1 = back(1, kept[1], two, dattn)
    gradient = sends(gradient, ("mlp", 1))

    values = {**weights, **kept[0], **mid0, "normed": mid0["normed_out"], "middle": mid0["middle_out"], "grad": gradient}
    one0 = mlp(0, True, False, False, True, ("peer",), size, order, values)
    values.update(dn=sends(one0["dn_out"], ("attn", 1), ("mlp", 1)))
    low = mlp(0, False, True, False, True, ("own",), size, order, values)
    add(0, "mlp", low["grads_own"], (one0["down_grad"], one0["up_grad"]), 1)
    dattn = sends(low["dattn"], ("mlp", 0), ("mlp", 1))
    gradient, skip_grad0, sums0 = back(0, kept[0], low, dattn, ("attn", 1))
    shared = jnp.concatenate([low["sums"][:4], two["sums"][:4], sums0[:3], sums1[:3]], axis=0)
    items["vectors", 0] = sum_vectors(
        shared,
        jnp.concatenate([low["up_bias_grad_own"], two["up_bias_grad_own"]], axis=0),
        jnp.concatenate([one0["up_bias_grad_peer"], one["up_bias_grad_peer"]], axis=0),
        size,
    )
    finish = gradient
    for keys in (
        (("mlp", 0), ("attn", 1)),
        (("attn", 0),),
        (("vectors", 0),),
        (("mlp", 0), ("attn", 1), ("vectors", 0)),
        (("attn", 0), ("vectors", 0)),
        (("mlp", 0), ("vectors", 0)),
        (("attn", 0),),
        (("attn", 0),),
    ):
        finish = sends(finish, *keys)
    while any(item.order for item in items.values()):
        finish = sends(finish, *items)
    result = {key: item.result() for key, item in items.items()}
    count = shared.shape[0]
    vectors = result["vectors", 0][0, :count]
    up_bias_grad = result["vectors", 0][0, count:].reshape(layers, -1)
    input_grad = globalize(core, gradient.astype(BF16))
    skip_grad = globalize(core, skip_grad0, skip_grad1).transpose(1, 0, 2)
    outer = vectors[:8].reshape(2, 4, -1)
    inner = vectors[8:].reshape(2, 3, -1)

    half = model // 2

    def columns(start, stop):
        return jnp.stack([result["attn", layer][:, start:stop] for layer in range(layers)])

    def matrix(which):
        return jnp.stack([result["mlp", layer][which] for layer in range(layers)])

    return (
        output, input_grad, skip_grad, columns(3 * half, 5 * half)[:, None],
        inner[:, 2], inner[:, 0], inner[:, 1],
        columns(0, 3 * half).reshape(layers, -1, 3, qkv_weight.shape[3]), columns(5 * half, 6 * half),
        outer[:, 3], outer[:, 1], outer[:, 2],
        matrix(1), up_bias_grad, matrix(0), outer[:, 0],
    )


def solution(mesh):
    return jax.shard_map(
        body,
        mesh=mesh,
        in_specs=(
            P("dp", None), P(None, "dp", None), P("dp", None), P(None, "tensor", None, None), P(), P(),
            P(), P(None, None, None, "tensor"), P(None, None, "tensor"), P(), P(), P(),
            P(None, None, "tensor"), P(None, "tensor"), P(None, None, "tensor"), P(),
        ),
        out_specs=(
            P("dp", None), P("dp", None), P(None, "dp", None), P(None, "tensor", "dp", None),
            P(None, "dp"), P(None, "dp"), P(None, "dp"), P(None, "dp", None, "tensor"),
            P(None, "dp", "tensor"), P(None, "dp"), P(None, "dp"), P(None, "dp"),
            P(None, "dp", "tensor"), P(None, ("tensor", "dp")), P(None, "dp", "tensor"), P(None, "dp"),
        ),
        check_vma=False,
    )
```

```python
import functools
import math
import types

import jax
import jax.numpy as jnp
from jax import lax
from jax.experimental import pallas as pl
from jax.experimental.pallas import tpu as pltpu
from jax.sharding import PartitionSpec as P

F32 = jnp.float32
BF16 = jnp.bfloat16
HD = 64
MAIN = 512
PAD = 528
GROUP = 256
HEADS_IN_GROUP = GROUP // HD
MIB = 1024 * 1024
SCALE = 0.5


def cost(microseconds):
    return pl.CostEstimate(flops=1, bytes_accessed=int(microseconds * SCALE * 3.5e6), transcendentals=0)


def _dot(a, b, dims):
    return lax.dot_general(a, b, (dims, ((), ())), preferred_element_type=F32)


def _extra_rows(mine_ref, other_ref):
    row = lax.broadcasted_iota(jnp.int32, (16, GROUP), 0)
    lane = lax.broadcasted_iota(jnp.int32, (16, GROUP), 1)
    mine = jnp.broadcast_to(mine_ref[MAIN : MAIN + 16, :][0:1].astype(F32), (16, GROUP))
    other = jnp.broadcast_to(other_ref[MAIN : MAIN + 16, :][0:1].astype(F32), (16, GROUP))
    value = jnp.where(row % 2 == 0, mine, other)
    return jnp.where(row // 2 == lane // HD, value, 0.0).astype(BF16)


def _attn_fwd_kernel(q_ref, km_ref, vm_ref, ko_ref, vo_ref, o_ref, of_ref, e_ref, ex_ref, il_ref, k_s, v_s):
    k_s[:MAIN] = km_ref[:MAIN]
    k_s[MAIN:] = ko_ref[:MAIN]
    v_s[:MAIN] = vm_ref[:MAIN]
    v_s[MAIN:] = vo_ref[:MAIN]
    lane = lax.broadcasted_iota(jnp.int32, (PAD, GROUP), 1) // HD
    slot = lax.broadcasted_iota(jnp.int32, (PAD, 16), 1) // 2
    q = q_ref[...] * jnp.asarray(HD**-0.5, BF16)
    kx = _extra_rows(km_ref, ko_ref)
    vx = _extra_rows(vm_ref, vo_ref)
    sx = _dot(q, kx, ((1,), (1,)))
    out = jnp.zeros((PAD, GROUP), F32)
    ex_all = jnp.zeros((PAD, 16), F32)
    il_all = jnp.zeros((PAD, 16), F32)
    for h in range(HEADS_IN_GROUP):
        qh = jnp.where(lane == h, q, jnp.zeros_like(q))
        s = _dot(qh, k_s[...], ((1,), (1,)))
        sxh = jnp.where(slot == h, sx, -jnp.inf)
        top = jnp.maximum(jnp.max(s, axis=1, keepdims=True), jnp.max(sxh, axis=1, keepdims=True))
        e = jnp.exp(s - top)
        exh = jnp.exp(sxh - top)
        total = jnp.sum(e, axis=1, keepdims=True) + jnp.sum(exh, axis=1, keepdims=True)
        inverse = 1.0 / total
        low = e.astype(BF16)
        e_ref[h] = low
        out = out + jnp.where(lane == h, _dot(low, v_s[...], ((1,), (0,))) * inverse, 0.0)
        ex_all = ex_all + exh
        il_all = il_all + jnp.where(slot == h, inverse, 0.0)
    out = out + _dot((ex_all * il_all).astype(BF16), vx, ((1,), (0,)))
    o_ref[...] = out.astype(BF16)
    of_ref[...] = out
    ex_ref[0] = ex_all
    il_ref[0] = il_all


def _far(value):
    return pltpu.with_memory_space_constraint(value, pltpu.HBM)


def attn_forward(q, kv, kv_other):
    width = q.shape[1]
    groups = width // GROUP

    def near(offset):
        return pl.BlockSpec((PAD, GROUP), lambda g: (0, g + offset))

    def far(offset):
        return pl.BlockSpec((PAD, GROUP), lambda g: (0, (g + groups // 2) % groups + offset))

    heads = width // HD
    kv, kv_other = _far(kv), _far(kv_other)
    return pl.pallas_call(
        _attn_fwd_kernel,
        grid=(groups,),
        in_specs=[near(0), near(0), near(groups), far(0), far(groups)],
        out_specs=[
            near(0),
            near(0),
            pl.BlockSpec((HEADS_IN_GROUP, PAD, 2 * MAIN), lambda g: (g, 0, 0)),
            pl.BlockSpec((1, PAD, 16), lambda g: (g, 0, 0)),
            pl.BlockSpec((1, PAD, 16), lambda g: (g, 0, 0)),
        ],
        out_shape=[
            pltpu.HBM((PAD, width), BF16),
            pltpu.HBM((PAD, width), F32),
            pltpu.HBM((heads, PAD, 2 * MAIN), BF16),
            pltpu.HBM((groups, PAD, 16), F32),
            pltpu.HBM((groups, PAD, 16), F32),
        ],
        scratch_shapes=[pltpu.VMEM((2 * MAIN, GROUP), BF16), pltpu.VMEM((2 * MAIN, GROUP), BF16)],
        compiler_params=pltpu.CompilerParams(vmem_limit_bytes=24 * MIB),
        cost_estimate=cost(19),
        name="attn_forward",
    )(q, kv, kv, kv_other, kv_other)


def _attn_bwd_kernel(
    q_ref, km_ref, vm_ref, ko_ref, vo_ref, do_ref, o_ref, e_ref, ex_ref, il_ref,
    dq_ref, dkm_ref, dko_ref, dvm_ref, dvo_ref, k_s, v_s, dk_s, dv_s,
):
    k_s[:MAIN] = km_ref[:MAIN]
    k_s[MAIN:] = ko_ref[:MAIN]
    v_s[:MAIN] = vm_ref[:MAIN]
    v_s[MAIN:] = vo_ref[:MAIN]
    scale = HD**-0.5
    lane = lax.broadcasted_iota(jnp.int32, (PAD, GROUP), 1) // HD
    slot = lax.broadcasted_iota(jnp.int32, (PAD, 16), 1) // 2
    q = q_ref[...] * jnp.asarray(scale, BF16)
    kx = _extra_rows(km_ref, ko_ref)
    vx = _extra_rows(vm_ref, vo_ref)
    il = il_ref[0]
    do = do_ref[...].astype(F32)
    spread = jnp.zeros((PAD, GROUP), F32)
    for h in range(HEADS_IN_GROUP):
        spread = jnp.where(lane == h, il[:, 2 * h : 2 * h + 1], spread)
    dos = (do * spread).astype(BF16)
    product = dos.astype(F32) * o_ref[...]
    inner = jnp.zeros((PAD, 16), F32)
    inners = []
    for h in range(HEADS_IN_GROUP):
        one = jnp.sum(jnp.where(lane == h, product, 0.0), axis=1, keepdims=True)
        inners.append(one)
        inner = jnp.where(slot == h, one, inner)
    dos_t = dos.T
    q_t = q.T
    dq = jnp.zeros((PAD, GROUP), F32)
    for h in range(HEADS_IN_GROUP):
        rows = slice(h * HD, (h + 1) * HD)
        dosh = jnp.where(lane == h, dos, jnp.zeros_like(dos))
        e = e_ref[h]
        dp = _dot(dosh, v_s[...], ((1,), (1,)))
        ds = (e.astype(F32) * (dp - inners[h])).astype(BF16)
        dq = dq + jnp.where(lane == h, _dot(ds, k_s[...], ((1,), (0,))), 0.0)
        dk_s[rows, :] = (
            _dot(q_t[rows, :MAIN], ds[:MAIN], ((1,), (0,)))
            + q_t[rows, MAIN : MAIN + 1].astype(F32) * ds[MAIN : MAIN + 16].astype(F32)[0:1]
        )
        dv_s[rows, :] = (
            _dot(dos_t[rows, :MAIN], e[:MAIN], ((1,), (0,)))
            + dos_t[rows, MAIN : MAIN + 1].astype(F32) * e[MAIN : MAIN + 16].astype(F32)[0:1]
        )
    ex = ex_ref[0]
    dsx = (ex * (_dot(dos, vx, ((1,), (1,))) - inner)).astype(BF16)
    dq = dq + _dot(dsx, kx, ((1,), (0,)))
    dq_ref[...] = (dq * scale).astype(BF16)
    dkx = _dot(dsx, q, ((0,), (0,)))
    dvx = _dot(ex.astype(BF16), dos, ((0,), (0,)))
    row = lax.broadcasted_iota(jnp.int32, (16, GROUP), 0)
    own = row // 2 == lax.broadcasted_iota(jnp.int32, (16, GROUP), 1) // HD
    for half, (dk_ref, dv_ref) in enumerate(((dkm_ref, dvm_ref), (dko_ref, dvo_ref))):
        keep = jnp.logical_and(own, row % 2 == half)
        for ref, grad_s, tail in ((dk_ref, dk_s, dkx), (dv_ref, dv_s, dvx)):
            ref[:MAIN] = grad_s[:, half * MAIN : (half + 1) * MAIN].T.astype(BF16)
            last = jnp.sum(jnp.where(keep, tail, 0.0), axis=0, keepdims=True)
            ref[MAIN:] = jnp.where(row == 0, jnp.broadcast_to(last, (16, GROUP)), 0.0).astype(BF16)


def attn_backward(q, kv, kv_other, dout, out, e, ex, il):
    width = q.shape[1]
    groups = width // GROUP

    def near(offset):
        return pl.BlockSpec((PAD, GROUP), lambda g: (0, g + offset))

    def far(offset):
        return pl.BlockSpec((PAD, GROUP), lambda g: (0, (g + groups // 2) % groups + offset))

    small = pl.BlockSpec((1, PAD, 16), lambda g: (g, 0, 0))
    heads = width // HD
    block = jax.ShapeDtypeStruct((PAD, width), BF16)
    far_out = pl.BlockSpec((PAD, GROUP), lambda g: (0, (g + groups // 2) % groups))
    q, kv, kv_other, out, e, ex, il = (_far(value) for value in (q, kv, kv_other, out, e, ex, il))
    return pl.pallas_call(
        _attn_bwd_kernel,
        grid=(groups,),
        in_specs=[
            near(0), near(0), near(groups), far(0), far(groups), near(0), near(0),
            pl.BlockSpec((HEADS_IN_GROUP, PAD, 2 * MAIN), lambda g: (g, 0, 0)), small, small,
        ],
        out_specs=[near(0), near(0), far_out, near(0), far_out],
        out_shape=[block] * 5,
        scratch_shapes=[
            pltpu.VMEM((2 * MAIN, GROUP), BF16),
            pltpu.VMEM((2 * MAIN, GROUP), BF16),
            pltpu.VMEM((GROUP, 2 * MAIN), F32),
            pltpu.VMEM((GROUP, 2 * MAIN), F32),
        ],
        compiler_params=pltpu.CompilerParams(vmem_limit_bytes=23 * MIB),
        cost_estimate=cost(23),
        name="attn_backward",
    )(q, kv, kv, kv_other, kv_other, dout, out, e, ex, il)


EPSILON = 1e-05
TILE = 512
SUB = 256


def _row(ref, layer):
    return ref[layer : layer + 1, :].astype(F32)


def _fill_turned(coords_ref, order, pieces, x_ref, xt_s, column_s, theirs=False):
    features = xt_s.shape[0]
    rows = features // pieces
    span = max(rows, 128)
    me = coords_ref[0]
    for start in range(0, features, span):
        turned = x_ref[:MAIN, start : start + span].T
        last = x_ref[MAIN:, start : start + span].T.astype(F32)[:, 0:1]
        for part in range(span // rows):
            relative = jnp.bitwise_xor(me, start // rows + part)
            place = jnp.int32(0)
            for bit in order:
                shift = jnp.bitwise_xor(coords_ref[1], bit ^ int(theirs)) if bit < 2 else bit
                place = place * 2 + (jnp.right_shift(relative, shift) & 1)
            at = pl.ds(pl.multiple_of(place * rows, rows), rows)
            xt_s[at, :] = turned[part * rows : (part + 1) * rows]
            column_s[at, :] = jnp.broadcast_to(last[part * rows : (part + 1) * rows], (rows, 128))


def _outer(xt_s, column_s, dy, out_ref):
    width = dy.shape[1]
    last_row = dy[MAIN:].astype(F32)[0:1]
    step = xt_s.shape[0] // 2
    for start in range(0, xt_s.shape[0], step):
        at = slice(start, start + step)
        column = jnp.concatenate([column_s[at, :]] * (width // 128), axis=1)
        total = _dot(xt_s[at, :], dy[:MAIN], ((1,), (0,))) + column * last_row
        out_ref[at, :] = total.astype(BF16)


def _moments(values):
    average = jnp.mean(values, axis=-1, keepdims=True)
    centred = values - average
    inverse = lax.rsqrt(jnp.mean(centred * centred, axis=-1, keepdims=True) + EPSILON)
    return centred * inverse, inverse


def _norm_back(normed, inverse, gain, grad):
    scaled = grad * gain
    first = jnp.mean(scaled, axis=-1, keepdims=True)
    second = jnp.mean(scaled * normed, axis=-1, keepdims=True)
    return (scaled - first - normed * second) * inverse


def _gelu_parts(up):
    square = up * up
    bell = jnp.exp(-0.5 * square)
    size = jnp.abs(up)
    t = 1.0 / (1.0 + (0.375 * 0.5**0.5) * size)
    terms = (
        0.21133947372436523, 0.21568892896175385, 0.16666550934314728, 0.2830598056316376,
        -0.1295955926179886, 0.3879369795322418, -0.1350957304239273,
    )
    value = jnp.full_like(t, 0.5 * terms[-1])
    for term in terms[-2::-1]:
        value = value * t + 0.5 * term
    tail = value * t * bell
    cumulative = jnp.where(up < 0.0, tail, 1.0 - tail)
    return up * cumulative, cumulative + up * (bell * 0.3989422804014327)


def _entry_kernel(
    layer, coords_ref, xa_ref, xb_ref, wa_ref, wb_ref, bias_ref, gain_ref, shift_ref, qa_ref, qb_ref,
    hidden_ref, normed_ref, q_ref, kv_ref, normed_s,
):
    step = pl.program_id(0)

    @pl.when(step == 0)
    def _():
        first = coords_ref[1] == 0
        xa, xb = xa_ref[...], xb_ref[...]
        hidden = (
            _dot(jnp.where(first, xa, xb), wa_ref[...], ((1,), (0,)))
            + _dot(jnp.where(first, xb, xa), wb_ref[...], ((1,), (0,)))
            + _row(bias_ref, layer)
        )
        hidden_ref[...] = hidden
        normed, _unused = _moments(hidden)
        low = (normed * _row(gain_ref, layer) + _row(shift_ref, layer)).astype(BF16)
        normed_s[...] = low
        normed_ref[...] = low

    @pl.when(jnp.logical_and(step >= 1, step <= 2))
    def _():
        half = qa_ref.shape[1]
        kv_ref[:, :half] = _dot(normed_s[...], qa_ref[...], ((1,), (0,))).astype(BF16)
        kv_ref[:, half:] = _dot(normed_s[...], qb_ref[...], ((1,), (0,))).astype(BF16)

    @pl.when(step == 3)
    def _():
        half = qa_ref.shape[1]
        q_ref[:, :half] = _dot(normed_s[...], qa_ref[...], ((1,), (0,))).astype(BF16)
        q_ref[:, half:] = _dot(normed_s[...], qb_ref[...], ((1,), (0,))).astype(BF16)


def entry_forward(layer, coords, residual, skip_rows, wa, wb, bias, gain, shift, qa, qb):
    model = residual.shape[1]
    half = qa.shape[3]

    def part(step):
        return jnp.where(step == 3, 0, jnp.maximum(step, 1))

    once = pl.Buffered(1)
    rows = pl.BlockSpec((PAD, model), lambda j, c: (0, 0), pipeline_mode=once)
    square = pl.BlockSpec((None, None, model, model), lambda j, c: (layer, 0, 0, 0), pipeline_mode=once)
    vector = pl.BlockSpec(bias.shape, lambda j, c: (0, 0))
    third = pl.BlockSpec((None, None, model, half), lambda j, c: (layer, part(j), 0, 0))
    return pl.pallas_call(
        functools.partial(_entry_kernel, layer),
        grid_spec=pltpu.PrefetchScalarGridSpec(
            num_scalar_prefetch=1,
            grid=(4,),
            in_specs=[rows, rows, square, square, vector, vector, vector, third, third],
            out_specs=[
                rows,
                rows,
                rows,
                pl.BlockSpec((PAD, 2 * half), lambda j, c: (0, jnp.clip(j - 1, 0, 1))),
            ],
            scratch_shapes=[pltpu.VMEM((PAD, model), BF16)],
        ),
        out_shape=[
            pltpu.HBM((PAD, model), F32),
            pltpu.HBM((PAD, model), BF16),
            pltpu.HBM((PAD, 2 * half), BF16),
            pltpu.HBM((PAD, 4 * half), BF16),
        ],
        compiler_params=pltpu.CompilerParams(vmem_limit_bytes=22 * MIB),
        cost_estimate=cost(14),
        name="entry_forward",
    )(coords, residual, skip_rows, wa, wb, bias, gain, shift, qa, qb)


def _mlp_kernel(names, plan, coords_ref, *refs):
    layer, first, last, forward, backward, sets, pieces, order = plan
    ref = types.SimpleNamespace(**dict(zip(names, refs, strict=True)))
    step = pl.program_id(0)
    steps_per_set = pl.num_programs(0) // len(sets)

    @pl.when(step == 0)
    def _():
        if first and forward:
            half = ref.proj_own.shape[1]
            middle = (
                ref.hidden[...]
                + _dot(ref.attended[:, :half], ref.proj_own[...], ((1,), (1,)))
                + _dot(ref.attended[:, half:], ref.proj_peer[...], ((1,), (1,)))
                + _row(ref.proj_bias, layer)
            )
            ref.middle_out[...] = middle
            normed, _unused = _moments(middle)
            low = (normed * _row(ref.gain, layer) + _row(ref.shift, layer)).astype(BF16)
            ref.normed_out[...] = low
            ref.normed_s[...] = low
            ref.acc_s[...] = middle + _row(ref.down_bias, layer)
        else:
            ref.normed_s[...] = ref.normed[...]
            if forward:
                ref.acc_s[...] = ref.acc[...]
        if backward:
            assert len(sets) == 1
            theirs = sets[0] == "peer"
            ref.grad_s[...] = ref.grad[...].astype(BF16)
            if first:
                ref.dn_s[...] = jnp.zeros_like(ref.dn_s)
            else:
                ref.dn_s[...] = ref.dn[...]
            _fill_turned(coords_ref, order, pieces, ref.grad_s, ref.grad_t, ref.grad_c, theirs)
            _fill_turned(coords_ref, order, pieces, ref.normed_s, ref.normed_t, ref.normed_c, theirs)

    for number, name in enumerate(sets):

        def tile(name=name):
            up_w, down_w = getattr(ref, "up_" + name), getattr(ref, "down_" + name)
            spans = [slice(at, at + SUB) for at in range(0, TILE, SUB)]
            active, slopes = [], []
            if forward:
                bias = _row(getattr(ref, "up_bias_" + name), layer)
                for span in spans:
                    up = _dot(ref.normed_s[...], up_w[:, span], ((1,), (0,))) + bias[:, span]
                    value, slope = _gelu_parts(up)
                    active.append(value.astype(BF16))
                    slopes.append(slope if backward else slope.astype(BF16))
                ref.acc_s[...] += sum(
                    _dot(value, down_w[:, span], ((1,), (1,))) for value, span in zip(active, spans)
                )
                if not backward:
                    for value, slope, span in zip(active, slopes, spans):
                        getattr(ref, "active_" + name)[:, span] = value
                        getattr(ref, "slope_" + name)[:, span] = slope
            else:
                for span in spans:
                    active.append(getattr(ref, "active_" + name)[:, span])
                    slopes.append(getattr(ref, "slope_" + name)[:, span].astype(F32))
            if backward:
                if name == "own":
                    down_out, up_out = ref.grads_own.at[0], ref.grads_own.at[1]
                else:
                    down_out, up_out = ref.down_grad, ref.up_grad
                units = []
                for slope, span in zip(slopes, spans):
                    du = _dot(ref.grad_s[...], down_w[:, span], ((1,), (0,))) * slope
                    getattr(ref, "bias_grad_" + name)[:, span] = jnp.sum(du, axis=0, keepdims=True)
                    units.append(du.astype(BF16))
                ref.dn_s[...] += sum(_dot(du, up_w[:, span], ((1,), (1,))) for du, span in zip(units, spans))
                for value, du, span in zip(active, units, spans):
                    _outer(ref.grad_t, ref.grad_c, value, down_out.at[:, span])
                    _outer(ref.normed_t, ref.normed_c, du, up_out.at[:, span])

        if len(sets) == 1:
            tile()
        else:
            pl.when(step // steps_per_set == number)(tile)

    @pl.when(step == pl.num_programs(0) - 1)
    def _():
        if not last:
            if forward:
                ref.acc_out[...] = ref.acc_s[...]
            if backward:
                ref.dn_out[...] = ref.dn_s[...]
            return
        if forward:
            ref.result[...] = ref.acc_s[...].astype(BF16)
        if backward:
            gradient = ref.grad[...].astype(F32)
            dn = ref.dn_s[...]
            normed, inverse = _moments(ref.middle[...])
            sums = ref.sums
            sums[0:1, :] = jnp.sum(gradient, axis=0, keepdims=True)
            sums[1:2, :] = jnp.sum(dn * normed, axis=0, keepdims=True)
            sums[2:3, :] = jnp.sum(dn, axis=0, keepdims=True)
            dmid = gradient + _norm_back(normed, inverse, _row(ref.gain, layer), dn)
            sums[3:4, :] = jnp.sum(dmid, axis=0, keepdims=True)
            sums[4:8, :] = jnp.zeros_like(sums[4:8, :])
            ref.dmid[...] = dmid
            low = dmid.astype(BF16)
            half = ref.proj_own.shape[1]
            ref.dattn[:, :half] = _dot(low, ref.proj_own[...], ((1,), (0,))).astype(BF16)
            ref.dattn[:, half:] = _dot(low, ref.proj_peer[...], ((1,), (0,))).astype(BF16)


def mlp(layer, first, last, forward, backward, sets, pieces, order, values):
    _unused, model, units = values["up_" + sets[0]].shape
    steps = units // TILE
    plan = (layer, first, last, forward, backward, sets, pieces, order)
    names, in_specs, operands = [], [], []
    once = pl.Buffered(1)
    rows = pl.BlockSpec((PAD, model), lambda j, c: (0, 0), pipeline_mode=once)
    vector = pl.BlockSpec(values["gain"].shape, lambda j, c: (0, 0), pipeline_mode=once)

    def take(**specs):
        for name, spec in specs.items():
            names.append(name)
            in_specs.append(spec)
            operands.append(values[name])

    def moving(number, shape):
        def index(j, c):
            tile = (0, jnp.clip(j - number * steps, 0, steps - 1))
            return tile if len(shape) == 2 else (layer, *tile)

        return pl.BlockSpec(shape, index)

    half = values["proj_own"].shape[2]
    proj = pl.BlockSpec((None, model, half), lambda j, c: (layer, 0, 0), pipeline_mode=once)
    if first and forward:
        take(hidden=rows, attended=rows, proj_own=proj, proj_peer=proj, proj_bias=vector, gain=vector, shift=vector,
             down_bias=vector)
    else:
        take(normed=rows)
        if forward:
            take(acc=rows)
    if backward:
        take(grad=rows)
        if not first:
            take(dn=rows)
        if last:
            take(middle=rows, proj_own=proj, proj_peer=proj, gain=vector)
    for number, name in enumerate(sets):
        take(**{"up_" + name: moving(number, (None, model, TILE)), "down_" + name: moving(number, (None, model, TILE))})
        if forward:
            take(**{"up_bias_" + name: moving(number, (2, TILE))})
        else:
            take(**{"active_" + name: moving(number, (PAD, TILE)), "slope_" + name: moving(number, (PAD, TILE))})
    out_names, out_specs, out_shape = [], [], []

    def give(spec, shape, kind, *given, make=jax.ShapeDtypeStruct):
        for name in given:
            out_names.append(name)
            out_specs.append(spec)
            out_shape.append(make(shape, kind))

    full = (PAD, model)
    if first and forward:
        give(rows, full, F32, "middle_out", make=pltpu.HBM)
        give(rows, full, BF16, "normed_out", make=pltpu.HBM)
    if not last:
        if forward:
            give(rows, full, F32, "acc_out")
        if backward:
            give(rows, full, F32, "dn_out")
    else:
        if forward:
            give(rows, full, BF16, "result")
        if backward:
            give(pl.BlockSpec((8, model), lambda j, c: (0, 0)), (8, model), F32, "sums")
            give(rows, full, F32, "dmid")
            give(rows, full, BF16, "dattn")
    for number, name in enumerate(sets):
        if forward and not backward:
            give(moving(number, (PAD, TILE)), (PAD, units), BF16, "active_" + name, "slope_" + name, make=pltpu.HBM)
        if backward:
            if name == "own":
                stacked = pl.BlockSpec((2, model, TILE), lambda j, c: (0, 0, j))
                give(stacked, (2, model, units), BF16, "grads_own", make=pltpu.HBM)
            else:
                give(moving(number, (model, TILE)), (model, units), BF16, "down_grad", "up_grad")
            give(moving(number, (1, TILE)), (1, units), F32, "bias_grad_" + name)
    scratch = dict(normed_s=pltpu.VMEM(full, BF16))
    if forward:
        scratch.update(acc_s=pltpu.VMEM(full, F32))
    if backward:
        scratch.update(
            grad_s=pltpu.VMEM(full, BF16),
            dn_s=pltpu.VMEM(full, F32),
            grad_t=pltpu.VMEM((model, MAIN), BF16),
            grad_c=pltpu.VMEM((model, 128), F32),
            normed_t=pltpu.VMEM((model, MAIN), BF16),
            normed_c=pltpu.VMEM((model, 128), F32),
        )
    results = pl.pallas_call(
        functools.partial(_mlp_kernel, (*names, *out_names, *scratch), plan),
        grid_spec=pltpu.PrefetchScalarGridSpec(
            num_scalar_prefetch=1,
            grid=(steps * len(sets),),
            in_specs=in_specs,
            out_specs=out_specs,
            scratch_shapes=list(scratch.values()),
        ),
        out_shape=out_shape,
        compiler_params=pltpu.CompilerParams(vmem_limit_bytes=(30 if not backward else 44 if forward else 38 if last else 27) * MIB),
        cost_estimate=cost(5 * steps * len(sets) * ((0.7 if forward else 0) + (0.9 if backward else 0))),
        name="mlp_" + ("f" if forward else "") + ("b" if backward else "") + "_" + "_".join(sets),
    )(values["coords"], *operands)
    return dict(zip(out_names, results, strict=True))


def _head_grad_kernel(
    pieces, order, coords_ref, dq_ref, dk_ref, dk_got_ref, dv_ref, dv_got_ref, dmid_ref, normed_ref, attended_ref,
    own_ref, peer_ref, dkv_ref, low_s, xt_s, column_s, yt_s, column_y,
):
    step = pl.program_id(0)
    half = own_ref.shape[1]

    def turn(x_ref):
        _fill_turned(coords_ref, order, pieces, x_ref, xt_s, column_s, False)
        _fill_turned(coords_ref, order, pieces, x_ref, yt_s, column_y, True)

    def outer(total):
        _outer(xt_s, column_s, total[:, :half], own_ref)
        _outer(yt_s, column_y, total[:, half:], peer_ref)

    @pl.when(step == 0)
    def _():
        turn(normed_ref)
        outer(dq_ref[...])

    for number, (mine, got) in enumerate(((dk_ref, dk_got_ref), (dv_ref, dv_got_ref))):

        @pl.when(step == 1 + number)
        def _(number=number, mine=mine, got=got):
            total = (mine[...].astype(F32) + got[...].astype(F32)).astype(BF16)
            dkv_ref[:, number * 2 * half : (number + 1) * 2 * half] = total
            outer(total)

    @pl.when(step == 3)
    def _():
        low_s[...] = dmid_ref[...].astype(BF16)
        turn(low_s)
        outer(attended_ref[...])


def head_gradients(pieces, order, coords, dq, dk, dk_got, dv, dv_got, dmid, normed, attended):
    model = dq.shape[1]
    half = model // 2
    rows = pl.BlockSpec((PAD, model), lambda j, c: (0, 0), pipeline_mode=pl.Buffered(1))
    grads = pl.BlockSpec((model, half), lambda j, c: (0, j))
    weight = pltpu.HBM((model, 4 * half), BF16)
    return pl.pallas_call(
        functools.partial(_head_grad_kernel, pieces, order),
        grid_spec=pltpu.PrefetchScalarGridSpec(
            num_scalar_prefetch=1,
            grid=(4,),
            in_specs=[rows] * 8,
            out_specs=[grads, grads, pl.BlockSpec((PAD, 2 * model), lambda j, c: (0, 0))],
            scratch_shapes=[
                pltpu.VMEM((PAD, model), BF16),
                pltpu.VMEM((model, MAIN), BF16),
                pltpu.VMEM((model, 128), F32),
                pltpu.VMEM((model, MAIN), BF16),
                pltpu.VMEM((model, 128), F32),
            ],
        ),
        out_shape=[weight, weight, jax.ShapeDtypeStruct((PAD, 2 * model), BF16)],
        compiler_params=pltpu.CompilerParams(vmem_limit_bytes=25 * MIB),
        cost_estimate=cost(13),
        name="head_gradients",
    )(coords, dq, dk, dk_got, dv, dv_got, dmid, normed, attended)


def _entry_back_kernel(
    layer, pieces, order, coords_ref, dq_ref, dkv_ref, dmid_ref, hidden_ref, xa_ref, xb_ref, gain_ref,
    qa_ref, qb_ref, wa_ref, wb_ref, own_ref, peer_ref, back_ref, skip_back_ref, sums_ref,
    da_s, low_s, xt_s, column_s, yt_s, column_y,
):
    step = pl.program_id(0)
    half = qa_ref.shape[1]

    def columns(ref, at):
        def run():
            total = _dot(ref[:, at : at + half], qa_ref[...], ((1,), (1,)))
            total = total + _dot(ref[:, at + half : at + 2 * half], qb_ref[...], ((1,), (1,)))
            da_s[...] = total if ref is dq_ref else da_s[...] + total

        return run

    pl.when(step == 0)(columns(dq_ref, 0))
    pl.when(step == 1)(columns(dkv_ref, 0))
    pl.when(step == 2)(columns(dkv_ref, 2 * half))

    @pl.when(step == 3)
    def _():
        da = da_s[...]
        normed, inverse = _moments(hidden_ref[...])
        sums_ref[0:1, :] = jnp.sum(da * normed, axis=0, keepdims=True)
        sums_ref[1:2, :] = jnp.sum(da, axis=0, keepdims=True)
        dhid = dmid_ref[...] + _norm_back(normed, inverse, _row(gain_ref, layer), da)
        sums_ref[2:3, :] = jnp.sum(dhid, axis=0, keepdims=True)
        sums_ref[3:8, :] = jnp.zeros_like(sums_ref[3:8, :])
        first = coords_ref[1] == 0
        low_s[...] = jnp.where(first, xa_ref[...], xb_ref[...])
        _fill_turned(coords_ref, order, pieces, low_s, xt_s, column_s, False)
        low_s[...] = jnp.where(first, xb_ref[...], xa_ref[...])
        _fill_turned(coords_ref, order, pieces, low_s, yt_s, column_y, True)
        low_s[...] = dhid.astype(BF16)

    for number in range(2):

        @pl.when(step == 3 + number)
        def _(number=number):
            dy = low_s[:, number * half : (number + 1) * half]
            _outer(xt_s, column_s, dy, own_ref)
            _outer(yt_s, column_y, dy, peer_ref)

    @pl.when(step == 4)
    def _():
        first = coords_ref[1] == 0
        one = _dot(low_s[...], wa_ref[...], ((1,), (1,)))
        two = _dot(low_s[...], wb_ref[...], ((1,), (1,)))
        back_ref[...] = jnp.where(first, one, two).astype(back_ref.dtype)
        skip_back_ref[...] = jnp.where(first, two, one).astype(BF16)


def entry_backward(layer, pieces, order, coords, dq, dkv, dmid, hidden, xa, xb, gain, qa, qb, wa, wb):
    model = xa.shape[1]
    half = qa.shape[3]
    once = pl.Buffered(1)
    rows = pl.BlockSpec((PAD, model), lambda j, c: (0, 0), pipeline_mode=once)
    pair = pl.BlockSpec((PAD, 2 * model), lambda j, c: (0, 0), pipeline_mode=once)
    linear = pl.BlockSpec((None, None, model, model), lambda j, c: (layer, 0, 0, 0), pipeline_mode=once)
    vector = pl.BlockSpec(gain.shape, lambda j, c: (0, 0))
    third = pl.BlockSpec((None, None, model, half), lambda j, c: (layer, jnp.minimum(j, 2), 0, 0))
    grads = pl.BlockSpec((model, half), lambda j, c: (0, jnp.maximum(j, 3) - 3))
    weight = pltpu.HBM((model, 2 * half), BF16)
    return pl.pallas_call(
        functools.partial(_entry_back_kernel, layer, pieces, order),
        grid_spec=pltpu.PrefetchScalarGridSpec(
            num_scalar_prefetch=1,
            grid=(5,),
            in_specs=[rows, pair, rows, rows, rows, rows, vector, third, third, linear, linear],
            out_specs=[grads, grads, rows, rows, pl.BlockSpec((8, model), lambda j, c: (0, 0))],
            scratch_shapes=[
                pltpu.VMEM((PAD, model), F32),
                pltpu.VMEM((PAD, model), BF16),
                pltpu.VMEM((model, MAIN), BF16),
                pltpu.VMEM((model, 128), F32),
                pltpu.VMEM((model, MAIN), BF16),
                pltpu.VMEM((model, 128), F32),
            ],
        ),
        out_shape=[
            weight,
            weight,
            jax.ShapeDtypeStruct((PAD, model), BF16 if layer == 0 else F32),
            jax.ShapeDtypeStruct((PAD, model), BF16),
            jax.ShapeDtypeStruct((8, model), F32),
        ],
        compiler_params=pltpu.CompilerParams(vmem_limit_bytes=40 * MIB),
        cost_estimate=cost(20),
        name="entry_backward",
    )(coords, dq, dkv, dmid, hidden, xa, xb, gain, qa, qb, wa, wb)


def _gather_kernel(count, core_ref, *refs):
    first = core_ref[0] == 0
    out_ref = refs[-1]
    for layer in range(count):
        mine, theirs = refs[2 * layer][...], refs[2 * layer + 1][...]
        low = jnp.where(first, mine, theirs)
        high = jnp.where(first, theirs, mine)
        for start, part in ((0, low[:MAIN]), (MAIN, high[:MAIN]), (2 * MAIN, low[MAIN : MAIN + 1]), (2 * MAIN + 1, high[MAIN : MAIN + 1])):
            at = slice(start, start + part.shape[0])
            if count == 1:
                out_ref[at, :] = part
            else:
                out_ref[at, layer, :] = part


def gather_rows(core, *pairs):
    width = pairs[0][0].shape[1]
    count = len(pairs)
    shape = (2 * MAIN + 2, width) if count == 1 else (2 * MAIN + 2, count, width)
    flat = [value for pair in pairs for value in pair]
    return pl.pallas_call(
        functools.partial(_gather_kernel, count),
        in_specs=[pl.BlockSpec(memory_space=pltpu.SMEM)] + [pl.BlockSpec(memory_space=pltpu.VMEM)] * len(flat),
        out_specs=pl.BlockSpec(memory_space=pltpu.VMEM),
        out_shape=jax.ShapeDtypeStruct(shape, BF16),
        compiler_params=pltpu.CompilerParams(vmem_limit_bytes=16 * MIB),
        cost_estimate=cost(3),
        name="gather_rows",
    )(jnp.reshape(core, (1,)).astype(jnp.int32), *flat)


def _pack_kernel(counts, lead, *refs):
    out_ref = refs[-1]
    for which in range(lead):
        value, at = None, 0
        for count in counts:
            term = (refs[at][which] if lead == 2 else refs[at][...]) if count == 1 else refs[at + which][...]
            value = term.astype(F32) if value is None else value + term.astype(F32)
            at += count
        if lead == 2:
            out_ref[which] = value.astype(BF16)
        else:
            out_ref[...] = value.astype(BF16)


def pack(parts, start, stop):
    block = math.gcd(math.gcd(start, stop), 128)
    columns = parts[0][0][0].shape[-1]
    lead = 2 if parts[0][0][0].ndim == 3 else 1
    in_specs, operands = [], []
    for arrays, at in parts:
        first = (at + start) // block
        for array in arrays:
            if array.ndim == 3:
                in_specs.append(pl.BlockSpec((2, block, columns), lambda j, first=first: (0, first + j, 0)))
            else:
                in_specs.append(pl.BlockSpec((block, columns), lambda j, first=first: (first + j, 0)))
            operands.append(_far(array))
    if lead == 2:
        out_spec = pl.BlockSpec((2, block, columns), lambda j: (0, j, 0))
        out_shape = jax.ShapeDtypeStruct((2, stop - start, columns), BF16)
    else:
        out_spec = pl.BlockSpec((block, columns), lambda j: (j, 0))
        out_shape = jax.ShapeDtypeStruct((stop - start, columns), BF16)
    return pl.pallas_call(
        functools.partial(_pack_kernel, tuple(len(arrays) for arrays, _ in parts), lead),
        grid=((stop - start) // block,),
        in_specs=in_specs,
        out_specs=out_spec,
        out_shape=out_shape,
        compiler_params=pltpu.CompilerParams(vmem_limit_bytes=12 * MIB),
        cost_estimate=cost(3 * (stop - start) * columns * lead / 2**20),
        name="pack",
    )(*operands)


def swap_cores(value):
    return lax.ppermute(value, "tensor", [(0, 1), (1, 0)])


def swap_bits(value, bits, size, crossed):
    cores = 2
    pairs = []
    for index in range(size):
        for core in range(cores):
            other = index
            for bit in bits:
                other = other ^ (1 << ((bit ^ core) if crossed and bit < 2 else bit))
            pairs.append((index * cores + core, other * cores + core))
    return lax.ppermute(value, ("dp", "tensor"), pairs)


def after(value, *others):
    return lax.optimization_barrier((value, others))[0]


def total(parts):
    result = parts[0].astype(F32)
    for part in parts[1:]:
        result = result + part.astype(F32)
    return result


class Reduction:
    def __init__(self, parts, order, size, axis=0, crossed=True):
        self.parts = [(part if isinstance(part, tuple) else (part,), 0) for part in parts]
        self.length, self.order, self.size = parts[0].shape[axis], list(order), size
        self.axis, self.crossed = axis, crossed

    def span(self, start, stop):
        values = []
        for arrays, at in self.parts:
            if len(arrays) == 1:
                values.append(lax.slice_in_dim(arrays[0], at + start, at + stop, axis=self.axis))
            else:
                values.append(jnp.stack([array[at + start : at + stop] for array in arrays]))
        return total(values)

    def piece(self, start, stop):
        if self.parts[0][0][0].dtype == BF16:
            return pack(self.parts, start, stop)
        return self.span(start, stop)

    def send(self, gate, count=1):
        bits, self.order = self.order[:count], self.order[count:]
        held = lax.optimization_barrier(([arrays for arrays, _ in self.parts], gate))[0]
        self.parts = [(arrays, at) for arrays, (_, at) in zip(held, self.parts)]
        self.length >>= len(bits)
        sent, got = [], []
        for block in range(1, 1 << len(bits)):
            start = block * self.length
            sent.append(self.piece(start, start + self.length))
            across = [bit for place, bit in enumerate(reversed(bits)) if (block >> place) & 1]
            got.append(swap_bits(sent[-1], across, self.size, self.crossed))
        self.parts += [((value,), 0) for value in got]
        return sent, got

    def result(self, gate):
        held = lax.optimization_barrier(([arrays for arrays, _ in self.parts], gate))[0]
        self.parts = [(arrays, at) for arrays, (_, at) in zip(held, self.parts)]
        return self.span(0, self.length)


def arrange(value, order, size):
    bits = size.bit_length() - 1
    index = lax.axis_index("dp")
    view = value.reshape((2,) * bits + value.shape[1:])
    for bit in range(bits):
        axis = bits - 1 - bit
        view = jnp.where((index >> bit) & 1 == 1, jnp.flip(view, axis), view)
    axes = [bits - 1 - bit for bit in order] + list(range(bits, view.ndim))
    return view.transpose(axes).reshape(value.shape)


def localize(value, core):
    main = lax.dynamic_slice_in_dim(value, core * MAIN, MAIN, 0)
    extra = lax.dynamic_slice_in_dim(value, 2 * MAIN + core, 1, 0)
    blank = jnp.zeros((PAD - MAIN - 1,) + value.shape[1:], value.dtype)
    return jnp.concatenate([main, extra, blank], axis=0)


def globalize(core, *mine):
    return gather_rows(core, *((value, swap_cores(value)) for value in mine))


def sum_vectors(shared, up_own, up_peer, size):
    count, model = shared.shape
    layers, units = up_own.shape
    order = tuple(range(size.bit_length() - 1))

    def blocks(offsets):
        first = shared.reshape(count, size, model // size).transpose(1, 0, 2)
        second = offsets.reshape(layers, size, units // model, model // size)
        second = second.transpose(1, 0, 2, 3).reshape(size, -1, model // size)
        return arrange(jnp.concatenate([first, second], axis=1), order, size)

    return Reduction([blocks(up_own), swap_cores(blocks(up_peer))], order, size, crossed=False)


def body(
    inputs, skips, cotangent, skip_weight, skip_bias, attn_norm_gain, attn_norm_bias, qkv_weight,
    proj_weight, proj_bias, ffn_norm_gain, ffn_norm_bias, up_weight, up_bias, down_weight, down_bias,
):
    core = lax.axis_index("tensor")
    size = lax.axis_size("dp")
    bits = size.bit_length() - 1
    assert size == 1 << bits and bits >= 2
    order = tuple(range(bits))
    order_mlp = order
    layers, model = skip_bias.shape
    assert layers == 2
    coords = jnp.stack([lax.axis_index("dp"), core]).astype(jnp.int32)

    qkv_turned = qkv_weight.transpose(0, 2, 1, 3)
    skip_peer, qkv_peer, up_bias_peer = swap_cores(skip_weight), swap_cores(qkv_turned), swap_cores(up_bias)
    weights = dict(
        coords=coords, proj_own=proj_weight, up_own=up_weight, down_own=down_weight, up_bias_own=up_bias,
        up_bias_peer=up_bias_peer, proj_bias=proj_bias, down_bias=down_bias, gain=ffn_norm_gain, shift=ffn_norm_bias,
    )
    skip_parts = localize(skips.transpose(1, 0, 2), core)

    rows0 = localize(inputs, core)
    weights["up_peer"] = swap_cores(after(up_weight, skip_peer, qkv_peer, skip_parts, rows0))

    def enter(layer, residual):
        skip_rows = skip_parts[:, layer]
        hidden, normed, q, kv = entry_forward(
            layer, coords, residual, skip_rows, skip_weight, skip_peer, skip_bias, attn_norm_gain, attn_norm_bias,
            qkv_turned, qkv_peer,
        )
        kv_other = swap_cores(kv)
        if layer == 0:
            kv_other = after(kv_other, weights["up_peer"], up_bias_peer)
        attended, exact, e, ex, il = attn_forward(q, kv, kv_other)
        return dict(xa=residual, xb=skip_rows, hidden=hidden, normed=normed, q=q, kv=kv, kv_other=kv_other,
                    attended=attended, exact=exact, e=e, ex=ex, il=il)

    items, result, flying = {}, {}, []

    def add(name, layer, own, *peer):
        theirs = tuple(swap_cores(value) for value in peer)
        flying.extend(theirs)
        items[name, layer] = Reduction([own, theirs], order, size, own.ndim - 2)

    def settle(gate):
        gate = after(gate, *flying)
        flying.clear()
        return gate

    def sends(gate, *keys, count=1):
        made = []
        for key in keys:
            item = items[key]
            if item.order:
                sent, got = item.send(gate, count)
                made.extend(sent)
                flying.extend(got)
            elif key not in result:
                result[key] = item.result(gate)
                made.append(result[key])
        return after(gate, *made) if made else gate

    def back(layer, kept, mid, dattn, *keys):
        dq, dk, dk_other, dv, dv_other = attn_backward(
            kept["q"], kept["kv"], kept["kv_other"], dattn, kept["exact"], kept["e"], kept["ex"], kept["il"]
        )
        own, peer, dkv = head_gradients(
            size, order, coords, dq, dk, swap_cores(dk_other), dv, swap_cores(dv_other), mid["dmid"], kept["normed"],
            kept["attended"],
        )
        dkv = settle(dkv)
        add("head", layer, own, after(peer, dkv))
        dkv = sends(dkv, *keys)
        own, peer, gradient, skip_grad, sums = entry_backward(
            layer, size, order, coords, dq, dkv, mid["dmid"], kept["hidden"], kept["xa"], kept["xb"], attn_norm_gain,
            qkv_turned, qkv_peer, skip_weight, skip_peer,
        )
        gradient = settle(gradient)
        add("skip", layer, own, after(peer, gradient))
        return gradient, skip_grad, sums

    kept = [None] * layers
    kept[0] = enter(0, rows0)
    late = after((proj_weight, down_weight), kept[0]["kv_other"])
    weights["proj_peer"], weights["down_peer"] = (swap_cores(item) for item in late)
    mid0 = mlp(0, True, True, True, False, ("peer", "own"), size, order_mlp, {**weights, **kept[0]})
    kept[1] = enter(1, mid0["result"])
    values = {**weights, **kept[1], "grad": localize(cotangent, core)}
    one = mlp(1, True, False, True, True, ("peer",), size, order_mlp, values)
    values.update(normed=one["normed_out"], middle=one["middle_out"], acc=one["acc_out"], dn=one["dn_out"])
    theirs = tuple(swap_cores(one[name]) for name in ("down_grad", "up_grad"))
    flying.extend(theirs)
    two = mlp(1, False, True, True, True, ("own",), size, order, values)
    items["mlp", 1] = Reduction([two["grads_own"], theirs], order, size, 1)
    dattn = sends(settle(two["dattn"]), ("mlp", 1))
    gradient, skip_grad1, sums1 = back(1, kept[1], two, dattn, ("mlp", 1))
    gradient = sends(gradient, ("head", 1), ("mlp", 1))

    values = {**weights, **kept[0], **mid0, "normed": mid0["normed_out"], "middle": mid0["middle_out"], "grad": gradient}
    one0 = mlp(0, True, False, False, True, ("peer",), size, order, values)
    gate = settle(one0["dn_out"])
    peers = [after(one0[name], gate) for name in ("down_grad", "up_grad")]
    theirs = tuple(swap_cores(value) for value in peers)
    flying.extend(theirs)
    values.update(dn=sends(gate, ("skip", 1), ("head", 1), ("mlp", 1)))
    low = mlp(0, False, True, False, True, ("own",), size, order, values)
    items["mlp", 0] = Reduction([low["grads_own"], theirs], order, size, 1)
    dattn = sends(settle(low["dattn"]), ("mlp", 0), ("head", 1), ("mlp", 1), ("skip", 1))
    gradient, skip_grad0, sums0 = back(0, kept[0], low, dattn, ("mlp", 0), ("head", 1), ("skip", 1))
    shared = jnp.concatenate([low["sums"][:4], two["sums"][:4], sums0[:3], sums1[:3]], axis=0)
    items["vectors", 0] = sum_vectors(
        shared,
        jnp.concatenate([low["bias_grad_own"], two["bias_grad_own"]], axis=0),
        jnp.concatenate([one0["bias_grad_peer"], one["bias_grad_peer"]], axis=0),
        size,
    )
    rest = bits - 2
    finish = sends(gradient, ("head", 0), ("mlp", 0), ("skip", 1), ("head", 1))
    others = [swap_cores(after(value, finish)) for value in (gradient, skip_grad0, skip_grad1, two["result"])]
    input_grad = gather_rows(core, (after(gradient, finish), others[0]))
    skip_grad = gather_rows(core, (after(skip_grad0, input_grad), others[1]), (skip_grad1, others[2]))
    output = gather_rows(core, (after(two["result"], skip_grad), others[3]))
    finish = settle(after(finish, output))
    finish = sends(finish, ("head", 0), ("skip", 0), ("mlp", 0), ("skip", 1))
    finish = settle(sends(finish, ("vectors", 0), count=2))
    finish = sends(finish, ("head", 0), count=rest)
    finish = settle(sends(finish, ("skip", 0), ("vectors", 0), ("mlp", 0)))
    finish = sends(finish, ("skip", 0), count=rest)
    finish = settle(sends(finish, ("vectors", 0), ("head", 0)))
    while len(result) < len(items):
        finish = settle(sends(finish, *items))
    count = shared.shape[0]
    vectors = result["vectors", 0][0, :count]
    up_bias_grad = result["vectors", 0][0, count:].reshape(layers, -1)
    skip_grad = skip_grad.transpose(1, 0, 2)
    outer = vectors[:8].reshape(2, 4, -1)
    inner = vectors[8:].reshape(2, 3, -1)

    half = model // 2

    def columns(start, stop):
        return jnp.stack([result["head", layer][:, start:stop] for layer in range(layers)])

    def matrix(which):
        return jnp.stack([result["mlp", layer][which] for layer in range(layers)])

    return (
        output, input_grad, skip_grad, jnp.stack([result["skip", layer] for layer in range(layers)])[:, None],
        inner[:, 2], inner[:, 0], inner[:, 1],
        columns(0, 3 * half).reshape(layers, -1, 3, qkv_weight.shape[3]), columns(3 * half, 4 * half),
        outer[:, 3], outer[:, 1], outer[:, 2],
        matrix(1), up_bias_grad, matrix(0), outer[:, 0],
    )


def solution(mesh):
    return jax.shard_map(
        body,
        mesh=mesh,
        in_specs=(
            P("dp", None), P(None, "dp", None), P("dp", None), P(None, "tensor", None, None), P(), P(),
            P(), P(None, None, None, "tensor"), P(None, None, "tensor"), P(), P(), P(),
            P(None, None, "tensor"), P(None, "tensor"), P(None, None, "tensor"), P(),
        ),
        out_specs=(
            P("dp", None), P("dp", None), P(None, "dp", None), P(None, "tensor", "dp", None),
            P(None, "dp"), P(None, "dp"), P(None, "dp"), P(None, "dp", None, "tensor"),
            P(None, "dp", "tensor"), P(None, "dp"), P(None, "dp"), P(None, "dp"),
            P(None, "dp", "tensor"), P(None, ("tensor", "dp")), P(None, "dp", "tensor"), P(None, "dp"),
        ),
        check_vma=False,
    )
```

```python
import functools
import math
import types

import jax
import jax.numpy as jnp
from jax import lax
from jax.experimental import pallas as pl
from jax.experimental.pallas import tpu as pltpu
from jax.sharding import PartitionSpec as P

F32 = jnp.float32
BF16 = jnp.bfloat16
HD = 64
MAIN = 512
PAD = 528
GROUP = 256
HEADS_IN_GROUP = GROUP // HD
MIB = 1024 * 1024
SCALE = 0.1


def cost(microseconds):
    return pl.CostEstimate(flops=1, bytes_accessed=int(microseconds * SCALE * 3.5e6), transcendentals=0)


def _dot(a, b, dims):
    return lax.dot_general(a, b, (dims, ((), ())), preferred_element_type=F32)


def _extra_rows(mine_ref, other_ref):
    row = lax.broadcasted_iota(jnp.int32, (16, GROUP), 0)
    lane = lax.broadcasted_iota(jnp.int32, (16, GROUP), 1)
    mine = jnp.broadcast_to(mine_ref[MAIN : MAIN + 16, :][0:1].astype(F32), (16, GROUP))
    other = jnp.broadcast_to(other_ref[MAIN : MAIN + 16, :][0:1].astype(F32), (16, GROUP))
    value = jnp.where(row % 2 == 0, mine, other)
    return jnp.where(row // 2 == lane // HD, value, 0.0).astype(BF16)


def _attn_fwd_kernel(q_ref, km_ref, vm_ref, ko_ref, vo_ref, o_ref, of_ref, e_ref, ex_ref, il_ref, k_s, v_s):
    k_s[:MAIN] = km_ref[:MAIN]
    k_s[MAIN:] = ko_ref[:MAIN]
    v_s[:MAIN] = vm_ref[:MAIN]
    v_s[MAIN:] = vo_ref[:MAIN]
    lane = lax.broadcasted_iota(jnp.int32, (PAD, GROUP), 1) // HD
    slot = lax.broadcasted_iota(jnp.int32, (PAD, 16), 1) // 2
    q = q_ref[...] * jnp.asarray(HD**-0.5, BF16)
    kx = _extra_rows(km_ref, ko_ref)
    vx = _extra_rows(vm_ref, vo_ref)
    sx = _dot(q, kx, ((1,), (1,)))
    out = jnp.zeros((PAD, GROUP), F32)
    ex_all = jnp.zeros((PAD, 16), F32)
    il_all = jnp.zeros((PAD, 16), F32)
    for h in range(HEADS_IN_GROUP):
        qh = jnp.where(lane == h, q, jnp.zeros_like(q))
        s = _dot(qh, k_s[...], ((1,), (1,)))
        sxh = jnp.where(slot == h, sx, -jnp.inf)
        top = jnp.maximum(jnp.max(s, axis=1, keepdims=True), jnp.max(sxh, axis=1, keepdims=True))
        e = jnp.exp(s - top)
        exh = jnp.exp(sxh - top)
        total = jnp.sum(e, axis=1, keepdims=True) + jnp.sum(exh, axis=1, keepdims=True)
        inverse = 1.0 / total
        low = e.astype(BF16)
        e_ref[h] = low
        out = out + jnp.where(lane == h, _dot(low, v_s[...], ((1,), (0,))) * inverse, 0.0)
        ex_all = ex_all + exh
        il_all = il_all + jnp.where(slot == h, inverse, 0.0)
    out = out + _dot((ex_all * il_all).astype(BF16), vx, ((1,), (0,)))
    o_ref[...] = out.astype(BF16)
    of_ref[...] = out
    ex_ref[0] = ex_all
    il_ref[0] = il_all


def _far(value):
    return pltpu.with_memory_space_constraint(value, pltpu.HBM)


def attn_forward(q, kv, kv_other):
    width = q.shape[1]
    groups = width // GROUP

    def near(offset):
        return pl.BlockSpec((PAD, GROUP), lambda g: (0, g + offset))

    def far(offset):
        return pl.BlockSpec((PAD, GROUP), lambda g: (0, (g + groups // 2) % groups + offset))

    heads = width // HD
    kv, kv_other = _far(kv), _far(kv_other)
    return pl.pallas_call(
        _attn_fwd_kernel,
        grid=(groups,),
        in_specs=[near(0), near(0), near(groups), far(0), far(groups)],
        out_specs=[
            near(0),
            near(0),
            pl.BlockSpec((HEADS_IN_GROUP, PAD, 2 * MAIN), lambda g: (g, 0, 0)),
            pl.BlockSpec((1, PAD, 16), lambda g: (g, 0, 0)),
            pl.BlockSpec((1, PAD, 16), lambda g: (g, 0, 0)),
        ],
        out_shape=[
            pltpu.HBM((PAD, width), BF16),
            pltpu.HBM((PAD, width), F32),
            pltpu.HBM((heads, PAD, 2 * MAIN), BF16),
            pltpu.HBM((groups, PAD, 16), F32),
            pltpu.HBM((groups, PAD, 16), F32),
        ],
        scratch_shapes=[pltpu.VMEM((2 * MAIN, GROUP), BF16), pltpu.VMEM((2 * MAIN, GROUP), BF16)],
        compiler_params=pltpu.CompilerParams(vmem_limit_bytes=24 * MIB),
        cost_estimate=cost(19),
        name="attn_forward",
    )(q, kv, kv, kv_other, kv_other)


def _attn_bwd_kernel(
    q_ref, km_ref, vm_ref, ko_ref, vo_ref, do_ref, o_ref, e_ref, ex_ref, il_ref,
    dq_ref, dkm_ref, dko_ref, dvm_ref, dvo_ref, k_s, v_s, dk_s, dv_s,
):
    k_s[:MAIN] = km_ref[:MAIN]
    k_s[MAIN:] = ko_ref[:MAIN]
    v_s[:MAIN] = vm_ref[:MAIN]
    v_s[MAIN:] = vo_ref[:MAIN]
    scale = HD**-0.5
    lane = lax.broadcasted_iota(jnp.int32, (PAD, GROUP), 1) // HD
    slot = lax.broadcasted_iota(jnp.int32, (PAD, 16), 1) // 2
    q = q_ref[...] * jnp.asarray(scale, BF16)
    kx = _extra_rows(km_ref, ko_ref)
    vx = _extra_rows(vm_ref, vo_ref)
    il = il_ref[0]
    do = do_ref[...].astype(F32)
    spread = jnp.zeros((PAD, GROUP), F32)
    for h in range(HEADS_IN_GROUP):
        spread = jnp.where(lane == h, il[:, 2 * h : 2 * h + 1], spread)
    dos = (do * spread).astype(BF16)
    product = dos.astype(F32) * o_ref[...]
    inner = jnp.zeros((PAD, 16), F32)
    inners = []
    for h in range(HEADS_IN_GROUP):
        one = jnp.sum(jnp.where(lane == h, product, 0.0), axis=1, keepdims=True)
        inners.append(one)
        inner = jnp.where(slot == h, one, inner)
    dos_t = dos.T
    q_t = q.T
    dq = jnp.zeros((PAD, GROUP), F32)
    for h in range(HEADS_IN_GROUP):
        rows = slice(h * HD, (h + 1) * HD)
        dosh = jnp.where(lane == h, dos, jnp.zeros_like(dos))
        e = e_ref[h]
        dp = _dot(dosh, v_s[...], ((1,), (1,)))
        ds = (e.astype(F32) * (dp - inners[h])).astype(BF16)
        dq = dq + jnp.where(lane == h, _dot(ds, k_s[...], ((1,), (0,))), 0.0)
        dk_s[rows, :] = (
            _dot(q_t[rows, :MAIN], ds[:MAIN], ((1,), (0,)))
            + q_t[rows, MAIN : MAIN + 1].astype(F32) * ds[MAIN : MAIN + 16].astype(F32)[0:1]
        )
        dv_s[rows, :] = (
            _dot(dos_t[rows, :MAIN], e[:MAIN], ((1,), (0,)))
            + dos_t[rows, MAIN : MAIN + 1].astype(F32) * e[MAIN : MAIN + 16].astype(F32)[0:1]
        )
    ex = ex_ref[0]
    dsx = (ex * (_dot(dos, vx, ((1,), (1,))) - inner)).astype(BF16)
    dq = dq + _dot(dsx, kx, ((1,), (0,)))
    dq_ref[...] = (dq * scale).astype(BF16)
    dkx = _dot(dsx, q, ((0,), (0,)))
    dvx = _dot(ex.astype(BF16), dos, ((0,), (0,)))
    row = lax.broadcasted_iota(jnp.int32, (16, GROUP), 0)
    own = row // 2 == lax.broadcasted_iota(jnp.int32, (16, GROUP), 1) // HD
    for half, (dk_ref, dv_ref) in enumerate(((dkm_ref, dvm_ref), (dko_ref, dvo_ref))):
        keep = jnp.logical_and(own, row % 2 == half)
        for ref, grad_s, tail in ((dk_ref, dk_s, dkx), (dv_ref, dv_s, dvx)):
            ref[:MAIN] = grad_s[:, half * MAIN : (half + 1) * MAIN].T.astype(BF16)
            last = jnp.sum(jnp.where(keep, tail, 0.0), axis=0, keepdims=True)
            ref[MAIN:] = jnp.where(row == 0, jnp.broadcast_to(last, (16, GROUP)), 0.0).astype(BF16)


def attn_backward(q, kv, kv_other, dout, out, e, ex, il):
    width = q.shape[1]
    groups = width // GROUP

    def near(offset):
        return pl.BlockSpec((PAD, GROUP), lambda g: (0, g + offset))

    def far(offset):
        return pl.BlockSpec((PAD, GROUP), lambda g: (0, (g + groups // 2) % groups + offset))

    small = pl.BlockSpec((1, PAD, 16), lambda g: (g, 0, 0))
    heads = width // HD
    block = jax.ShapeDtypeStruct((PAD, width), BF16)
    far_out = pl.BlockSpec((PAD, GROUP), lambda g: (0, (g + groups // 2) % groups))
    q, kv, kv_other, out, e, ex, il = (_far(value) for value in (q, kv, kv_other, out, e, ex, il))
    return pl.pallas_call(
        _attn_bwd_kernel,
        grid=(groups,),
        in_specs=[
            near(0), near(0), near(groups), far(0), far(groups), near(0), near(0),
            pl.BlockSpec((HEADS_IN_GROUP, PAD, 2 * MAIN), lambda g: (g, 0, 0)), small, small,
        ],
        out_specs=[near(0), near(0), far_out, near(0), far_out],
        out_shape=[block] * 5,
        scratch_shapes=[
            pltpu.VMEM((2 * MAIN, GROUP), BF16),
            pltpu.VMEM((2 * MAIN, GROUP), BF16),
            pltpu.VMEM((GROUP, 2 * MAIN), F32),
            pltpu.VMEM((GROUP, 2 * MAIN), F32),
        ],
        compiler_params=pltpu.CompilerParams(vmem_limit_bytes=23 * MIB),
        cost_estimate=cost(23),
        name="attn_backward",
    )(q, kv, kv, kv_other, kv_other, dout, out, e, ex, il)


EPSILON = 1e-05
TILE = 512
SUB = 256


def _row(ref, layer):
    return ref[layer : layer + 1, :].astype(F32)


def _fill_turned(coords_ref, order, pieces, x_ref, xt_s, column_s, theirs=False):
    features = xt_s.shape[0]
    rows = features // pieces
    span = max(rows, 128)
    me = coords_ref[0]
    for start in range(0, features, span):
        turned = x_ref[:MAIN, start : start + span].T
        last = x_ref[MAIN:, start : start + span].T.astype(F32)[:, 0:1]
        for part in range(span // rows):
            relative = jnp.bitwise_xor(me, start // rows + part)
            place = jnp.int32(0)
            for bit in order:
                shift = jnp.bitwise_xor(coords_ref[1], bit ^ int(theirs)) if bit < 2 else bit
                place = place * 2 + (jnp.right_shift(relative, shift) & 1)
            at = pl.ds(pl.multiple_of(place * rows, rows), rows)
            xt_s[at, :] = turned[part * rows : (part + 1) * rows]
            column_s[at, :] = jnp.broadcast_to(last[part * rows : (part + 1) * rows], (rows, 128))


def _outer(xt_s, column_s, dy, out_ref):
    width = dy.shape[1]
    last_row = dy[MAIN:].astype(F32)[0:1]
    step = xt_s.shape[0] // 2
    for start in range(0, xt_s.shape[0], step):
        at = slice(start, start + step)
        column = jnp.concatenate([column_s[at, :]] * (width // 128), axis=1)
        total = _dot(xt_s[at, :], dy[:MAIN], ((1,), (0,))) + column * last_row
        out_ref[at, :] = total.astype(BF16)


def _moments(values):
    average = jnp.mean(values, axis=-1, keepdims=True)
    centred = values - average
    inverse = lax.rsqrt(jnp.mean(centred * centred, axis=-1, keepdims=True) + EPSILON)
    return centred * inverse, inverse


def _norm_back(normed, inverse, gain, grad):
    scaled = grad * gain
    first = jnp.mean(scaled, axis=-1, keepdims=True)
    second = jnp.mean(scaled * normed, axis=-1, keepdims=True)
    return (scaled - first - normed * second) * inverse


def _gelu_parts(up):
    square = up * up
    bell = jnp.exp(-0.5 * square)
    size = jnp.abs(up)
    t = 1.0 / (1.0 + (0.375 * 0.5**0.5) * size)
    terms = (
        0.21133947372436523, 0.21568892896175385, 0.16666550934314728, 0.2830598056316376,
        -0.1295955926179886, 0.3879369795322418, -0.1350957304239273,
    )
    value = jnp.full_like(t, 0.5 * terms[-1])
    for term in terms[-2::-1]:
        value = value * t + 0.5 * term
    tail = value * t * bell
    cumulative = jnp.where(up < 0.0, tail, 1.0 - tail)
    return up * cumulative, cumulative + up * (bell * 0.3989422804014327)


def _entry_kernel(
    layer, coords_ref, xa_ref, xb_ref, wa_ref, wb_ref, bias_ref, gain_ref, shift_ref, qa_ref, qb_ref,
    hidden_ref, normed_ref, q_ref, kv_ref, normed_s,
):
    step = pl.program_id(0)

    @pl.when(step == 0)
    def _():
        first = coords_ref[1] == 0
        xa, xb = xa_ref[...], xb_ref[...]
        hidden = (
            _dot(jnp.where(first, xa, xb), wa_ref[...], ((1,), (0,)))
            + _dot(jnp.where(first, xb, xa), wb_ref[...], ((1,), (0,)))
            + _row(bias_ref, layer)
        )
        hidden_ref[...] = hidden
        normed, _unused = _moments(hidden)
        low = (normed * _row(gain_ref, layer) + _row(shift_ref, layer)).astype(BF16)
        normed_s[...] = low
        normed_ref[...] = low

    @pl.when(jnp.logical_and(step >= 1, step <= 2))
    def _():
        half = qa_ref.shape[1]
        kv_ref[:, :half] = _dot(normed_s[...], qa_ref[...], ((1,), (0,))).astype(BF16)
        kv_ref[:, half:] = _dot(normed_s[...], qb_ref[...], ((1,), (0,))).astype(BF16)

    @pl.when(step == 3)
    def _():
        half = qa_ref.shape[1]
        q_ref[:, :half] = _dot(normed_s[...], qa_ref[...], ((1,), (0,))).astype(BF16)
        q_ref[:, half:] = _dot(normed_s[...], qb_ref[...], ((1,), (0,))).astype(BF16)


def entry_forward(layer, coords, residual, skip_rows, wa, wb, bias, gain, shift, qa, qb):
    model = residual.shape[1]
    half = qa.shape[3]

    def part(step):
        return jnp.where(step == 3, 0, jnp.maximum(step, 1))

    once = pl.Buffered(1)
    rows = pl.BlockSpec((PAD, model), lambda j, c: (0, 0), pipeline_mode=once)
    square = pl.BlockSpec((None, None, model, model), lambda j, c: (layer, 0, 0, 0), pipeline_mode=once)
    vector = pl.BlockSpec(bias.shape, lambda j, c: (0, 0))
    third = pl.BlockSpec((None, None, model, half), lambda j, c: (layer, part(j), 0, 0))
    return pl.pallas_call(
        functools.partial(_entry_kernel, layer),
        grid_spec=pltpu.PrefetchScalarGridSpec(
            num_scalar_prefetch=1,
            grid=(4,),
            in_specs=[rows, rows, square, square, vector, vector, vector, third, third],
            out_specs=[
                rows,
                rows,
                rows,
                pl.BlockSpec((PAD, 2 * half), lambda j, c: (0, jnp.clip(j - 1, 0, 1))),
            ],
            scratch_shapes=[pltpu.VMEM((PAD, model), BF16)],
        ),
        out_shape=[
            pltpu.HBM((PAD, model), F32),
            pltpu.HBM((PAD, model), BF16),
            pltpu.HBM((PAD, 2 * half), BF16),
            pltpu.HBM((PAD, 4 * half), BF16),
        ],
        compiler_params=pltpu.CompilerParams(vmem_limit_bytes=22 * MIB),
        cost_estimate=cost(14),
        name="entry_forward",
    )(coords, residual, skip_rows, _far(wa), _far(wb), bias, gain, shift, _far(qa), _far(qb))


def _mlp_kernel(names, plan, coords_ref, *refs):
    layer, first, last, forward, backward, sets, pieces, order = plan
    ref = types.SimpleNamespace(**dict(zip(names, refs, strict=True)))
    step = pl.program_id(0)
    steps_per_set = pl.num_programs(0) // len(sets)

    @pl.when(step == 0)
    def _():
        if first and forward:
            half = ref.proj_own.shape[1]
            middle = (
                ref.hidden[...]
                + _dot(ref.attended[:, :half], ref.proj_own[...], ((1,), (1,)))
                + _dot(ref.attended[:, half:], ref.proj_peer[...], ((1,), (1,)))
                + _row(ref.proj_bias, layer)
            )
            ref.middle_out[...] = middle
            normed, _unused = _moments(middle)
            low = (normed * _row(ref.gain, layer) + _row(ref.shift, layer)).astype(BF16)
            ref.normed_out[...] = low
            ref.normed_s[...] = low
            ref.acc_s[...] = middle + _row(ref.down_bias, layer)
        else:
            ref.normed_s[...] = ref.normed[...]
            if forward:
                ref.acc_s[...] = ref.acc[...]
        if backward:
            assert len(sets) == 1
            theirs = sets[0] == "peer"
            ref.grad_s[...] = ref.grad[...].astype(BF16)
            if first:
                ref.dn_s[...] = jnp.zeros_like(ref.dn_s)
            else:
                ref.dn_s[...] = ref.dn[...]
            _fill_turned(coords_ref, order, pieces, ref.grad_s, ref.grad_t, ref.grad_c, theirs)
            _fill_turned(coords_ref, order, pieces, ref.normed_s, ref.normed_t, ref.normed_c, theirs)

    for number, name in enumerate(sets):

        def tile(name=name):
            up_w, down_w = getattr(ref, "up_" + name), getattr(ref, "down_" + name)
            spans = [slice(at, at + SUB) for at in range(0, TILE, SUB)]
            active, slopes = [], []
            if forward:
                bias = _row(getattr(ref, "up_bias_" + name), layer)
                for span in spans:
                    up = _dot(ref.normed_s[...], up_w[:, span], ((1,), (0,))) + bias[:, span]
                    value, slope = _gelu_parts(up)
                    active.append(value.astype(BF16))
                    slopes.append(slope if backward else slope.astype(BF16))
                ref.acc_s[...] += sum(
                    _dot(value, down_w[:, span], ((1,), (1,))) for value, span in zip(active, spans)
                )
                if not backward:
                    for value, slope, span in zip(active, slopes, spans):
                        getattr(ref, "active_" + name)[:, span] = value
                        getattr(ref, "slope_" + name)[:, span] = slope
            else:
                for span in spans:
                    active.append(getattr(ref, "active_" + name)[:, span])
                    slopes.append(getattr(ref, "slope_" + name)[:, span].astype(F32))
            if backward:
                if name == "own":
                    down_out, up_out = ref.grads_own.at[0], ref.grads_own.at[1]
                else:
                    down_out, up_out = ref.down_grad, ref.up_grad
                units = []
                for slope, span in zip(slopes, spans):
                    du = _dot(ref.grad_s[...], down_w[:, span], ((1,), (0,))) * slope
                    getattr(ref, "bias_grad_" + name)[:, span] = jnp.sum(du, axis=0, keepdims=True)
                    units.append(du.astype(BF16))
                ref.dn_s[...] += sum(_dot(du, up_w[:, span], ((1,), (1,))) for du, span in zip(units, spans))
                for value, du, span in zip(active, units, spans):
                    _outer(ref.grad_t, ref.grad_c, value, down_out.at[:, span])
                    _outer(ref.normed_t, ref.normed_c, du, up_out.at[:, span])

        if len(sets) == 1:
            tile()
        else:
            pl.when(step // steps_per_set == number)(tile)

    @pl.when(step == pl.num_programs(0) - 1)
    def _():
        if not last:
            if forward:
                ref.acc_out[...] = ref.acc_s[...]
            if backward:
                ref.dn_out[...] = ref.dn_s[...]
            return
        if forward:
            ref.result[...] = ref.acc_s[...].astype(BF16)
        if backward:
            gradient = ref.grad[...].astype(F32)
            dn = ref.dn_s[...]
            normed, inverse = _moments(ref.middle[...])
            sums = ref.sums
            sums[0:1, :] = jnp.sum(gradient, axis=0, keepdims=True)
            sums[1:2, :] = jnp.sum(dn * normed, axis=0, keepdims=True)
            sums[2:3, :] = jnp.sum(dn, axis=0, keepdims=True)
            dmid = gradient + _norm_back(normed, inverse, _row(ref.gain, layer), dn)
            sums[3:4, :] = jnp.sum(dmid, axis=0, keepdims=True)
            sums[4:8, :] = jnp.zeros_like(sums[4:8, :])
            ref.dmid[...] = dmid
            low = dmid.astype(BF16)
            half = ref.proj_own.shape[1]
            ref.dattn[:, :half] = _dot(low, ref.proj_own[...], ((1,), (0,))).astype(BF16)
            ref.dattn[:, half:] = _dot(low, ref.proj_peer[...], ((1,), (0,))).astype(BF16)


def mlp(layer, first, last, forward, backward, sets, pieces, order, values):
    _unused, model, units = values["up_" + sets[0]].shape
    steps = units // TILE
    plan = (layer, first, last, forward, backward, sets, pieces, order)
    names, in_specs, operands = [], [], []
    once = pl.Buffered(1)
    rows = pl.BlockSpec((PAD, model), lambda j, c: (0, 0), pipeline_mode=once)
    vector = pl.BlockSpec(values["gain"].shape, lambda j, c: (0, 0), pipeline_mode=once)

    def take(**specs):
        for name, spec in specs.items():
            names.append(name)
            in_specs.append(spec)
            operands.append(values[name])

    def moving(number, shape):
        def index(j, c):
            tile = (0, jnp.clip(j - number * steps, 0, steps - 1))
            return tile if len(shape) == 2 else (layer, *tile)

        return pl.BlockSpec(shape, index)

    half = values["proj_own"].shape[2]
    proj = pl.BlockSpec((None, model, half), lambda j, c: (layer, 0, 0), pipeline_mode=once)
    if first and forward:
        take(hidden=rows, attended=rows, proj_own=proj, proj_peer=proj, proj_bias=vector, gain=vector, shift=vector,
             down_bias=vector)
    else:
        take(normed=rows)
        if forward:
            take(acc=rows)
    if backward:
        take(grad=rows)
        if not first:
            take(dn=rows)
        if last:
            take(middle=rows, proj_own=proj, proj_peer=proj, gain=vector)
    for number, name in enumerate(sets):
        take(**{"up_" + name: moving(number, (None, model, TILE)), "down_" + name: moving(number, (None, model, TILE))})
        if forward:
            take(**{"up_bias_" + name: moving(number, (2, TILE))})
        else:
            take(**{"active_" + name: moving(number, (PAD, TILE)), "slope_" + name: moving(number, (PAD, TILE))})
    out_names, out_specs, out_shape = [], [], []

    def give(spec, shape, kind, *given, make=jax.ShapeDtypeStruct):
        for name in given:
            out_names.append(name)
            out_specs.append(spec)
            out_shape.append(make(shape, kind))

    full = (PAD, model)
    if first and forward:
        give(rows, full, F32, "middle_out", make=pltpu.HBM)
        give(rows, full, BF16, "normed_out", make=pltpu.HBM)
    if not last:
        if forward:
            give(rows, full, F32, "acc_out")
        if backward:
            give(rows, full, F32, "dn_out")
    else:
        if forward:
            give(rows, full, BF16, "result")
        if backward:
            give(pl.BlockSpec((8, model), lambda j, c: (0, 0)), (8, model), F32, "sums")
            give(rows, full, F32, "dmid")
            give(rows, full, BF16, "dattn")
    for number, name in enumerate(sets):
        if forward and not backward:
            give(moving(number, (PAD, TILE)), (PAD, units), BF16, "active_" + name, "slope_" + name, make=pltpu.HBM)
        if backward:
            if name == "own":
                stacked = pl.BlockSpec((2, model, TILE), lambda j, c: (0, 0, j))
                give(stacked, (2, model, units), BF16, "grads_own", make=pltpu.HBM)
            else:
                give(moving(number, (model, TILE)), (model, units), BF16, "down_grad", "up_grad")
            give(moving(number, (1, TILE)), (1, units), F32, "bias_grad_" + name)
    scratch = dict(normed_s=pltpu.VMEM(full, BF16))
    if forward:
        scratch.update(acc_s=pltpu.VMEM(full, F32))
    if backward:
        scratch.update(
            grad_s=pltpu.VMEM(full, BF16),
            dn_s=pltpu.VMEM(full, F32),
            grad_t=pltpu.VMEM((model, MAIN), BF16),
            grad_c=pltpu.VMEM((model, 128), F32),
            normed_t=pltpu.VMEM((model, MAIN), BF16),
            normed_c=pltpu.VMEM((model, 128), F32),
        )
    results = pl.pallas_call(
        functools.partial(_mlp_kernel, (*names, *out_names, *scratch), plan),
        grid_spec=pltpu.PrefetchScalarGridSpec(
            num_scalar_prefetch=1,
            grid=(steps * len(sets),),
            in_specs=in_specs,
            out_specs=out_specs,
            scratch_shapes=list(scratch.values()),
        ),
        out_shape=out_shape,
        compiler_params=pltpu.CompilerParams(vmem_limit_bytes=(30 if not backward else 44 if forward else 38 if last else 27) * MIB),
        cost_estimate=cost(5 * steps * len(sets) * ((0.7 if forward else 0) + (0.9 if backward else 0))),
        name="mlp_" + ("f" if forward else "") + ("b" if backward else "") + "_" + "_".join(sets),
    )(values["coords"], *operands)
    return dict(zip(out_names, results, strict=True))


def _head_grad_kernel(
    pieces, order, coords_ref, dq_ref, dk_ref, dk_got_ref, dv_ref, dv_got_ref, dmid_ref, normed_ref, attended_ref,
    own_ref, peer_ref, dkv_ref, low_s, xt_s, column_s, yt_s, column_y,
):
    step = pl.program_id(0)
    half = own_ref.shape[1]

    def turn(x_ref):
        _fill_turned(coords_ref, order, pieces, x_ref, xt_s, column_s, False)
        _fill_turned(coords_ref, order, pieces, x_ref, yt_s, column_y, True)

    def outer(total):
        _outer(xt_s, column_s, total[:, :half], own_ref)
        _outer(yt_s, column_y, total[:, half:], peer_ref)

    @pl.when(step == 0)
    def _():
        turn(normed_ref)
        outer(dq_ref[...])

    for number, (mine, got) in enumerate(((dk_ref, dk_got_ref), (dv_ref, dv_got_ref))):

        @pl.when(step == 1 + number)
        def _(number=number, mine=mine, got=got):
            total = (mine[...].astype(F32) + got[...].astype(F32)).astype(BF16)
            dkv_ref[:, number * 2 * half : (number + 1) * 2 * half] = total
            outer(total)

    @pl.when(step == 3)
    def _():
        low_s[...] = dmid_ref[...].astype(BF16)
        turn(low_s)
        outer(attended_ref[...])


def head_gradients(pieces, order, coords, dq, dk, dk_got, dv, dv_got, dmid, normed, attended):
    model = dq.shape[1]
    half = model // 2
    rows = pl.BlockSpec((PAD, model), lambda j, c: (0, 0), pipeline_mode=pl.Buffered(1))
    grads = pl.BlockSpec((model, half), lambda j, c: (0, j))
    weight = pltpu.HBM((model, 4 * half), BF16)
    return pl.pallas_call(
        functools.partial(_head_grad_kernel, pieces, order),
        grid_spec=pltpu.PrefetchScalarGridSpec(
            num_scalar_prefetch=1,
            grid=(4,),
            in_specs=[rows] * 8,
            out_specs=[grads, grads, pl.BlockSpec((PAD, 2 * model), lambda j, c: (0, 0))],
            scratch_shapes=[
                pltpu.VMEM((PAD, model), BF16),
                pltpu.VMEM((model, MAIN), BF16),
                pltpu.VMEM((model, 128), F32),
                pltpu.VMEM((model, MAIN), BF16),
                pltpu.VMEM((model, 128), F32),
            ],
        ),
        out_shape=[weight, weight, jax.ShapeDtypeStruct((PAD, 2 * model), BF16)],
        compiler_params=pltpu.CompilerParams(vmem_limit_bytes=25 * MIB),
        cost_estimate=cost(13),
        name="head_gradients",
    )(coords, dq, dk, dk_got, dv, dv_got, dmid, normed, attended)


def _entry_back_kernel(
    layer, pieces, order, coords_ref, dq_ref, dkv_ref, dmid_ref, hidden_ref, xa_ref, xb_ref, gain_ref,
    qa_ref, qb_ref, wa_ref, wb_ref, own_ref, peer_ref, back_ref, skip_back_ref, sums_ref,
    da_s, low_s, xt_s, column_s, yt_s, column_y,
):
    step = pl.program_id(0)
    half = qa_ref.shape[1]

    def columns(ref, at):
        def run():
            total = _dot(ref[:, at : at + half], qa_ref[...], ((1,), (1,)))
            total = total + _dot(ref[:, at + half : at + 2 * half], qb_ref[...], ((1,), (1,)))
            da_s[...] = total if ref is dq_ref else da_s[...] + total

        return run

    pl.when(step == 0)(columns(dq_ref, 0))
    pl.when(step == 1)(columns(dkv_ref, 0))
    pl.when(step == 2)(columns(dkv_ref, 2 * half))

    @pl.when(step == 3)
    def _():
        da = da_s[...]
        normed, inverse = _moments(hidden_ref[...])
        sums_ref[0:1, :] = jnp.sum(da * normed, axis=0, keepdims=True)
        sums_ref[1:2, :] = jnp.sum(da, axis=0, keepdims=True)
        dhid = dmid_ref[...] + _norm_back(normed, inverse, _row(gain_ref, layer), da)
        sums_ref[2:3, :] = jnp.sum(dhid, axis=0, keepdims=True)
        sums_ref[3:8, :] = jnp.zeros_like(sums_ref[3:8, :])
        first = coords_ref[1] == 0
        low_s[...] = jnp.where(first, xa_ref[...], xb_ref[...])
        _fill_turned(coords_ref, order, pieces, low_s, xt_s, column_s, False)
        low_s[...] = jnp.where(first, xb_ref[...], xa_ref[...])
        _fill_turned(coords_ref, order, pieces, low_s, yt_s, column_y, True)
        low_s[...] = dhid.astype(BF16)

    for number in range(2):

        @pl.when(step == 3 + number)
        def _(number=number):
            dy = low_s[:, number * half : (number + 1) * half]
            _outer(xt_s, column_s, dy, own_ref)
            _outer(yt_s, column_y, dy, peer_ref)

    @pl.when(step == 4)
    def _():
        first = coords_ref[1] == 0
        one = _dot(low_s[...], wa_ref[...], ((1,), (1,)))
        two = _dot(low_s[...], wb_ref[...], ((1,), (1,)))
        back_ref[...] = jnp.where(first, one, two).astype(back_ref.dtype)
        skip_back_ref[...] = jnp.where(first, two, one).astype(BF16)


def entry_backward(layer, pieces, order, coords, dq, dkv, dmid, hidden, xa, xb, gain, qa, qb, wa, wb):
    model = xa.shape[1]
    half = qa.shape[3]
    once = pl.Buffered(1)
    rows = pl.BlockSpec((PAD, model), lambda j, c: (0, 0), pipeline_mode=once)
    pair = pl.BlockSpec((PAD, 2 * model), lambda j, c: (0, 0), pipeline_mode=once)
    linear = pl.BlockSpec((None, None, model, model), lambda j, c: (layer, 0, 0, 0), pipeline_mode=once)
    vector = pl.BlockSpec(gain.shape, lambda j, c: (0, 0))
    third = pl.BlockSpec((None, None, model, half), lambda j, c: (layer, jnp.minimum(j, 2), 0, 0))
    grads = pl.BlockSpec((model, half), lambda j, c: (0, jnp.maximum(j, 3) - 3))
    weight = pltpu.HBM((model, 2 * half), BF16)
    return pl.pallas_call(
        functools.partial(_entry_back_kernel, layer, pieces, order),
        grid_spec=pltpu.PrefetchScalarGridSpec(
            num_scalar_prefetch=1,
            grid=(5,),
            in_specs=[rows, pair, rows, rows, rows, rows, vector, third, third, linear, linear],
            out_specs=[grads, grads, rows, rows, pl.BlockSpec((8, model), lambda j, c: (0, 0))],
            scratch_shapes=[
                pltpu.VMEM((PAD, model), F32),
                pltpu.VMEM((PAD, model), BF16),
                pltpu.VMEM((model, MAIN), BF16),
                pltpu.VMEM((model, 128), F32),
                pltpu.VMEM((model, MAIN), BF16),
                pltpu.VMEM((model, 128), F32),
            ],
        ),
        out_shape=[
            weight,
            weight,
            jax.ShapeDtypeStruct((PAD, model), BF16 if layer == 0 else F32),
            jax.ShapeDtypeStruct((PAD, model), BF16),
            jax.ShapeDtypeStruct((8, model), F32),
        ],
        compiler_params=pltpu.CompilerParams(vmem_limit_bytes=40 * MIB),
        cost_estimate=cost(20),
        name="entry_backward",
    )(coords, dq, dkv, dmid, hidden, xa, xb, gain, qa, qb, wa, wb)


def _gather_kernel(count, core_ref, *refs):
    first = core_ref[0] == 0
    out_ref = refs[-1]
    for layer in range(count):
        mine, theirs = refs[2 * layer][...], refs[2 * layer + 1][...]
        low = jnp.where(first, mine, theirs)
        high = jnp.where(first, theirs, mine)
        for start, part in ((0, low[:MAIN]), (MAIN, high[:MAIN]), (2 * MAIN, low[MAIN : MAIN + 1]), (2 * MAIN + 1, high[MAIN : MAIN + 1])):
            at = slice(start, start + part.shape[0])
            if count == 1:
                out_ref[at, :] = part
            else:
                out_ref[at, layer, :] = part


def gather_rows(core, *pairs):
    width = pairs[0][0].shape[1]
    count = len(pairs)
    shape = (2 * MAIN + 2, width) if count == 1 else (2 * MAIN + 2, count, width)
    flat = [value for pair in pairs for value in pair]
    return pl.pallas_call(
        functools.partial(_gather_kernel, count),
        in_specs=[pl.BlockSpec(memory_space=pltpu.SMEM)] + [pl.BlockSpec(memory_space=pltpu.VMEM)] * len(flat),
        out_specs=pl.BlockSpec(memory_space=pltpu.VMEM),
        out_shape=jax.ShapeDtypeStruct(shape, BF16),
        compiler_params=pltpu.CompilerParams(vmem_limit_bytes=16 * MIB),
        cost_estimate=cost(3),
        name="gather_rows",
    )(jnp.reshape(core, (1,)).astype(jnp.int32), *flat)


def _pack_kernel(counts, lead, *refs):
    out_ref = refs[-1]
    for which in range(lead):
        value, at = None, 0
        for count in counts:
            term = (refs[at][which] if lead == 2 else refs[at][...]) if count == 1 else refs[at + which][...]
            value = term.astype(F32) if value is None else value + term.astype(F32)
            at += count
        if lead == 2:
            out_ref[which] = value.astype(BF16)
        else:
            out_ref[...] = value.astype(BF16)


def pack(parts, start, stop):
    block = math.gcd(math.gcd(start, stop), 128)
    columns = parts[0][0][0].shape[-1]
    lead = 2 if parts[0][0][0].ndim == 3 else 1
    in_specs, operands = [], []
    for arrays, at in parts:
        first = (at + start) // block
        for array in arrays:
            if array.ndim == 3:
                in_specs.append(pl.BlockSpec((2, block, columns), lambda j, first=first: (0, first + j, 0)))
            else:
                in_specs.append(pl.BlockSpec((block, columns), lambda j, first=first: (first + j, 0)))
            operands.append(_far(array))
    if lead == 2:
        out_spec = pl.BlockSpec((2, block, columns), lambda j: (0, j, 0))
        out_shape = jax.ShapeDtypeStruct((2, stop - start, columns), BF16)
    else:
        out_spec = pl.BlockSpec((block, columns), lambda j: (j, 0))
        out_shape = jax.ShapeDtypeStruct((stop - start, columns), BF16)
    return pl.pallas_call(
        functools.partial(_pack_kernel, tuple(len(arrays) for arrays, _ in parts), lead),
        grid=((stop - start) // block,),
        in_specs=in_specs,
        out_specs=out_spec,
        out_shape=out_shape,
        compiler_params=pltpu.CompilerParams(vmem_limit_bytes=12 * MIB),
        cost_estimate=cost(80),
        name="pack",
    )(*operands)


def swap_cores(value):
    return lax.ppermute(value, "tensor", [(0, 1), (1, 0)])


def swap_bits(value, bits, size, crossed):
    cores = 2
    pairs = []
    for index in range(size):
        for core in range(cores):
            other = index
            for bit in bits:
                other = other ^ (1 << ((bit ^ core) if crossed and bit < 2 else bit))
            pairs.append((index * cores + core, other * cores + core))
    return lax.ppermute(value, ("dp", "tensor"), pairs)


def after(value, *others):
    return lax.optimization_barrier((value, others))[0]


def total(parts):
    result = parts[0].astype(F32)
    for part in parts[1:]:
        result = result + part.astype(F32)
    return result


class Reduction:
    def __init__(self, parts, order, size, axis=0, crossed=True):
        self.parts = [(part if isinstance(part, tuple) else (part,), 0) for part in parts]
        self.length, self.order, self.size = parts[0].shape[axis], list(order), size
        self.axis, self.crossed = axis, crossed

    def span(self, start, stop):
        values = []
        for arrays, at in self.parts:
            if len(arrays) == 1:
                values.append(lax.slice_in_dim(arrays[0], at + start, at + stop, axis=self.axis))
            else:
                values.append(jnp.stack([array[at + start : at + stop] for array in arrays]))
        return total(values)

    def piece(self, start, stop):
        if self.parts[0][0][0].dtype == BF16:
            return pack(self.parts, start, stop)
        return self.span(start, stop)

    def send(self, gate, count=1, hold=()):
        bits, self.order = self.order[:count], self.order[count:]
        held = lax.optimization_barrier(([arrays for arrays, _ in self.parts], gate))[0]
        self.parts = [(arrays, at) for arrays, (_, at) in zip(held, self.parts)]
        self.length >>= len(bits)
        sent, got = [], []
        for block in range(1, 1 << len(bits)):
            start = block * self.length
            sent.append(self.piece(start, start + self.length))
            across = [bit for place, bit in enumerate(reversed(bits)) if (block >> place) & 1]
            ready = after(sent[-1], *hold) if hold else sent[-1]
            got.append(swap_bits(ready, across, self.size, self.crossed))
        self.parts += [((value,), 0) for value in got]
        return sent, got

    def result(self, gate):
        held = lax.optimization_barrier(([arrays for arrays, _ in self.parts], gate))[0]
        self.parts = [(arrays, at) for arrays, (_, at) in zip(held, self.parts)]
        return self.span(0, self.length)


def arrange(value, order, size):
    bits = size.bit_length() - 1
    index = lax.axis_index("dp")
    view = value.reshape((2,) * bits + value.shape[1:])
    for bit in range(bits):
        axis = bits - 1 - bit
        view = jnp.where((index >> bit) & 1 == 1, jnp.flip(view, axis), view)
    axes = [bits - 1 - bit for bit in order] + list(range(bits, view.ndim))
    return view.transpose(axes).reshape(value.shape)


def localize(value, core):
    main = lax.dynamic_slice_in_dim(value, core * MAIN, MAIN, 0)
    extra = lax.dynamic_slice_in_dim(value, 2 * MAIN + core, 1, 0)
    blank = jnp.zeros((PAD - MAIN - 1,) + value.shape[1:], value.dtype)
    return jnp.concatenate([main, extra, blank], axis=0)


def globalize(core, *mine):
    return gather_rows(core, *((value, swap_cores(value)) for value in mine))


def sum_vectors(shared, up_own, up_peer, size):
    count, model = shared.shape
    layers, units = up_own.shape
    order = tuple(range(size.bit_length() - 1))

    def blocks(offsets):
        first = shared.reshape(count, size, model // size).transpose(1, 0, 2)
        second = offsets.reshape(layers, size, units // model, model // size)
        second = second.transpose(1, 0, 2, 3).reshape(size, -1, model // size)
        return arrange(jnp.concatenate([first, second], axis=1), order, size)

    return Reduction([blocks(up_own), swap_cores(blocks(up_peer))], order, size, crossed=False)


def body(
    inputs, skips, cotangent, skip_weight, skip_bias, attn_norm_gain, attn_norm_bias, qkv_weight,
    proj_weight, proj_bias, ffn_norm_gain, ffn_norm_bias, up_weight, up_bias, down_weight, down_bias,
):
    core = lax.axis_index("tensor")
    size = lax.axis_size("dp")
    bits = size.bit_length() - 1
    assert size == 1 << bits and bits >= 2
    order = tuple(range(bits))
    order_mlp = order
    layers, model = skip_bias.shape
    assert layers == 2
    coords = jnp.stack([lax.axis_index("dp"), core]).astype(jnp.int32)

    qkv_turned = qkv_weight.transpose(0, 2, 1, 3)
    skip_peer, qkv_peer, up_bias_peer = swap_cores(skip_weight), swap_cores(qkv_turned), swap_cores(up_bias)
    weights = dict(
        coords=coords, proj_own=proj_weight, up_own=up_weight, down_own=down_weight, up_bias_own=up_bias,
        up_bias_peer=up_bias_peer, proj_bias=proj_bias, down_bias=down_bias, gain=ffn_norm_gain, shift=ffn_norm_bias,
    )
    skip_parts = localize(skips.transpose(1, 0, 2), core)

    rows0 = localize(inputs, core)
    weights["up_peer"] = swap_cores(after(up_weight, skip_peer, qkv_peer, skip_parts, rows0))

    def enter(layer, residual):
        skip_rows = skip_parts[:, layer]
        hidden, normed, q, kv = entry_forward(
            layer, coords, residual, skip_rows, skip_weight, skip_peer, skip_bias, attn_norm_gain, attn_norm_bias,
            qkv_turned, qkv_peer,
        )
        kv_other = swap_cores(kv)
        if layer == 0:
            kv_other = after(kv_other, weights["up_peer"], up_bias_peer)
        attended, exact, e, ex, il = attn_forward(q, kv, kv_other)
        return dict(xa=residual, xb=skip_rows, hidden=hidden, normed=normed, q=q, kv=kv, kv_other=kv_other,
                    attended=attended, exact=exact, e=e, ex=ex, il=il)

    items, result, flying, crossing = {}, {}, [], []

    def add(name, layer, own, *peer):
        theirs = tuple(swap_cores(value) for value in peer)
        crossing.extend(theirs)
        items[name, layer] = Reduction([own, theirs], order, size, own.ndim - 2)

    def sends(gate, *keys, count=1, hold=()):
        made = []
        for key in keys:
            item = items[key]
            if item.order:
                sent, got = item.send(gate, count, hold)
                made.extend(sent)
                flying.extend(got)
            elif key not in result:
                result[key] = item.result(gate)
                made.append(result[key])
        return after(gate, *made) if made else gate

    def turn(gate, early=(), late=(), made=()):
        gate = after(gate, *crossing)
        crossing.clear()
        waiting = list(flying)
        flying.clear()
        gate = sends(sends(gate, *early), *made, hold=waiting)
        return sends(after(gate, *waiting), *late)

    def back(layer, kept, mid, dattn, keys, then):
        dq, dk, dk_other, dv, dv_other = attn_backward(
            kept["q"], kept["kv"], kept["kv_other"], dattn, kept["exact"], kept["e"], kept["ex"], kept["il"]
        )
        own, peer, dkv = head_gradients(
            size, order, coords, dq, dk, swap_cores(dk_other), dv, swap_cores(dv_other), mid["dmid"], kept["normed"],
            kept["attended"],
        )
        dkv = turn(dkv, (), keys)
        add("head", layer, own, after(peer, dkv))
        own, peer, gradient, skip_grad, sums = entry_backward(
            layer, size, order, coords, dq, dkv, mid["dmid"], kept["hidden"], kept["xa"], kept["xb"], attn_norm_gain,
            qkv_turned, qkv_peer, skip_weight, skip_peer,
        )
        gradient = turn(gradient, *then)
        add("skip", layer, own, after(peer, gradient))
        return gradient, skip_grad, sums

    kept = [None] * layers
    kept[0] = enter(0, rows0)
    late = after((proj_weight, down_weight), kept[0]["kv_other"])
    weights["proj_peer"], weights["down_peer"] = (swap_cores(item) for item in late)
    mid0 = mlp(0, True, True, True, False, ("peer", "own"), size, order_mlp, {**weights, **kept[0]})
    kept[1] = enter(1, mid0["result"])
    values = {**weights, **kept[1], "grad": localize(cotangent, core)}
    one = mlp(1, True, False, True, True, ("peer",), size, order_mlp, values)
    values.update(normed=one["normed_out"], middle=one["middle_out"], acc=one["acc_out"], dn=one["dn_out"])
    theirs = tuple(swap_cores(one[name]) for name in ("down_grad", "up_grad"))
    crossing.extend(theirs)
    two = mlp(1, False, True, True, True, ("own",), size, order, values)
    items["mlp", 1] = Reduction([two["grads_own"], theirs], order, size, 1)
    dattn = turn(two["dattn"], (("mlp", 1),))
    gradient, skip_grad1, sums1 = back(1, kept[1], two, dattn, (("mlp", 1),), ((("head", 1),), (("mlp", 1),)))

    values = {**weights, **kept[0], **mid0, "normed": mid0["normed_out"], "middle": mid0["middle_out"], "grad": gradient}
    one0 = mlp(0, True, False, False, True, ("peer",), size, order, values)
    gate = turn(one0["dn_out"], (("skip", 1),), (("head", 1), ("mlp", 1)))
    peers = [after(one0[name], gate) for name in ("down_grad", "up_grad")]
    theirs = tuple(swap_cores(value) for value in peers)
    crossing.extend(theirs)
    values.update(dn=gate)
    low = mlp(0, False, True, False, True, ("own",), size, order, values)
    items["mlp", 0] = Reduction([low["grads_own"], theirs], order, size, 1)
    dattn = turn(low["dattn"], (), (("head", 1), ("mlp", 1), ("skip", 1)), (("mlp", 0),))
    gradient, skip_grad0, sums0 = back(
        0, kept[0], low, dattn, (("mlp", 0), ("head", 1), ("skip", 1)), ((("head", 0),), (("mlp", 0), ("skip", 1)))
    )
    shared = jnp.concatenate([low["sums"][:4], two["sums"][:4], sums0[:3], sums1[:3]], axis=0)
    items["vectors", 0] = sum_vectors(
        shared,
        jnp.concatenate([low["bias_grad_own"], two["bias_grad_own"]], axis=0),
        jnp.concatenate([one0["bias_grad_peer"], one["bias_grad_peer"]], axis=0),
        size,
    )
    rest = bits - 2
    others = [swap_cores(after(value, gradient)) for value in (gradient, skip_grad0, skip_grad1, two["result"])]
    input_grad = gather_rows(core, (gradient, others[0]))
    skip_grad = gather_rows(core, (after(skip_grad0, input_grad), others[1]), (skip_grad1, others[2]))
    output = gather_rows(core, (after(two["result"], skip_grad), others[3]))
    finish = turn(after(gradient, output), (("skip", 0),), (("mlp", 0), ("head", 0), ("skip", 1)))
    finish = sends(finish, ("vectors", 0), count=2)
    finish = turn(finish)
    finish = sends(finish, ("head", 0), count=rest)
    finish = turn(sends(finish, ("skip", 0), ("vectors", 0), ("mlp", 0), ("head", 1)))
    finish = sends(finish, ("skip", 0), count=rest)
    finish = turn(sends(finish, ("vectors", 0), ("head", 0)))
    while len(result) < len(items):
        finish = turn(sends(finish, *items))
    count = shared.shape[0]
    vectors = result["vectors", 0][0, :count]
    up_bias_grad = result["vectors", 0][0, count:].reshape(layers, -1)
    skip_grad = skip_grad.transpose(1, 0, 2)
    outer = vectors[:8].reshape(2, 4, -1)
    inner = vectors[8:].reshape(2, 3, -1)

    half = model // 2

    def columns(start, stop):
        return jnp.stack([result["head", layer][:, start:stop] for layer in range(layers)])

    def matrix(which):
        return jnp.stack([result["mlp", layer][which] for layer in range(layers)])

    return (
        output, input_grad, skip_grad, jnp.stack([result["skip", layer] for layer in range(layers)])[:, None],
        inner[:, 2], inner[:, 0], inner[:, 1],
        columns(0, 3 * half).reshape(layers, -1, 3, qkv_weight.shape[3]), columns(3 * half, 4 * half),
        outer[:, 3], outer[:, 1], outer[:, 2],
        matrix(1), up_bias_grad, matrix(0), outer[:, 0],
    )


def solution(mesh):
    return jax.shard_map(
        body,
        mesh=mesh,
        in_specs=(
            P("dp", None), P(None, "dp", None), P("dp", None), P(None, "tensor", None, None), P(), P(),
            P(), P(None, None, None, "tensor"), P(None, None, "tensor"), P(), P(), P(),
            P(None, None, "tensor"), P(None, "tensor"), P(None, None, "tensor"), P(),
        ),
        out_specs=(
            P("dp", None), P("dp", None), P(None, "dp", None), P(None, "tensor", "dp", None),
            P(None, "dp"), P(None, "dp"), P(None, "dp"), P(None, "dp", None, "tensor"),
            P(None, "dp", "tensor"), P(None, "dp"), P(None, "dp"), P(None, "dp"),
            P(None, "dp", "tensor"), P(None, ("tensor", "dp")), P(None, "dp", "tensor"), P(None, "dp"),
        ),
        check_vma=False,
    )
```

```python
import functools
import math
import types

import jax
import jax.numpy as jnp
from jax import lax
from jax.experimental import pallas as pl
from jax.experimental.pallas import tpu as pltpu
from jax.sharding import PartitionSpec as P

F32 = jnp.float32
BF16 = jnp.bfloat16
HD = 64
MAIN = 512
PAD = 528
GROUP = 256
HEADS_IN_GROUP = GROUP // HD
MIB = 1024 * 1024
SCALE = 0.1


def cost(microseconds):
    return pl.CostEstimate(flops=1, bytes_accessed=int(microseconds * SCALE * 3.5e6), transcendentals=0)


def _dot(a, b, dims):
    return lax.dot_general(a, b, (dims, ((), ())), preferred_element_type=F32)


def _extra_rows(mine_ref, other_ref):
    row = lax.broadcasted_iota(jnp.int32, (16, GROUP), 0)
    lane = lax.broadcasted_iota(jnp.int32, (16, GROUP), 1)
    mine = jnp.broadcast_to(mine_ref[MAIN : MAIN + 16, :][0:1].astype(F32), (16, GROUP))
    other = jnp.broadcast_to(other_ref[MAIN : MAIN + 16, :][0:1].astype(F32), (16, GROUP))
    value = jnp.where(row % 2 == 0, mine, other)
    return jnp.where(row // 2 == lane // HD, value, 0.0).astype(BF16)


def _attn_fwd_kernel(q_ref, km_ref, vm_ref, ko_ref, vo_ref, o_ref, of_ref, e_ref, ex_ref, il_ref, k_s, v_s):
    k_s[:MAIN] = km_ref[:MAIN]
    k_s[MAIN:] = ko_ref[:MAIN]
    v_s[:MAIN] = vm_ref[:MAIN]
    v_s[MAIN:] = vo_ref[:MAIN]
    lane = lax.broadcasted_iota(jnp.int32, (PAD, GROUP), 1) // HD
    slot = lax.broadcasted_iota(jnp.int32, (PAD, 16), 1) // 2
    q = q_ref[...] * jnp.asarray(HD**-0.5, BF16)
    kx = _extra_rows(km_ref, ko_ref)
    vx = _extra_rows(vm_ref, vo_ref)
    sx = _dot(q, kx, ((1,), (1,)))
    out = jnp.zeros((PAD, GROUP), F32)
    ex_all = jnp.zeros((PAD, 16), F32)
    il_all = jnp.zeros((PAD, 16), F32)
    lane_v = lax.broadcasted_iota(jnp.int32, (2 * MAIN, GROUP), 1) // HD
    ones = jnp.ones((2 * MAIN, GROUP), BF16)
    for h in range(HEADS_IN_GROUP):
        qh = jnp.where(lane == h, q, jnp.zeros_like(q))
        s = _dot(qh, k_s[...], ((1,), (1,)))
        sxh = jnp.where(slot == h, sx, -jnp.inf)
        top = jnp.maximum(jnp.max(s, axis=1, keepdims=True), jnp.max(sxh, axis=1, keepdims=True))
        low = jnp.exp(s - top).astype(BF16)
        e_ref[h] = low
        exh = jnp.exp(sxh - top)
        other = (h + 1) % HEADS_IN_GROUP
        summed = _dot(low, jnp.where(lane_v == h, v_s[...], ones), ((1,), (0,)))
        total = summed[:, other * HD : other * HD + 1] + jnp.sum(exh, axis=1, keepdims=True)
        inverse = 1.0 / total
        out = out + jnp.where(lane == h, summed * inverse, 0.0)
        ex_all = ex_all + exh
        il_all = il_all + jnp.where(slot == h, inverse, 0.0)
    out = out + _dot((ex_all * il_all).astype(BF16), vx, ((1,), (0,)))
    o_ref[...] = out.astype(BF16)
    of_ref[...] = out
    ex_ref[0] = ex_all
    il_ref[0] = il_all


def _far(value):
    return pltpu.with_memory_space_constraint(value, pltpu.HBM)


def attn_forward(q, kv, kv_other):
    width = q.shape[1]
    groups = width // GROUP

    def near(offset):
        return pl.BlockSpec((PAD, GROUP), lambda g: (0, g + offset))

    def far(offset):
        return pl.BlockSpec((PAD, GROUP), lambda g: (0, (g + groups // 2) % groups + offset))

    heads = width // HD
    kv, kv_other = _far(kv), _far(kv_other)
    return pl.pallas_call(
        _attn_fwd_kernel,
        grid=(groups,),
        in_specs=[near(0), near(0), near(groups), far(0), far(groups)],
        out_specs=[
            near(0),
            near(0),
            pl.BlockSpec((HEADS_IN_GROUP, PAD, 2 * MAIN), lambda g: (g, 0, 0)),
            pl.BlockSpec((1, PAD, 16), lambda g: (g, 0, 0)),
            pl.BlockSpec((1, PAD, 16), lambda g: (g, 0, 0)),
        ],
        out_shape=[
            pltpu.HBM((PAD, width), BF16),
            pltpu.HBM((PAD, width), F32),
            pltpu.HBM((heads, PAD, 2 * MAIN), BF16),
            pltpu.HBM((groups, PAD, 16), F32),
            pltpu.HBM((groups, PAD, 16), F32),
        ],
        scratch_shapes=[pltpu.VMEM((2 * MAIN, GROUP), BF16), pltpu.VMEM((2 * MAIN, GROUP), BF16)],
        compiler_params=pltpu.CompilerParams(vmem_limit_bytes=24 * MIB),
        cost_estimate=cost(19),
        name="attn_forward",
    )(q, kv, kv, kv_other, kv_other)


def _attn_bwd_kernel(
    q_ref, km_ref, vm_ref, ko_ref, vo_ref, do_ref, o_ref, e_ref, ex_ref, il_ref,
    dq_ref, dkm_ref, dko_ref, dvm_ref, dvo_ref, k_s, v_s, dk_s, dv_s,
):
    k_s[:MAIN] = km_ref[:MAIN]
    k_s[MAIN:] = ko_ref[:MAIN]
    v_s[:MAIN] = vm_ref[:MAIN]
    v_s[MAIN:] = vo_ref[:MAIN]
    scale = HD**-0.5
    lane = lax.broadcasted_iota(jnp.int32, (PAD, GROUP), 1) // HD
    slot = lax.broadcasted_iota(jnp.int32, (PAD, 16), 1) // 2
    q = q_ref[...] * jnp.asarray(scale, BF16)
    kx = _extra_rows(km_ref, ko_ref)
    vx = _extra_rows(vm_ref, vo_ref)
    il = il_ref[0]
    do = do_ref[...].astype(F32)
    spread = jnp.zeros((PAD, GROUP), F32)
    for h in range(HEADS_IN_GROUP):
        spread = jnp.where(lane == h, il[:, 2 * h : 2 * h + 1], spread)
    dos = (do * spread).astype(BF16)
    product = dos.astype(F32) * o_ref[...]
    inner = jnp.zeros((PAD, 16), F32)
    inners = []
    for h in range(HEADS_IN_GROUP):
        one = jnp.sum(jnp.where(lane == h, product, 0.0), axis=1, keepdims=True)
        inners.append(one)
        inner = jnp.where(slot == h, one, inner)
    dos_t = dos.T
    q_t = q.T
    dq = jnp.zeros((PAD, GROUP), F32)
    for h in range(HEADS_IN_GROUP):
        rows = slice(h * HD, (h + 1) * HD)
        dosh = jnp.where(lane == h, dos, jnp.zeros_like(dos))
        e = e_ref[h]
        dp = _dot(dosh, v_s[...], ((1,), (1,)))
        ds = (e.astype(F32) * (dp - inners[h])).astype(BF16)
        dq = dq + jnp.where(lane == h, _dot(ds, k_s[...], ((1,), (0,))), 0.0)
        dk_s[rows, :] = (
            _dot(q_t[rows, :MAIN], ds[:MAIN], ((1,), (0,)))
            + q_t[rows, MAIN : MAIN + 1].astype(F32) * ds[MAIN : MAIN + 16].astype(F32)[0:1]
        )
        dv_s[rows, :] = (
            _dot(dos_t[rows, :MAIN], e[:MAIN], ((1,), (0,)))
            + dos_t[rows, MAIN : MAIN + 1].astype(F32) * e[MAIN : MAIN + 16].astype(F32)[0:1]
        )
    ex = ex_ref[0]
    dsx = (ex * (_dot(dos, vx, ((1,), (1,))) - inner)).astype(BF16)
    dq = dq + _dot(dsx, kx, ((1,), (0,)))
    dq_ref[...] = (dq * scale).astype(BF16)
    dkx = _dot(dsx, q, ((0,), (0,)))
    dvx = _dot(ex.astype(BF16), dos, ((0,), (0,)))
    row = lax.broadcasted_iota(jnp.int32, (16, GROUP), 0)
    own = row // 2 == lax.broadcasted_iota(jnp.int32, (16, GROUP), 1) // HD
    for half, (dk_ref, dv_ref) in enumerate(((dkm_ref, dvm_ref), (dko_ref, dvo_ref))):
        keep = jnp.logical_and(own, row % 2 == half)
        for ref, grad_s, tail in ((dk_ref, dk_s, dkx), (dv_ref, dv_s, dvx)):
            ref[:MAIN] = grad_s[:, half * MAIN : (half + 1) * MAIN].T.astype(BF16)
            last = jnp.sum(jnp.where(keep, tail, 0.0), axis=0, keepdims=True)
            ref[MAIN:] = jnp.where(row == 0, jnp.broadcast_to(last, (16, GROUP)), 0.0).astype(BF16)


def attn_backward(q, kv, kv_other, dout, out, e, ex, il):
    width = q.shape[1]
    groups = width // GROUP

    def near(offset):
        return pl.BlockSpec((PAD, GROUP), lambda g: (0, g + offset))

    def far(offset):
        return pl.BlockSpec((PAD, GROUP), lambda g: (0, (g + groups // 2) % groups + offset))

    small = pl.BlockSpec((1, PAD, 16), lambda g: (g, 0, 0))
    heads = width // HD
    block = jax.ShapeDtypeStruct((PAD, width), BF16)
    far_out = pl.BlockSpec((PAD, GROUP), lambda g: (0, (g + groups // 2) % groups))
    q, kv, kv_other, out, e, ex, il = (_far(value) for value in (q, kv, kv_other, out, e, ex, il))
    return pl.pallas_call(
        _attn_bwd_kernel,
        grid=(groups,),
        in_specs=[
            near(0), near(0), near(groups), far(0), far(groups), near(0), near(0),
            pl.BlockSpec((HEADS_IN_GROUP, PAD, 2 * MAIN), lambda g: (g, 0, 0)), small, small,
        ],
        out_specs=[near(0), near(0), far_out, near(0), far_out],
        out_shape=[block] * 5,
        scratch_shapes=[
            pltpu.VMEM((2 * MAIN, GROUP), BF16),
            pltpu.VMEM((2 * MAIN, GROUP), BF16),
            pltpu.VMEM((GROUP, 2 * MAIN), F32),
            pltpu.VMEM((GROUP, 2 * MAIN), F32),
        ],
        compiler_params=pltpu.CompilerParams(vmem_limit_bytes=23 * MIB),
        cost_estimate=cost(23),
        name="attn_backward",
    )(q, kv, kv, kv_other, kv_other, dout, out, e, ex, il)


EPSILON = 1e-05
TILE = 512
SUB = 256


def _row(ref, layer):
    return ref[layer : layer + 1, :].astype(F32)


def _fill_turned(coords_ref, order, pieces, x_ref, xt_s, column_s, theirs=False):
    features = xt_s.shape[0]
    rows = features // pieces
    span = max(rows, 128)
    me = coords_ref[0]
    for start in range(0, features, span):
        turned = x_ref[:MAIN, start : start + span].T
        last = x_ref[MAIN:, start : start + span].T.astype(F32)[:, 0:1]
        for part in range(span // rows):
            relative = jnp.bitwise_xor(me, start // rows + part)
            place = jnp.int32(0)
            for bit in order:
                shift = jnp.bitwise_xor(coords_ref[1], bit ^ int(theirs)) if bit < 2 else bit
                place = place * 2 + (jnp.right_shift(relative, shift) & 1)
            at = pl.ds(pl.multiple_of(place * rows, rows), rows)
            xt_s[at, :] = turned[part * rows : (part + 1) * rows]
            column_s[at, :] = jnp.broadcast_to(last[part * rows : (part + 1) * rows], (rows, 128))


def _outer(xt_s, column_s, dy, out_ref):
    width = dy.shape[1]
    last_row = dy[MAIN:].astype(F32)[0:1]
    step = xt_s.shape[0] // 2
    for start in range(0, xt_s.shape[0], step):
        at = slice(start, start + step)
        column = jnp.concatenate([column_s[at, :]] * (width // 128), axis=1)
        total = _dot(xt_s[at, :], dy[:MAIN], ((1,), (0,))) + column * last_row
        out_ref[at, :] = total.astype(BF16)


def _moments(values):
    average = jnp.mean(values, axis=-1, keepdims=True)
    centred = values - average
    inverse = lax.rsqrt(jnp.mean(centred * centred, axis=-1, keepdims=True) + EPSILON)
    return centred * inverse, inverse


def _norm_back(normed, inverse, gain, grad):
    scaled = grad * gain
    first = jnp.mean(scaled, axis=-1, keepdims=True)
    second = jnp.mean(scaled * normed, axis=-1, keepdims=True)
    return (scaled - first - normed * second) * inverse


def _gelu_parts(up):
    square = up * up
    bell = jnp.exp(-0.5 * square)
    size = jnp.abs(up)
    t = 1.0 / (1.0 + (0.375 * 0.5**0.5) * size)
    terms = (
        0.21133947372436523, 0.21568892896175385, 0.16666550934314728, 0.2830598056316376,
        -0.1295955926179886, 0.3879369795322418, -0.1350957304239273,
    )
    value = jnp.full_like(t, 0.5 * terms[-1])
    for term in terms[-2::-1]:
        value = value * t + 0.5 * term
    tail = value * t * bell
    cumulative = jnp.where(up < 0.0, tail, 1.0 - tail)
    return up * cumulative, cumulative + up * (bell * 0.3989422804014327)


def _entry_kernel(
    layer, coords_ref, xa_ref, xb_ref, wa_ref, wb_ref, bias_ref, gain_ref, shift_ref, qa_ref, qb_ref,
    hidden_ref, normed_ref, q_ref, kv_ref, normed_s,
):
    step = pl.program_id(0)

    @pl.when(step == 0)
    def _():
        first = coords_ref[1] == 0
        xa, xb = xa_ref[...], xb_ref[...]
        hidden = (
            _dot(jnp.where(first, xa, xb), wa_ref[...], ((1,), (0,)))
            + _dot(jnp.where(first, xb, xa), wb_ref[...], ((1,), (0,)))
            + _row(bias_ref, layer)
        )
        hidden_ref[...] = hidden
        normed, _unused = _moments(hidden)
        low = (normed * _row(gain_ref, layer) + _row(shift_ref, layer)).astype(BF16)
        normed_s[...] = low
        normed_ref[...] = low

    @pl.when(jnp.logical_and(step >= 1, step <= 2))
    def _():
        half = qa_ref.shape[1]
        kv_ref[:, :half] = _dot(normed_s[...], qa_ref[...], ((1,), (0,))).astype(BF16)
        kv_ref[:, half:] = _dot(normed_s[...], qb_ref[...], ((1,), (0,))).astype(BF16)

    @pl.when(step == 3)
    def _():
        half = qa_ref.shape[1]
        q_ref[:, :half] = _dot(normed_s[...], qa_ref[...], ((1,), (0,))).astype(BF16)
        q_ref[:, half:] = _dot(normed_s[...], qb_ref[...], ((1,), (0,))).astype(BF16)


def entry_forward(layer, coords, residual, skip_rows, wa, wb, bias, gain, shift, qa, qb):
    model = residual.shape[1]
    half = qa.shape[3]

    def part(step):
        return jnp.where(step == 3, 0, jnp.maximum(step, 1))

    once = pl.Buffered(1)
    rows = pl.BlockSpec((PAD, model), lambda j, c: (0, 0), pipeline_mode=once)
    square = pl.BlockSpec((None, None, model, model), lambda j, c: (layer, 0, 0, 0), pipeline_mode=once)
    vector = pl.BlockSpec(bias.shape, lambda j, c: (0, 0))
    third = pl.BlockSpec((None, None, model, half), lambda j, c: (layer, part(j), 0, 0))
    return pl.pallas_call(
        functools.partial(_entry_kernel, layer),
        grid_spec=pltpu.PrefetchScalarGridSpec(
            num_scalar_prefetch=1,
            grid=(4,),
            in_specs=[rows, rows, square, square, vector, vector, vector, third, third],
            out_specs=[
                rows,
                rows,
                rows,
                pl.BlockSpec((PAD, 2 * half), lambda j, c: (0, jnp.clip(j - 1, 0, 1))),
            ],
            scratch_shapes=[pltpu.VMEM((PAD, model), BF16)],
        ),
        out_shape=[
            pltpu.HBM((PAD, model), F32),
            pltpu.HBM((PAD, model), BF16),
            pltpu.HBM((PAD, 2 * half), BF16),
            pltpu.HBM((PAD, 4 * half), BF16),
        ],
        compiler_params=pltpu.CompilerParams(vmem_limit_bytes=22 * MIB),
        cost_estimate=cost(14),
        name="entry_forward",
    )(coords, residual, skip_rows, _far(wa), _far(wb), bias, gain, shift, _far(qa), _far(qb))


def _mlp_kernel(names, plan, coords_ref, *refs):
    layer, first, last, forward, backward, sets, pieces, order = plan
    ref = types.SimpleNamespace(**dict(zip(names, refs, strict=True)))
    step = pl.program_id(0)
    steps_per_set = pl.num_programs(0) // len(sets)

    @pl.when(step == 0)
    def _():
        if first and forward:
            half = ref.proj_own.shape[1]
            middle = (
                ref.hidden[...]
                + _dot(ref.attended[:, :half], ref.proj_own[...], ((1,), (1,)))
                + _dot(ref.attended[:, half:], ref.proj_peer[...], ((1,), (1,)))
                + _row(ref.proj_bias, layer)
            )
            ref.middle_out[...] = middle
            normed, _unused = _moments(middle)
            low = (normed * _row(ref.gain, layer) + _row(ref.shift, layer)).astype(BF16)
            ref.normed_out[...] = low
            ref.normed_s[...] = low
            ref.acc_s[...] = middle + _row(ref.down_bias, layer)
        else:
            ref.normed_s[...] = ref.normed[...]
            if forward:
                ref.acc_s[...] = ref.acc[...]
        if backward:
            assert len(sets) == 1
            theirs = sets[0] == "peer"
            ref.grad_s[...] = ref.grad[...].astype(BF16)
            if first:
                ref.dn_s[...] = jnp.zeros_like(ref.dn_s)
            else:
                ref.dn_s[...] = ref.dn[...]
            _fill_turned(coords_ref, order, pieces, ref.grad_s, ref.grad_t, ref.grad_c, theirs)
            _fill_turned(coords_ref, order, pieces, ref.normed_s, ref.normed_t, ref.normed_c, theirs)

    for number, name in enumerate(sets):

        def tile(name=name):
            up_w, down_w = getattr(ref, "up_" + name), getattr(ref, "down_" + name)
            spans = [slice(at, at + SUB) for at in range(0, TILE, SUB)]
            active, slopes = [], []
            if forward:
                bias = _row(getattr(ref, "up_bias_" + name), layer)
                for span in spans:
                    up = _dot(ref.normed_s[...], up_w[:, span], ((1,), (0,))) + bias[:, span]
                    value, slope = _gelu_parts(up)
                    active.append(value.astype(BF16))
                    slopes.append(slope if backward else slope.astype(BF16))
                ref.acc_s[...] += sum(
                    _dot(value, down_w[:, span], ((1,), (1,))) for value, span in zip(active, spans)
                )
                if not backward:
                    for value, slope, span in zip(active, slopes, spans):
                        getattr(ref, "active_" + name)[:, span] = value
                        getattr(ref, "slope_" + name)[:, span] = slope
            else:
                for span in spans:
                    active.append(getattr(ref, "active_" + name)[:, span])
                    slopes.append(getattr(ref, "slope_" + name)[:, span].astype(F32))
            if backward:
                if name == "own":
                    down_out, up_out = ref.grads_own.at[0], ref.grads_own.at[1]
                else:
                    down_out, up_out = ref.down_grad, ref.up_grad
                units = []
                for slope, span in zip(slopes, spans):
                    du = _dot(ref.grad_s[...], down_w[:, span], ((1,), (0,))) * slope
                    getattr(ref, "bias_grad_" + name)[:, span] = jnp.sum(du, axis=0, keepdims=True)
                    units.append(du.astype(BF16))
                ref.dn_s[...] += sum(_dot(du, up_w[:, span], ((1,), (1,))) for du, span in zip(units, spans))
                for value, du, span in zip(active, units, spans):
                    _outer(ref.grad_t, ref.grad_c, value, down_out.at[:, span])
                    _outer(ref.normed_t, ref.normed_c, du, up_out.at[:, span])

        if len(sets) == 1:
            tile()
        else:
            pl.when(step // steps_per_set == number)(tile)

    @pl.when(step == pl.num_programs(0) - 1)
    def _():
        if not last:
            if forward:
                ref.acc_out[...] = ref.acc_s[...]
            if backward:
                ref.dn_out[...] = ref.dn_s[...]
            return
        if forward:
            ref.result[...] = ref.acc_s[...].astype(BF16)
        if backward:
            gradient = ref.grad[...].astype(F32)
            dn = ref.dn_s[...]
            normed, inverse = _moments(ref.middle[...])
            sums = ref.sums
            sums[0:1, :] = jnp.sum(gradient, axis=0, keepdims=True)
            sums[1:2, :] = jnp.sum(dn * normed, axis=0, keepdims=True)
            sums[2:3, :] = jnp.sum(dn, axis=0, keepdims=True)
            dmid = gradient + _norm_back(normed, inverse, _row(ref.gain, layer), dn)
            sums[3:4, :] = jnp.sum(dmid, axis=0, keepdims=True)
            sums[4:8, :] = jnp.zeros_like(sums[4:8, :])
            ref.dmid[...] = dmid
            low = dmid.astype(BF16)
            half = ref.proj_own.shape[1]
            ref.dattn[:, :half] = _dot(low, ref.proj_own[...], ((1,), (0,))).astype(BF16)
            ref.dattn[:, half:] = _dot(low, ref.proj_peer[...], ((1,), (0,))).astype(BF16)


def mlp(layer, first, last, forward, backward, sets, pieces, order, values):
    _unused, model, units = values["up_" + sets[0]].shape
    steps = units // TILE
    plan = (layer, first, last, forward, backward, sets, pieces, order)
    names, in_specs, operands = [], [], []
    once = pl.Buffered(1)
    rows = pl.BlockSpec((PAD, model), lambda j, c: (0, 0), pipeline_mode=once)
    vector = pl.BlockSpec(values["gain"].shape, lambda j, c: (0, 0), pipeline_mode=once)

    def take(**specs):
        for name, spec in specs.items():
            names.append(name)
            in_specs.append(spec)
            operands.append(values[name])

    def moving(number, shape):
        def index(j, c):
            tile = (0, jnp.clip(j - number * steps, 0, steps - 1))
            return tile if len(shape) == 2 else (layer, *tile)

        return pl.BlockSpec(shape, index)

    half = values["proj_own"].shape[2]
    proj = pl.BlockSpec((None, model, half), lambda j, c: (layer, 0, 0), pipeline_mode=once)
    if first and forward:
        take(hidden=rows, attended=rows, proj_own=proj, proj_peer=proj, proj_bias=vector, gain=vector, shift=vector,
             down_bias=vector)
    else:
        take(normed=rows)
        if forward:
            take(acc=rows)
    if backward:
        take(grad=rows)
        if not first:
            take(dn=rows)
        if last:
            take(middle=rows, proj_own=proj, proj_peer=proj, gain=vector)
    for number, name in enumerate(sets):
        take(**{"up_" + name: moving(number, (None, model, TILE)), "down_" + name: moving(number, (None, model, TILE))})
        if forward:
            take(**{"up_bias_" + name: moving(number, (2, TILE))})
        else:
            take(**{"active_" + name: moving(number, (PAD, TILE)), "slope_" + name: moving(number, (PAD, TILE))})
    out_names, out_specs, out_shape = [], [], []

    def give(spec, shape, kind, *given, make=jax.ShapeDtypeStruct):
        for name in given:
            out_names.append(name)
            out_specs.append(spec)
            out_shape.append(make(shape, kind))

    full = (PAD, model)
    if first and forward:
        give(rows, full, F32, "middle_out", make=pltpu.HBM)
        give(rows, full, BF16, "normed_out", make=pltpu.HBM)
    if not last:
        if forward:
            give(rows, full, F32, "acc_out")
        if backward:
            give(rows, full, F32, "dn_out")
    else:
        if forward:
            give(rows, full, BF16, "result")
        if backward:
            give(pl.BlockSpec((8, model), lambda j, c: (0, 0)), (8, model), F32, "sums")
            give(rows, full, F32, "dmid")
            give(rows, full, BF16, "dattn")
    for number, name in enumerate(sets):
        if forward and not backward:
            give(moving(number, (PAD, TILE)), (PAD, units), BF16, "active_" + name, "slope_" + name, make=pltpu.HBM)
        if backward:
            if name == "own":
                stacked = pl.BlockSpec((2, model, TILE), lambda j, c: (0, 0, j))
                give(stacked, (2, model, units), BF16, "grads_own", make=pltpu.HBM)
            else:
                give(moving(number, (model, TILE)), (model, units), BF16, "down_grad", "up_grad")
            give(moving(number, (1, TILE)), (1, units), F32, "bias_grad_" + name)
    scratch = dict(normed_s=pltpu.VMEM(full, BF16))
    if forward:
        scratch.update(acc_s=pltpu.VMEM(full, F32))
    if backward:
        scratch.update(
            grad_s=pltpu.VMEM(full, BF16),
            dn_s=pltpu.VMEM(full, F32),
            grad_t=pltpu.VMEM((model, MAIN), BF16),
            grad_c=pltpu.VMEM((model, 128), F32),
            normed_t=pltpu.VMEM((model, MAIN), BF16),
            normed_c=pltpu.VMEM((model, 128), F32),
        )
    results = pl.pallas_call(
        functools.partial(_mlp_kernel, (*names, *out_names, *scratch), plan),
        grid_spec=pltpu.PrefetchScalarGridSpec(
            num_scalar_prefetch=1,
            grid=(steps * len(sets),),
            in_specs=in_specs,
            out_specs=out_specs,
            scratch_shapes=list(scratch.values()),
        ),
        out_shape=out_shape,
        compiler_params=pltpu.CompilerParams(vmem_limit_bytes=(30 if not backward else 44 if forward else 38 if last else 27) * MIB),
        cost_estimate=cost(5 * steps * len(sets) * ((0.7 if forward else 0) + (0.9 if backward else 0))),
        name="mlp_" + ("f" if forward else "") + ("b" if backward else "") + "_" + "_".join(sets),
    )(values["coords"], *operands)
    return dict(zip(out_names, results, strict=True))


def _head_grad_kernel(
    pieces, order, coords_ref, dq_ref, dk_ref, dk_got_ref, dv_ref, dv_got_ref, dmid_ref, normed_ref, attended_ref,
    own_ref, peer_ref, dkv_ref, low_s, xt_s, column_s, yt_s, column_y,
):
    step = pl.program_id(0)
    half = own_ref.shape[1]

    def turn(x_ref):
        _fill_turned(coords_ref, order, pieces, x_ref, xt_s, column_s, False)
        _fill_turned(coords_ref, order, pieces, x_ref, yt_s, column_y, True)

    def outer(total):
        _outer(xt_s, column_s, total[:, :half], own_ref)
        _outer(yt_s, column_y, total[:, half:], peer_ref)

    @pl.when(step == 0)
    def _():
        turn(normed_ref)
        outer(dq_ref[...])

    for number, (mine, got) in enumerate(((dk_ref, dk_got_ref), (dv_ref, dv_got_ref))):

        @pl.when(step == 1 + number)
        def _(number=number, mine=mine, got=got):
            total = (mine[...].astype(F32) + got[...].astype(F32)).astype(BF16)
            dkv_ref[:, number * 2 * half : (number + 1) * 2 * half] = total
            outer(total)

    @pl.when(step == 3)
    def _():
        low_s[...] = dmid_ref[...].astype(BF16)
        turn(low_s)
        outer(attended_ref[...])


def head_gradients(pieces, order, coords, dq, dk, dk_got, dv, dv_got, dmid, normed, attended):
    model = dq.shape[1]
    half = model // 2
    rows = pl.BlockSpec((PAD, model), lambda j, c: (0, 0), pipeline_mode=pl.Buffered(1))
    grads = pl.BlockSpec((model, half), lambda j, c: (0, j))
    weight = pltpu.HBM((model, 4 * half), BF16)
    return pl.pallas_call(
        functools.partial(_head_grad_kernel, pieces, order),
        grid_spec=pltpu.PrefetchScalarGridSpec(
            num_scalar_prefetch=1,
            grid=(4,),
            in_specs=[rows] * 8,
            out_specs=[grads, grads, pl.BlockSpec((PAD, 2 * model), lambda j, c: (0, 0))],
            scratch_shapes=[
                pltpu.VMEM((PAD, model), BF16),
                pltpu.VMEM((model, MAIN), BF16),
                pltpu.VMEM((model, 128), F32),
                pltpu.VMEM((model, MAIN), BF16),
                pltpu.VMEM((model, 128), F32),
            ],
        ),
        out_shape=[weight, weight, jax.ShapeDtypeStruct((PAD, 2 * model), BF16)],
        compiler_params=pltpu.CompilerParams(vmem_limit_bytes=25 * MIB),
        cost_estimate=cost(13),
        name="head_gradients",
    )(coords, dq, dk, dk_got, dv, dv_got, dmid, normed, attended)


def _entry_back_kernel(
    layer, pieces, order, coords_ref, dq_ref, dkv_ref, dmid_ref, hidden_ref, xa_ref, xb_ref, gain_ref,
    qa_ref, qb_ref, wa_ref, wb_ref, own_ref, peer_ref, back_ref, skip_back_ref, sums_ref,
    da_s, low_s, xt_s, column_s, yt_s, column_y,
):
    step = pl.program_id(0)
    half = qa_ref.shape[1]

    def columns(ref, at):
        def run():
            total = _dot(ref[:, at : at + half], qa_ref[...], ((1,), (1,)))
            total = total + _dot(ref[:, at + half : at + 2 * half], qb_ref[...], ((1,), (1,)))
            da_s[...] = total if ref is dq_ref else da_s[...] + total

        return run

    pl.when(step == 0)(columns(dq_ref, 0))
    pl.when(step == 1)(columns(dkv_ref, 0))
    pl.when(step == 2)(columns(dkv_ref, 2 * half))

    @pl.when(step == 3)
    def _():
        da = da_s[...]
        normed, inverse = _moments(hidden_ref[...])
        sums_ref[0:1, :] = jnp.sum(da * normed, axis=0, keepdims=True)
        sums_ref[1:2, :] = jnp.sum(da, axis=0, keepdims=True)
        dhid = dmid_ref[...] + _norm_back(normed, inverse, _row(gain_ref, layer), da)
        sums_ref[2:3, :] = jnp.sum(dhid, axis=0, keepdims=True)
        sums_ref[3:8, :] = jnp.zeros_like(sums_ref[3:8, :])
        first = coords_ref[1] == 0
        low_s[...] = jnp.where(first, xa_ref[...], xb_ref[...])
        _fill_turned(coords_ref, order, pieces, low_s, xt_s, column_s, False)
        low_s[...] = jnp.where(first, xb_ref[...], xa_ref[...])
        _fill_turned(coords_ref, order, pieces, low_s, yt_s, column_y, True)
        low_s[...] = dhid.astype(BF16)

    for number in range(2):

        @pl.when(step == 3 + number)
        def _(number=number):
            dy = low_s[:, number * half : (number + 1) * half]
            _outer(xt_s, column_s, dy, own_ref)
            _outer(yt_s, column_y, dy, peer_ref)

    @pl.when(step == 4)
    def _():
        first = coords_ref[1] == 0
        one = _dot(low_s[...], wa_ref[...], ((1,), (1,)))
        two = _dot(low_s[...], wb_ref[...], ((1,), (1,)))
        back_ref[...] = jnp.where(first, one, two).astype(back_ref.dtype)
        skip_back_ref[...] = jnp.where(first, two, one).astype(BF16)


def entry_backward(layer, pieces, order, coords, dq, dkv, dmid, hidden, xa, xb, gain, qa, qb, wa, wb):
    model = xa.shape[1]
    half = qa.shape[3]
    once = pl.Buffered(1)
    rows = pl.BlockSpec((PAD, model), lambda j, c: (0, 0), pipeline_mode=once)
    pair = pl.BlockSpec((PAD, 2 * model), lambda j, c: (0, 0), pipeline_mode=once)
    linear = pl.BlockSpec((None, None, model, model), lambda j, c: (layer, 0, 0, 0), pipeline_mode=once)
    vector = pl.BlockSpec(gain.shape, lambda j, c: (0, 0))
    third = pl.BlockSpec((None, None, model, half), lambda j, c: (layer, jnp.minimum(j, 2), 0, 0))
    grads = pl.BlockSpec((model, half), lambda j, c: (0, jnp.maximum(j, 3) - 3))
    weight = pltpu.HBM((model, 2 * half), BF16)
    return pl.pallas_call(
        functools.partial(_entry_back_kernel, layer, pieces, order),
        grid_spec=pltpu.PrefetchScalarGridSpec(
            num_scalar_prefetch=1,
            grid=(5,),
            in_specs=[rows, pair, rows, rows, rows, rows, vector, third, third, linear, linear],
            out_specs=[grads, grads, rows, rows, pl.BlockSpec((8, model), lambda j, c: (0, 0))],
            scratch_shapes=[
                pltpu.VMEM((PAD, model), F32),
                pltpu.VMEM((PAD, model), BF16),
                pltpu.VMEM((model, MAIN), BF16),
                pltpu.VMEM((model, 128), F32),
                pltpu.VMEM((model, MAIN), BF16),
                pltpu.VMEM((model, 128), F32),
            ],
        ),
        out_shape=[
            weight,
            weight,
            jax.ShapeDtypeStruct((PAD, model), BF16 if layer == 0 else F32),
            jax.ShapeDtypeStruct((PAD, model), BF16),
            jax.ShapeDtypeStruct((8, model), F32),
        ],
        compiler_params=pltpu.CompilerParams(vmem_limit_bytes=40 * MIB),
        cost_estimate=cost(20),
        name="entry_backward",
    )(coords, dq, dkv, dmid, hidden, xa, xb, gain, qa, qb, wa, wb)


def _gather_kernel(count, core_ref, *refs):
    first = core_ref[0] == 0
    out_ref = refs[-1]
    for layer in range(count):
        mine, theirs = refs[2 * layer][...], refs[2 * layer + 1][...]
        low = jnp.where(first, mine, theirs)
        high = jnp.where(first, theirs, mine)
        for start, part in ((0, low[:MAIN]), (MAIN, high[:MAIN]), (2 * MAIN, low[MAIN : MAIN + 1]), (2 * MAIN + 1, high[MAIN : MAIN + 1])):
            at = slice(start, start + part.shape[0])
            if count == 1:
                out_ref[at, :] = part
            else:
                out_ref[at, layer, :] = part


def gather_rows(core, *pairs):
    width = pairs[0][0].shape[1]
    count = len(pairs)
    shape = (2 * MAIN + 2, width) if count == 1 else (2 * MAIN + 2, count, width)
    flat = [value for pair in pairs for value in pair]
    return pl.pallas_call(
        functools.partial(_gather_kernel, count),
        in_specs=[pl.BlockSpec(memory_space=pltpu.SMEM)] + [pl.BlockSpec(memory_space=pltpu.VMEM)] * len(flat),
        out_specs=pl.BlockSpec(memory_space=pltpu.VMEM),
        out_shape=jax.ShapeDtypeStruct(shape, BF16),
        compiler_params=pltpu.CompilerParams(vmem_limit_bytes=16 * MIB),
        cost_estimate=cost(3),
        name="gather_rows",
    )(jnp.reshape(core, (1,)).astype(jnp.int32), *flat)


def _pack_kernel(counts, lead, *refs):
    out_ref = refs[-1]
    for which in range(lead):
        value, at = None, 0
        for count in counts:
            term = (refs[at][which] if lead == 2 else refs[at][...]) if count == 1 else refs[at + which][...]
            value = term.astype(F32) if value is None else value + term.astype(F32)
            at += count
        if lead == 2:
            out_ref[which] = value.astype(BF16)
        else:
            out_ref[...] = value.astype(BF16)


def pack(parts, start, stop):
    block = math.gcd(math.gcd(start, stop), 128)
    columns = parts[0][0][0].shape[-1]
    lead = 2 if parts[0][0][0].ndim == 3 else 1
    in_specs, operands = [], []
    for arrays, at in parts:
        first = (at + start) // block
        for array in arrays:
            if array.ndim == 3:
                in_specs.append(pl.BlockSpec((2, block, columns), lambda j, first=first: (0, first + j, 0)))
            else:
                in_specs.append(pl.BlockSpec((block, columns), lambda j, first=first: (first + j, 0)))
            operands.append(_far(array))
    if lead == 2:
        out_spec = pl.BlockSpec((2, block, columns), lambda j: (0, j, 0))
        out_shape = jax.ShapeDtypeStruct((2, stop - start, columns), BF16)
    else:
        out_spec = pl.BlockSpec((block, columns), lambda j: (j, 0))
        out_shape = jax.ShapeDtypeStruct((stop - start, columns), BF16)
    return pl.pallas_call(
        functools.partial(_pack_kernel, tuple(len(arrays) for arrays, _ in parts), lead),
        grid=((stop - start) // block,),
        in_specs=in_specs,
        out_specs=out_spec,
        out_shape=out_shape,
        compiler_params=pltpu.CompilerParams(vmem_limit_bytes=12 * MIB),
        cost_estimate=cost(80),
        name="pack",
    )(*operands)


def swap_cores(value):
    return lax.ppermute(value, "tensor", [(0, 1), (1, 0)])


def swap_bits(value, bits, size, crossed):
    cores = 2
    pairs = []
    for index in range(size):
        for core in range(cores):
            other = index
            for bit in bits:
                other = other ^ (1 << ((bit ^ core) if crossed and bit < 2 else bit))
            pairs.append((index * cores + core, other * cores + core))
    return lax.ppermute(value, ("dp", "tensor"), pairs)


def after(value, *others):
    return lax.optimization_barrier((value, others))[0]


def total(parts):
    result = parts[0].astype(F32)
    for part in parts[1:]:
        result = result + part.astype(F32)
    return result


class Reduction:
    def __init__(self, parts, order, size, axis=0, crossed=True):
        self.parts = [(part if isinstance(part, tuple) else (part,), 0) for part in parts]
        self.length, self.order, self.size = parts[0].shape[axis], list(order), size
        self.axis, self.crossed = axis, crossed

    def span(self, start, stop):
        values = []
        for arrays, at in self.parts:
            if len(arrays) == 1:
                values.append(lax.slice_in_dim(arrays[0], at + start, at + stop, axis=self.axis))
            else:
                values.append(jnp.stack([array[at + start : at + stop] for array in arrays]))
        return total(values)

    def piece(self, start, stop):
        if self.parts[0][0][0].dtype == BF16:
            return pack(self.parts, start, stop)
        return self.span(start, stop)

    def send(self, gate, count=1, hold=()):
        bits, self.order = self.order[:count], self.order[count:]
        held = lax.optimization_barrier(([arrays for arrays, _ in self.parts], gate))[0]
        self.parts = [(arrays, at) for arrays, (_, at) in zip(held, self.parts)]
        self.length >>= len(bits)
        sent, got = [], []
        for block in range(1, 1 << len(bits)):
            start = block * self.length
            sent.append(self.piece(start, start + self.length))
            across = [bit for place, bit in enumerate(reversed(bits)) if (block >> place) & 1]
            ready = after(sent[-1], *hold) if hold else sent[-1]
            got.append(swap_bits(ready, across, self.size, self.crossed))
        self.parts += [((value,), 0) for value in got]
        return sent, got

    def result(self, gate):
        held = lax.optimization_barrier(([arrays for arrays, _ in self.parts], gate))[0]
        self.parts = [(arrays, at) for arrays, (_, at) in zip(held, self.parts)]
        return self.span(0, self.length)


def arrange(value, order, size):
    bits = size.bit_length() - 1
    index = lax.axis_index("dp")
    view = value.reshape((2,) * bits + value.shape[1:])
    for bit in range(bits):
        axis = bits - 1 - bit
        view = jnp.where((index >> bit) & 1 == 1, jnp.flip(view, axis), view)
    axes = [bits - 1 - bit for bit in order] + list(range(bits, view.ndim))
    return view.transpose(axes).reshape(value.shape)


def localize(value, core):
    main = lax.dynamic_slice_in_dim(value, core * MAIN, MAIN, 0)
    extra = lax.dynamic_slice_in_dim(value, 2 * MAIN + core, 1, 0)
    blank = jnp.zeros((PAD - MAIN - 1,) + value.shape[1:], value.dtype)
    return jnp.concatenate([main, extra, blank], axis=0)


def globalize(core, *mine):
    return gather_rows(core, *((value, swap_cores(value)) for value in mine))


def sum_vectors(shared, up_own, up_peer, size):
    count, model = shared.shape
    layers, units = up_own.shape
    order = tuple(range(size.bit_length() - 1))

    def blocks(offsets):
        first = shared.reshape(count, size, model // size).transpose(1, 0, 2)
        second = offsets.reshape(layers, size, units // model, model // size)
        second = second.transpose(1, 0, 2, 3).reshape(size, -1, model // size)
        return arrange(jnp.concatenate([first, second], axis=1), order, size)

    return Reduction([blocks(up_own), swap_cores(blocks(up_peer))], order, size, crossed=False)


def body(
    inputs, skips, cotangent, skip_weight, skip_bias, attn_norm_gain, attn_norm_bias, qkv_weight,
    proj_weight, proj_bias, ffn_norm_gain, ffn_norm_bias, up_weight, up_bias, down_weight, down_bias,
):
    core = lax.axis_index("tensor")
    size = lax.axis_size("dp")
    bits = size.bit_length() - 1
    assert size == 1 << bits and bits >= 2
    order = tuple(range(bits))
    order_mlp = order
    layers, model = skip_bias.shape
    assert layers == 2
    coords = jnp.stack([lax.axis_index("dp"), core]).astype(jnp.int32)

    qkv_turned = qkv_weight.transpose(0, 2, 1, 3)
    skip_peer, qkv_peer, up_bias_peer = swap_cores(skip_weight), swap_cores(qkv_turned), swap_cores(up_bias)
    weights = dict(
        coords=coords, proj_own=proj_weight, up_own=up_weight, down_own=down_weight, up_bias_own=up_bias,
        up_bias_peer=up_bias_peer, proj_bias=proj_bias, down_bias=down_bias, gain=ffn_norm_gain, shift=ffn_norm_bias,
    )
    skip_parts = localize(skips.transpose(1, 0, 2), core)

    skip_parts = [skip_parts[:, layer] for layer in range(layers)]
    rows0 = localize(inputs, core)
    weights["up_peer"] = swap_cores(after(up_weight, skip_peer, qkv_peer, skip_parts, rows0))

    def enter(layer, residual):
        skip_rows = skip_parts[layer]
        hidden, normed, q, kv = entry_forward(
            layer, coords, residual, skip_rows, skip_weight, skip_peer, skip_bias, attn_norm_gain, attn_norm_bias,
            qkv_turned, qkv_peer,
        )
        kv_other = swap_cores(kv)
        if layer == 0:
            kv_other = after(kv_other, weights["up_peer"], up_bias_peer)
        attended, exact, e, ex, il = attn_forward(q, kv, kv_other)
        return dict(xa=residual, xb=skip_rows, hidden=hidden, normed=normed, q=q, kv=kv, kv_other=kv_other,
                    attended=attended, exact=exact, e=e, ex=ex, il=il)

    items, result, flying, crossing = {}, {}, [], []

    def add(name, layer, own, *peer):
        theirs = tuple(swap_cores(value) for value in peer)
        crossing.extend(theirs)
        items[name, layer] = Reduction([own, theirs], order, size, own.ndim - 2)

    def sends(gate, *keys, count=1, hold=()):
        made = []
        for key in keys:
            item = items[key]
            if item.order:
                sent, got = item.send(gate, count, hold)
                made.extend(sent)
                flying.extend(got)
            elif key not in result:
                result[key] = item.result(gate)
                made.append(result[key])
        return after(gate, *made) if made else gate

    def turn(gate, early=(), late=(), made=()):
        gate = after(gate, *crossing)
        crossing.clear()
        waiting = list(flying)
        flying.clear()
        gate = sends(sends(gate, *early), *made, hold=waiting)
        return sends(after(gate, *waiting), *late)

    def back(layer, kept, mid, dattn, keys, then):
        dq, dk, dk_other, dv, dv_other = attn_backward(
            kept["q"], kept["kv"], kept["kv_other"], dattn, kept["exact"], kept["e"], kept["ex"], kept["il"]
        )
        own, peer, dkv = head_gradients(
            size, order, coords, dq, dk, swap_cores(dk_other), dv, swap_cores(dv_other), mid["dmid"], kept["normed"],
            kept["attended"],
        )
        dkv = turn(dkv, (), keys)
        add("head", layer, own, after(peer, dkv))
        own, peer, gradient, skip_grad, sums = entry_backward(
            layer, size, order, coords, dq, dkv, mid["dmid"], kept["hidden"], kept["xa"], kept["xb"], attn_norm_gain,
            qkv_turned, qkv_peer, skip_weight, skip_peer,
        )
        gradient = turn(gradient, *then)
        add("skip", layer, own, after(peer, gradient))
        return gradient, skip_grad, sums

    kept = [None] * layers
    kept[0] = enter(0, rows0)
    late = after((proj_weight, down_weight), kept[0]["kv_other"])
    weights["proj_peer"], weights["down_peer"] = (swap_cores(item) for item in late)
    mid0 = mlp(0, True, True, True, False, ("peer", "own"), size, order_mlp, {**weights, **kept[0]})
    kept[1] = enter(1, mid0["result"])
    values = {**weights, **kept[1], "grad": localize(cotangent, core)}
    one = mlp(1, True, False, True, True, ("peer",), size, order_mlp, values)
    values.update(normed=one["normed_out"], middle=one["middle_out"], acc=one["acc_out"], dn=one["dn_out"])
    theirs = tuple(swap_cores(one[name]) for name in ("down_grad", "up_grad"))
    crossing.extend(theirs)
    two = mlp(1, False, True, True, True, ("own",), size, order, values)
    items["mlp", 1] = Reduction([two["grads_own"], theirs], order, size, 1)
    dattn = turn(two["dattn"], (("mlp", 1),))
    gradient, skip_grad1, sums1 = back(1, kept[1], two, dattn, (("mlp", 1),), ((("head", 1),), (("mlp", 1),)))

    values = {**weights, **kept[0], **mid0, "normed": mid0["normed_out"], "middle": mid0["middle_out"], "grad": gradient}
    one0 = mlp(0, True, False, False, True, ("peer",), size, order, values)
    gate = turn(one0["dn_out"], (("skip", 1),), (("head", 1), ("mlp", 1)))
    peers = [after(one0[name], gate) for name in ("down_grad", "up_grad")]
    theirs = tuple(swap_cores(value) for value in peers)
    crossing.extend(theirs)
    values.update(dn=gate)
    low = mlp(0, False, True, False, True, ("own",), size, order, values)
    items["mlp", 0] = Reduction([low["grads_own"], theirs], order, size, 1)
    dattn = turn(low["dattn"], (), (("head", 1), ("mlp", 1), ("skip", 1)), (("mlp", 0),))
    gradient, skip_grad0, sums0 = back(
        0, kept[0], low, dattn, (("mlp", 0), ("head", 1), ("skip", 1)), ((("head", 0),), (("mlp", 0), ("skip", 1)))
    )
    shared = jnp.concatenate([low["sums"][:4], two["sums"][:4], sums0[:3], sums1[:3]], axis=0)
    items["vectors", 0] = sum_vectors(
        shared,
        jnp.concatenate([low["bias_grad_own"], two["bias_grad_own"]], axis=0),
        jnp.concatenate([one0["bias_grad_peer"], one["bias_grad_peer"]], axis=0),
        size,
    )
    rest = bits - 2
    others = [swap_cores(after(value, gradient)) for value in (gradient, skip_grad0, skip_grad1, two["result"])]
    input_grad = gather_rows(core, (gradient, others[0]))
    skip_grad = gather_rows(core, (after(skip_grad0, input_grad), others[1]), (skip_grad1, others[2]))
    output = gather_rows(core, (after(two["result"], skip_grad), others[3]))
    finish = turn(after(gradient, output), (("skip", 0),), (("mlp", 0), ("head", 0), ("skip", 1)))
    finish = sends(finish, ("vectors", 0), count=2)
    finish = turn(finish)
    finish = sends(finish, ("head", 0), count=rest)
    finish = turn(sends(finish, ("skip", 0), ("vectors", 0), ("mlp", 0), ("head", 1)))
    finish = sends(finish, ("skip", 0), count=rest)
    finish = turn(sends(finish, ("vectors", 0), ("head", 0)))
    while len(result) < len(items):
        finish = turn(sends(finish, *items))
    count = shared.shape[0]
    vectors = result["vectors", 0][0, :count]
    up_bias_grad = result["vectors", 0][0, count:].reshape(layers, -1)
    skip_grad = skip_grad.transpose(1, 0, 2)
    outer = vectors[:8].reshape(2, 4, -1)
    inner = vectors[8:].reshape(2, 3, -1)

    half = model // 2

    def columns(start, stop):
        return jnp.stack([result["head", layer][:, start:stop] for layer in range(layers)])

    def matrix(which):
        return jnp.stack([result["mlp", layer][which] for layer in range(layers)])

    return (
        output, input_grad, skip_grad, jnp.stack([result["skip", layer] for layer in range(layers)])[:, None],
        inner[:, 2], inner[:, 0], inner[:, 1],
        columns(0, 3 * half).reshape(layers, -1, 3, qkv_weight.shape[3]), columns(3 * half, 4 * half),
        outer[:, 3], outer[:, 1], outer[:, 2],
        matrix(1), up_bias_grad, matrix(0), outer[:, 0],
    )


def solution(mesh):
    return jax.shard_map(
        body,
        mesh=mesh,
        in_specs=(
            P("dp", None), P(None, "dp", None), P("dp", None), P(None, "tensor", None, None), P(), P(),
            P(), P(None, None, None, "tensor"), P(None, None, "tensor"), P(), P(), P(),
            P(None, None, "tensor"), P(None, "tensor"), P(None, None, "tensor"), P(),
        ),
        out_specs=(
            P("dp", None), P("dp", None), P(None, "dp", None), P(None, "tensor", "dp", None),
            P(None, "dp"), P(None, "dp"), P(None, "dp"), P(None, "dp", None, "tensor"),
            P(None, "dp", "tensor"), P(None, "dp"), P(None, "dp"), P(None, "dp"),
            P(None, "dp", "tensor"), P(None, ("tensor", "dp")), P(None, "dp", "tensor"), P(None, "dp"),
        ),
        check_vma=False,
    )
```
